128 devices in a mesh: row: 8 (over x, core), col: 16 (over y, z).
Axes of the slice: x: 4, y: 4, z: 4, core: 2. Of those that a mesh axis runs over, the one named last changes fastest.
Arguments:
- embeddings: float32 [65536, 1024], P(('row', 'col')), may hold values from -6 to 6
- dest_pos: int32 [65536], P(('row', 'col')), may hold values from 0 to 65535, as said below
- cluster_ids: int32 [8, 8192], P('row', 'col'), may hold values from 0 to 15, as said below
Outputs:
- best_match: float32 [8, 8192], P('row', 'col')
The draws below stay inside these ranges and needn't reach their ends.
Inputs may be any that keep to these rules, and one draw needn't show every extreme that they name: dest_pos is a permutation; of the 512 rows stored on one device at most 8 have positions in one device's block of 512 positions, and exactly 8 for some pairs of devices. In each group cluster_ids never falls along the positions; every cluster holds 200 to 5120 positions, and one cluster of each group exactly 5120.
All inputs are finite; a program needn't handle non-finite values.
Results may differ from the reference program's by a relative error of at most 0.0013.
Values may be sent and summed in bfloat16 or wider, within the bound.
A program may use at most 64 MiB of HBM per device.

```python
import jax
import jax.numpy as jnp
from jax import lax

E = 1024
ROWS_DEV = 512
CAP = 8
GROUP = 8192
MEMBERS = 65536
CLUSTERS = 16
MOST = 5120
SMALLEST = 200
N_ROW = 8
N_COL = 16


def draw_dest_pos(key, part):
    key = jax.random.fold_in(key, 7)
    devs = N_ROW * N_COL
    key_order, key_source, key_target = jax.random.split(key, 3)
    slots = devs * CAP
    first = devs // 2
    order = jax.random.permutation(key_order, slots)
    slot_offset = jnp.arange(slots, dtype=jnp.int32) // CAP
    ranking = jnp.where(slot_offset == first, order - slots, order)
    chosen = jnp.argsort(ranking)[:ROWS_DEV]
    offsets = slot_offset[chosen]
    source_perm = jax.vmap(lambda k: jax.random.permutation(k, ROWS_DEV))(jax.random.split(key_source, devs))
    target_perm = jax.vmap(lambda k: jax.random.permutation(k, ROWS_DEV))(jax.random.split(key_target, devs))
    sources = jnp.arange(devs, dtype=jnp.int32)[:, None]
    target = (sources + offsets[source_perm]) % devs
    places = target_perm[target, source_perm]
    return (target * ROWS_DEV + places).reshape(-1).astype(jnp.int32)


def one_group_ids(key):
    key_weight, key_order = jax.random.split(key, 2)
    others = CLUSTERS - 1
    extra = GROUP - MOST - others * SMALLEST
    powers = jax.random.randint(key_weight, (others,), 0, 8)
    weights = jnp.left_shift(jnp.ones((others,), jnp.int32), powers)
    shares = extra * weights // jnp.sum(weights)
    shares = shares.at[0].add(extra - jnp.sum(shares))
    sizes = jnp.concatenate([jnp.full((1,), MOST, jnp.int32), SMALLEST + shares]).astype(jnp.int32)
    sizes = sizes[jax.random.permutation(key_order, CLUSTERS)]
    ends = jnp.cumsum(sizes)[:-1]
    positions = jnp.arange(GROUP, dtype=jnp.int32)
    return jnp.sum((positions[:, None] >= ends[None, :]).astype(jnp.int32), axis=1).astype(jnp.int32)


def draw_cluster_ids(key, part):
    key = jax.random.fold_in(key, 11)
    return jax.vmap(one_group_ids)(jax.random.split(key, N_ROW)).astype(jnp.int32)


def block_scale(rng, dims, cuts, smallest, high):
    loudness = 1.0
    for dim, blocks in cuts:
        draws = jax.random.uniform(jax.random.fold_in(jax.random.fold_in(rng, 6), dim), (blocks,), jnp.float32, smallest / len(cuts), high / len(cuts))
        loudness = loudness * jnp.repeat(jnp.exp(draws), dims[dim] // blocks).reshape((-1,) + (1,) * (len(dims) - 1 - dim))
    return loudness


def centred(rng, dims, spread, limit, shards=(), held_as=jnp.bfloat16):
    array = spread * jax.random.normal(rng, dims, jnp.float32)
    if shards:
        array = array * block_scale(rng, dims, shards, -0.22, 0.18)
    return jnp.clip(array, -limit, limit).astype(held_as)


def setup_inputs(seed: int = 0) -> dict:
    key_list = jax.random.split(jax.random.key(seed), 4)
    embeddings = centred(key_list[0], (MEMBERS, E), 1.0, 6.0, ((0, 128),), jnp.float32)
    dest_pos = draw_dest_pos(jax.random.fold_in(key_list[3], 71), 0)
    cluster_ids = draw_cluster_ids(jax.random.fold_in(key_list[3], 71), 0)
    return {"embeddings": embeddings, "dest_pos": dest_pos, "cluster_ids": cluster_ids}


def normalize(rows):
    scale = lax.rsqrt(lax.optimization_barrier(jnp.sum(rows * rows, axis=1, keepdims=True)) + 1e-06)
    return (rows * scale).astype(jnp.bfloat16)

def group_best(rows, labels):
    block = min(512, GROUP)
    count = GROUP // block
    blocks = rows.reshape(count, block, E)
    block_labels = labels.reshape(count, block)
    places = jnp.arange(GROUP, dtype=jnp.int32).reshape(count, block)
    columns = jnp.arange(GROUP, dtype=jnp.int32)

    def one_block(item):
        left, left_labels, left_places = item
        sims = jnp.dot(left, rows.T, preferred_element_type=jnp.float32)
        keep = (left_labels[:, None] == labels[None, :]) & (left_places[:, None] != columns[None, :])
        return lax.optimization_barrier(jnp.max(jnp.where(keep, sims, jnp.float32(-1.0)), axis=1))
    return lax.map(one_block, (blocks, block_labels, places)).reshape(GROUP)

def reference(embeddings, dest_pos, cluster_ids):
    unit = normalize(embeddings)
    sorted_units = jnp.zeros((MEMBERS, E), jnp.bfloat16).at[dest_pos].set(unit)
    sorted_units = sorted_units.reshape(N_ROW, GROUP, E)
    results = [group_best(sorted_units[g], cluster_ids[g]) for g in range(N_ROW)]
    return jnp.stack(results)
```

```python
import functools

import jax
import jax.numpy as jnp
from jax import lax
from jax.experimental import pallas as pl
from jax.experimental.pallas import tpu as pltpu
from jax.sharding import PartitionSpec as P

MESH = pl.DeviceIdType.MESH
F32, BF16, I32 = jnp.float32, jnp.bfloat16, jnp.int32
DEVS = 128
ROWS = 512
WIDTH = 1024
HALF = WIDTH // 2
QUARTER = ROWS // 2
CHIP = (0, 1, 7, 2, 5, 4, 6, 3)
VERTEX = (0, 1, 3, 7, 5, 4, 6, 2)
HELD = ((0, 1, 9, 4), (1, 0, 2, 3), (8, 2, 0, 6), (2, 8, 1, 7), (5, 4, 6, 1), (4, 5, 3, 2), (6, 3, 5, 9), (3, 7, 4, 8))
SLOT = (0, 512, 1024, 1536)
SECOND, PATCH, HEAD = 2048, 2560, 2816
HEAD_ROWS = 272
X_ROWS = HEAD + HEAD_ROWS
SEND = (
    (0, 0, 0, 0, 0, 0, SECOND, 0),
    (0, 0, SECOND, 0, 0, 0, 0, 0),
    (512, 1024, SECOND, 512, 512, 1024, 0, 512),
)
PATCH_BLOCK = (5, 5, 5, 0, 0, 0, 0, 5)
PATCH_HALF = (0, 1, 0, 0, 0, 0, 1, 1)
PATCH_MEETS = (0, 512, 0, 1536, 0, 0, SECOND, 1536)
CHUNKS = 4
CHUNK = ROWS // CHUNKS


def pick(p, table):
    out = jnp.int32(table[0])
    for i in range(1, len(table)):
        if table[i] != table[0]:
            out = jnp.where(p == i, jnp.int32(table[i]), out)
    return out


def iota(shape, dim):
    return lax.broadcasted_iota(I32, shape, dim)


def ones(cond):
    return jnp.where(cond, jnp.float32(1.0), jnp.float32(0.0)).astype(BF16)


def dot_t(a, b):
    return lax.dot_general(a, b, (((1,), (1,)), ((), ())), preferred_element_type=F32)


def dot(a, b):
    return lax.dot_general(a, b, (((1,), (0,)), ((), ())), preferred_element_type=F32)


def kernel(
    emb_ref, dest_ref, ids_ref, out_ref,
    emb, unit, sbuf, rb, meta_s, meta_r, labs, q, xs, acc, ob, fin,
    emb_sem, own_sem, row_s, row_r, meta_ss, meta_rr, lab_s, lab_r,
    ici_s, ici_r, pair_s, pair_r, patch_s, patch_r, head_s, head_r, fin_s, fin_r,
):
    row, col = lax.axis_index("row"), lax.axis_index("col")
    x, k, y, z = row // 2, row % 2, col // 4, col % 4
    chip = x * 16 + y * 4 + z
    me = chip * 2 + k
    gx, gy, gz = x // 2, y // 2, z // 2
    group = (1 - gx) * 4 + gy * 2 + gz
    p = (x % 2) * 4 + (y % 2) * 2 + z % 2
    share = pick(p, CHIP)
    large_only = (p == 2) | (p == 6)

    emb_copy = pltpu.make_async_copy(emb_ref, emb, emb_sem)
    emb_copy.start()

    def relative(e):
        off = (e * 45) % DEVS
        dx, dy, dz, dk = off // 32, (off // 8) % 4, (off // 2) % 4, off % 2
        return (x + dx) % 4, (y + dy) % 4, (z + dz) % 4, (k + dk) % 2

    barrier = pltpu.get_barrier_semaphore()

    def greet(e, _):
        tx, ty, tz, tk = relative(e)
        pl.semaphore_signal(barrier, inc=1, device_id=(2 * tx + tk, 4 * ty + tz), device_id_type=MESH)
        return _

    lax.fori_loop(1, DEVS, greet, 0)

    dest = dest_ref[...]
    block = lax.shift_right_logical(dest, 9)
    place = dest & 511
    g, b = lax.shift_right_logical(block, 4), block & 15
    to = jnp.where(b < 6, b, jnp.where(b < 8, 6, jnp.where(b < 10, 7, b - 10)))
    half = jnp.where(b < 6, 0, jnp.where(b < 10, b & 1, 1))
    vert = pick(to, VERTEX)
    tx = 2 * (1 - lax.shift_right_logical(g, 2)) + lax.shift_right_logical(vert, 2)
    ty = 2 * (lax.shift_right_logical(g, 1) & 1) + (lax.shift_right_logical(vert, 1) & 1)
    tz = 2 * (g & 1) + (vert & 1)
    tchip = tx * 16 + ty * 4 + tz
    tb = tchip * 2 + half
    hot = iota((DEVS, ROWS), 0) == tb
    before = ones(iota((ROWS, ROWS), 0) < iota((ROWS, ROWS), 1))
    rank = dot(ones(hot), before)
    slot = jnp.sum(jnp.where(hot, rank, 0.0), axis=0, keepdims=True).astype(I32)
    line = tb * 8 + slot

    value = place + 1 + 512 * half
    to_chip = iota((64, ROWS), 0) == tchip
    lanes = ones(iota((128, ROWS), 0) == (half * 8 + slot + 16 * (me % 8)))
    high = jnp.where(to_chip, lax.shift_right_logical(value, 4).astype(F32), 0.0).astype(BF16)
    low = jnp.where(to_chip, (value & 15).astype(F32), 0.0).astype(BF16)
    meta = 16.0 * dot_t(high, lanes) + dot_t(low, lanes)
    for n in range(64):
        meta_s[n] = meta[n : n + 1, :]

    emb_copy.wait()
    rows = emb[...]
    scale = lax.rsqrt(jnp.sum(rows * rows, axis=1, keepdims=True) + 1e-06)
    unit[...] = (rows * scale).astype(BF16)
    for a in range(8):
        take = ones(iota((128, ROWS), 0) + 128 * a == line)
        packed = dot(take, unit[...]).astype(BF16)
        sbuf[0, pl.ds(128 * a, 128), :] = packed[:, :HALF]
        sbuf[1, pl.ds(128 * a, 128), :] = packed[:, HALF:]

    pl.semaphore_wait(barrier, DEVS - 1)

    def send_rows(e, _):
        tx, ty, tz, tk = relative(e)
        n = tx * 16 + ty * 4 + tz
        pltpu.make_async_remote_copy(
            src_ref=sbuf.at[tk, pl.ds(pl.multiple_of(16 * n, 16), 16)],
            dst_ref=rb.at[pl.ds(pl.multiple_of(16 * me, 16), 16)],
            send_sem=row_s, recv_sem=row_r,
            device_id=(2 * tx + tk, 4 * ty + tz), device_id_type=MESH,
        ).start()
        return _

    def send_meta(e, _):
        tx, ty, tz, tk = relative(e)
        n = tx * 16 + ty * 4 + tz
        pltpu.make_async_remote_copy(
            src_ref=meta_s.at[n], dst_ref=meta_r.at[me],
            send_sem=meta_ss, recv_sem=meta_rr,
            device_id=(2 * tx + tk, 4 * ty + tz), device_id_type=MESH,
        ).start()
        return _

    def send_ids(j, _):
        v, tk = j // 2, j % 2
        hx = 2 * (1 - row // 4) + v // 4
        hy = 2 * ((row // 2) % 2) + (v // 2) % 2
        hz = 2 * (row % 2) + v % 2
        pltpu.make_async_remote_copy(
            src_ref=ids_ref, dst_ref=labs.at[col],
            send_sem=lab_s, recv_sem=lab_r,
            device_id=(2 * hx + tk, 4 * hy + hz), device_id_type=MESH,
        ).start()
        return _

    lax.fori_loop(1, 17, send_rows, 0)
    lax.fori_loop(0, 16, send_ids, 0)
    lax.fori_loop(1, DEVS, send_meta, 0)
    lax.fori_loop(17, DEVS, send_rows, 0)
    own_copy = pltpu.make_async_copy(
        sbuf.at[k, pl.ds(pl.multiple_of(16 * chip, 16), 16)],
        rb.at[pl.ds(pl.multiple_of(16 * me, 16), 16)], own_sem,
    )
    own_copy.start()
    meta_r[me] = meta_s[chip]

    pltpu.make_async_copy(labs, labs, lab_r).wait()
    large = labs[7, :, 0:1]
    first = jnp.where(share < 6, share, 2 * share - 6)
    second = jnp.where(share < 6, share + 10, 2 * share - 5)
    is_large = labs[first] == large
    eye = ones(iota((ROWS, ROWS), 0) == iota((ROWS, ROWS), 1))

    def column(r):
        return dot_t(eye, jnp.broadcast_to(r, (8, ROWS)).astype(BF16))[:, 0:1]

    rest_ids = jnp.where(is_large, labs[second], labs[first]).astype(F32)
    rest_col = column(rest_ids)
    large_col = column(jnp.where(is_large, 1.0, 0.0))
    index_col = iota((ROWS, 1), 0).astype(F32) + 1.0
    key_large = index_col + 512.0 * (1.0 - large_col)
    key_rest = index_col + 512.0 * large_col

    pltpu.make_async_copy(meta_r.at[pl.ds(0, DEVS - 1)], meta_r.at[pl.ds(0, DEVS - 1)], meta_rr).wait()
    for a in range(16):
        r = meta_r[8 * a]
        for i in range(1, 8):
            r = r + meta_r[8 * a + i]
        q[0:ROWS, pl.ds(128 * a, 128)] = ones(key_large == r)
        q[ROWS : 2 * ROWS, pl.ds(128 * a, 128)] = ones(key_rest == r)

    own_copy.wait()
    pltpu.make_async_copy(rb.at[pl.ds(0, 16 * (DEVS - 1))], rb.at[pl.ds(0, 16 * (DEVS - 1))], row_r).wait()
    xs[k, pl.ds(0, ROWS), :] = dot(q[0:ROWS, :], rb[...]).astype(BF16)
    xs[k, pl.ds(SECOND, ROWS), :] = dot(q[ROWS : 2 * ROWS, :], rb[...]).astype(BF16)

    def along(bit):
        nx = x + 1 - 2 * (x % 2) if bit == 2 else x
        ny = y + 1 - 2 * (y % 2) if bit == 1 else y
        nz = z + 1 - 2 * (z % 2) if bit == 0 else z
        return (2 * nx + k, 4 * ny + nz)

    def between(src, dst, n, send, recv, device):
        return pltpu.make_async_remote_copy(
            src_ref=xs.at[k, pl.ds(src, n)], dst_ref=xs.at[k, pl.ds(dst, n)],
            send_sem=send, recv_sem=recv, device_id=device, device_id_type=MESH,
        )

    sibling = (2 * x + 1 - k, col)
    pairs = []

    def share_rows(start, n):
        i = len(pairs)
        cp = between(start, start, n, pair_s.at[i], pair_r.at[i], sibling)
        cp.start()
        pairs.append(cp)

    def block_copy(bit, c):
        src = pl.multiple_of(pick(p, SEND[bit]) + CHUNK * c, 16)
        return between(src, SLOT[1 + bit] + CHUNK * c, CHUNK, ici_s.at[bit, c], ici_r.at[bit, c], along(bit))

    copies = [[block_copy(bit, c) for c in range(CHUNKS)] for bit in range(3)]
    for c in range(CHUNKS):
        copies[0][c].start()
        copies[1][c].start()

        @pl.when(large_only)
        def _():
            copies[2][c].start()

    def patch_copy(i, src, bit):
        return between(src, PATCH, QUARTER, patch_s.at[i], patch_r, along(bit))

    @pl.when(p == 4)
    def _():
        patch_copy(0, 0, 2).start()

    head_steps = ((1, 0), (3, 1), (7, 2), (5, 1), (4, 0))
    for v, bit in head_steps:
        @pl.when(p == v)
        def _():
            between(SECOND, HEAD, HEAD_ROWS, head_s, head_r, along(bit)).start()

    share_rows(0, ROWS)
    share_rows(SECOND, ROWS)
    for c in range(CHUNKS):
        for bit in range(2):
            copies[bit][c].wait_recv()
            share_rows(SLOT[1 + bit] + CHUNK * c, CHUNK)

        @pl.when(jnp.logical_not(large_only))
        def _():
            copies[2][c].start()

    @pl.when(p == 5)
    def _():
        patch_copy(0, 768, 2).start()

    @pl.when(p == 2)
    def _():
        patch_copy(0, 1024, 0).start()
        patch_copy(1, 1280, 2).start()

    @pl.when(p == 6)
    def _():
        patch_copy(0, 1024, 2).start()
        patch_copy(1, 1280, 0).start()

    for c in range(CHUNKS):
        copies[2][c].wait_recv()
        share_rows(SLOT[3] + CHUNK * c, CHUNK)

    has_patch = (p != 4) & (p != 5)
    has_head = (p != 2) & (p != 6) & (p != 4)
    n_pairs = len(pairs)
    patch_pair = between(PATCH, PATCH, QUARTER, pair_s.at[n_pairs], pair_r.at[n_pairs], sibling)
    head_pair = between(HEAD, HEAD, HEAD_ROWS, pair_s.at[n_pairs + 1], pair_r.at[n_pairs + 1], sibling)

    @pl.when(has_head)
    def _():
        pltpu.make_async_copy(xs.at[k, pl.ds(HEAD, HEAD_ROWS)], xs.at[k, pl.ds(HEAD, HEAD_ROWS)], head_r).wait()
        head_pair.start()

    @pl.when(has_patch)
    def _():
        pltpu.make_async_copy(xs.at[k, pl.ds(PATCH, QUARTER)], xs.at[k, pl.ds(PATCH, QUARTER)], patch_r).wait()
        patch_pair.start()

    for cp in pairs:
        cp.wait_recv()

    @pl.when(has_head)
    def _():
        head_pair.wait_recv()

    @pl.when(has_patch)
    def _():
        patch_pair.wait_recv()

    def tile(j, nj, i, ni):
        return dot_t(xs[0, pl.ds(j, nj), :], xs[0, pl.ds(i, ni), :]) + dot_t(
            xs[1, pl.ds(j, nj), :], xs[1, pl.ds(i, ni), :]
        )

    def top(t):
        return jnp.max(t, axis=0, keepdims=True)

    mine = pl.multiple_of(QUARTER * k, QUARTER)
    own_tile = iota((ROWS, QUARTER), 0) == iota((ROWS, QUARTER), 1) + QUARTER * k
    ob[...] = jnp.full(ob.shape, -1.0, F32)
    for s in range(4):
        best = None
        for j in range(4):
            t = tile(SLOT[j], ROWS, pl.multiple_of(SLOT[s] + mine, QUARTER), QUARTER)
            if s == j:
                t = jnp.where(own_tile, -1.0, t)
            m = top(t)
            best = m if best is None else jnp.maximum(best, m)
        acc[s] = best
    rest_row = jnp.where(k == 0, rest_ids[:, :QUARTER], rest_ids[:, QUARTER:])
    second_cols = pl.multiple_of(SECOND + mine, QUARTER)
    t = tile(SECOND, ROWS, second_cols, QUARTER)
    acc[4] = top(jnp.where((rest_col == rest_row) & jnp.logical_not(own_tile), t, -1.0))

    def raise_to(b, at, n, v):
        ob[b, :, pl.ds(at, n)] = jnp.maximum(ob[b, :, pl.ds(at, n)], v)

    @pl.when(large_only)
    def _():
        for s in range(4):
            t = tile(SECOND, ROWS, pl.multiple_of(SLOT[s] + mine, QUARTER), QUARTER)
            acc[s] = jnp.maximum(acc[s], top(t))
            acc[4] = jnp.maximum(acc[4], top(tile(SLOT[s], ROWS, second_cols, QUARTER)))

    @pl.when(has_head)
    def _():
        nxt = labs[share + 1]
        head_ids = jnp.where(nxt == large, labs[share + 11], nxt).astype(F32)
        head_col = column(head_ids)[:HEAD_ROWS]
        t = tile(HEAD, HEAD_ROWS, second_cols, QUARTER)
        acc[4] = jnp.maximum(acc[4], top(jnp.where(head_col == rest_row, t, -1.0)))
        t = tile(second_cols, QUARTER, HEAD, HEAD_ROWS)
        some_col = jnp.where(k == 0, rest_col[:QUARTER], rest_col[QUARTER:])
        m = top(jnp.where(some_col == head_ids[:, :HEAD_ROWS], t, -1.0))
        m = jnp.concatenate([m, jnp.full((1, ROWS - HEAD_ROWS), -1.0, F32)], axis=1)
        raise_to(share + 1, 0, ROWS, jnp.where(nxt == large, -1.0, m))
        raise_to(share + 11, 0, ROWS, jnp.where(nxt == large, m, -1.0))

    @pl.when(has_patch)
    def _():
        meets = pick(p, PATCH_MEETS)
        t = tile(PATCH, QUARTER, pl.multiple_of(meets + mine, QUARTER), QUARTER)
        s = jnp.where(meets == SECOND, 4, meets // ROWS)
        acc[s] = jnp.maximum(acc[s], top(t))
        t = tile(pl.multiple_of(meets, ROWS), ROWS, pl.multiple_of(PATCH + 128 * k, 128), 128)
        at = pl.multiple_of(QUARTER * pick(p, PATCH_HALF) + 128 * k, 128)
        v = pick(p, PATCH_BLOCK)
        here = labs[v, :, pl.ds(at, 128)] == large
        raise_to(v, at, 128, jnp.where(here, top(t), -1.0))
        raise_to(v + 10, at, 128, jnp.where(here, -1.0, top(t)))

    for s in range(4):
        v = pick(p, tuple(h[s] for h in HELD))
        here = labs[v, :, pl.ds(mine, QUARTER)] == large
        raise_to(v, mine, QUARTER, jnp.where(here, acc[s], -1.0))

        @pl.when(v < 6)
        def _():
            raise_to(v + 10, mine, QUARTER, jnp.where(here, -1.0, acc[s]))

    here = labs[first, :, pl.ds(mine, QUARTER)] == large
    raise_to(second, mine, QUARTER, jnp.where(here, acc[4], -1.0))
    raise_to(first, mine, QUARTER, jnp.where(here, -1.0, acc[4]))

    def send_best(b, _):
        pltpu.make_async_remote_copy(
            src_ref=ob.at[b], dst_ref=fin.at[p * 2 + k],
            send_sem=fin_s, recv_sem=fin_r, device_id=(group, b), device_id_type=MESH,
        ).start()
        return _

    lax.fori_loop(0, 16, send_best, 0)

    pltpu.make_async_copy(sbuf.at[0, pl.ds(0, 1008)], sbuf.at[0, pl.ds(0, 1008)], row_s).wait()
    pltpu.make_async_copy(sbuf.at[0], sbuf.at[0], row_s).wait()
    pltpu.make_async_copy(meta_r.at[pl.ds(0, DEVS - 1)], meta_r.at[pl.ds(0, DEVS - 1)], meta_ss).wait()
    pltpu.make_async_copy(labs, labs, lab_s).wait()
    for per_bit in copies:
        for cp in per_bit:
            cp.wait_send()
    for cp in pairs:
        cp.wait_send()

    @pl.when(has_head)
    def _():
        head_pair.wait_send()

    @pl.when(has_patch)
    def _():
        patch_pair.wait_send()

    @pl.when((p == 1) | (p == 3) | (p == 7) | (p == 5) | (p == 4))
    def _():
        between(SECOND, HEAD, HEAD_ROWS, head_s, head_r, along(0)).wait_send()

    @pl.when((p == 4) | (p == 5) | (p == 2) | (p == 6))
    def _():
        patch_copy(0, 0, 0).wait_send()

    @pl.when((p == 2) | (p == 6))
    def _():
        patch_copy(1, 0, 0).wait_send()

    pltpu.make_async_copy(fin, fin, fin_s).wait()
    pltpu.make_async_copy(fin, fin, fin_r).wait()
    best = fin[0]
    for i in range(1, 16):
        best = jnp.maximum(best, fin[i])
    out_ref[...] = best


def shards(embeddings, dest_pos, cluster_ids):
    dma, n_pairs = pltpu.SemaphoreType.DMA, 4 + 3 * CHUNKS
    return pl.pallas_call(
        kernel,
        out_shape=jax.ShapeDtypeStruct((1, ROWS), F32),
        in_specs=[
            pl.BlockSpec(memory_space=pl.ANY),
            pl.BlockSpec(memory_space=pltpu.VMEM),
            pl.BlockSpec(memory_space=pltpu.VMEM),
        ],
        out_specs=pl.BlockSpec(memory_space=pltpu.VMEM),
        scratch_shapes=[
            pltpu.VMEM((ROWS, WIDTH), F32),
            pltpu.VMEM((ROWS, WIDTH), BF16),
            pltpu.VMEM((2, 1024, HALF), BF16),
            pltpu.VMEM((16 * DEVS, HALF), BF16),
            pltpu.VMEM((64, 1, 128), F32),
            pltpu.VMEM((DEVS, 1, 128), F32),
            pltpu.VMEM((16, 1, ROWS), I32),
            pltpu.VMEM((2 * ROWS, 16 * DEVS), BF16),
            pltpu.VMEM((2, X_ROWS, HALF), BF16),
            pltpu.VMEM((5, 1, QUARTER), F32),
            pltpu.VMEM((16, 1, ROWS), F32),
            pltpu.VMEM((16, 1, ROWS), F32),
            dma, dma, dma, dma, dma, dma, dma, dma,
            dma((3, CHUNKS)), dma((3, CHUNKS)), dma((n_pairs,)), dma((n_pairs,)),
            dma((2,)), dma, dma, dma, dma, dma,
        ],
        compiler_params=pltpu.CompilerParams(
            collective_id=0, has_side_effects=True, vmem_limit_bytes=44 * 2**20
        ),
        name="best_match",
    )(embeddings, dest_pos.reshape(1, ROWS), cluster_ids)


def solution(mesh):
    return jax.shard_map(
        shards,
        mesh=mesh,
        in_specs=(P(("row", "col"), None), P(("row", "col")), P("row", "col")),
        out_specs=P("row", "col"),
        check_vma=False,
    )
```

```python
import functools

import jax
import jax.numpy as jnp
from jax import lax
from jax.experimental import pallas as pl
from jax.experimental.pallas import tpu as pltpu
from jax.sharding import PartitionSpec as P

MESH = pl.DeviceIdType.MESH
F32, BF16, I32 = jnp.float32, jnp.bfloat16, jnp.int32
DEVS = 128
ROWS = 512
WIDTH = 1024
HALF = WIDTH // 2
QUARTER = ROWS // 2
CHIP = (0, 1, 7, 2, 5, 4, 6, 3)
VERTEX = (0, 1, 3, 7, 5, 4, 6, 2)
HELD = ((0, 1, 9, 4), (1, 0, 2, 3), (8, 2, 0, 6), (2, 8, 1, 7), (5, 4, 6, 1), (4, 5, 3, 2), (6, 3, 5, 9), (3, 7, 4, 8))
SLOT = (0, 512, 1024, 1536)
SECOND, PATCH, HEAD = 2048, 2560, 2816
HEAD_ROWS = 272
X_ROWS = HEAD + HEAD_ROWS
SEND = (
    (0, 0, 0, 0, 0, 0, SECOND, 0),
    (0, 0, SECOND, 0, 0, 0, 0, 0),
    (512, 1024, SECOND, 512, 512, 1024, 0, 512),
)
PATCH_BLOCK = (5, 0, 5, 0, 0, 0, 0, 5)
PATCH_HALF = (1, 0, 0, 0, 0, 0, 1, 1)
PATCH_MEETS = (0, 0, 0, 1536, 0, 0, SECOND, 1536)
PATCHES = ((4, 0, 2, 256), (6, 2, 2, 1024), (6, 7, 0, 1280), (2, 3, 0, 1024), (2, 6, 2, 1280))
CHUNKS = ((0, 64), (64, 64), (128, 128), (256, 128), (384, 128))


def pick(p, table):
    out = jnp.int32(table[0])
    for i in range(1, len(table)):
        if table[i] != table[0]:
            out = jnp.where(p == i, jnp.int32(table[i]), out)
    return out


def iota(shape, dim):
    return lax.broadcasted_iota(I32, shape, dim)


def ones(cond):
    return jnp.where(cond, jnp.float32(1.0), jnp.float32(0.0)).astype(BF16)


def dot_t(a, b):
    return lax.dot_general(a, b, (((1,), (1,)), ((), ())), preferred_element_type=F32)


def dot(a, b):
    return lax.dot_general(a, b, (((1,), (0,)), ((), ())), preferred_element_type=F32)


def kernel(
    emb_hbm, dest_hbm, ids_hbm, out_ref,
    emb, dest_ref, ids_ref, unit, sbuf, rb, meta_s, meta_r, labs, q, xs, acc, ob, fin,
    emb_sem, dest_sem, ids_sem, own_sem, row_s, row_r, meta_ss, meta_rr, lab_s, lab_r,
    ici_s, ici_r, pair_s, pair_r, patch_s, patch_r, head_s, head_r, fin_s, fin_r,
):
    row, col = lax.axis_index("row"), lax.axis_index("col")
    x, k, y, z = row // 2, row % 2, col // 4, col % 4
    chip = x * 16 + y * 4 + z
    me = chip * 2 + k
    group = 2 * x + y // 2
    p = (y % 2) * 4 + (z // 2) * 2 + (z // 2 + z) % 2
    share = pick(p, CHIP)
    large_only = (p == 2) | (p == 6)

    dest_copy = pltpu.make_async_copy(dest_hbm, dest_ref, dest_sem)
    dest_copy.start()
    emb_copy = pltpu.make_async_copy(emb_hbm, emb, emb_sem)
    emb_copy.start()
    ids_copy = pltpu.make_async_copy(ids_hbm, ids_ref, ids_sem)
    ids_copy.start()

    def relative(e):
        off = (e * 45) % DEVS
        dx, dy, dz, dk = off // 32, (off // 8) % 4, (off // 2) % 4, off % 2
        return (x + dx) % 4, (y + dy) % 4, (z + dz) % 4, (k + dk) % 2

    barrier = pltpu.get_barrier_semaphore()

    def greet(tx, ty, tz, tk):
        pl.semaphore_signal(barrier, inc=1, device_id=(2 * tx + tk, 4 * ty + tz), device_id_type=MESH)

    lead = (x % 2 == 0) & (y % 2 == 0) & (z % 2 == 1) & (k == 0)
    root = (x == 2) & (y == 2) & (z == 3) & (k == 0)

    @pl.when(jnp.logical_not(lead))
    def _():
        greet(x - x % 2, y - y % 2, z - z % 2 + 1, 0)

    dest_copy.wait()
    dest = dest_ref[...]
    block = lax.shift_right_logical(dest, 9)
    place = dest & 511
    g, b = lax.shift_right_logical(block, 4), block & 15
    to = jnp.where(b < 6, b, jnp.where(b < 8, 6, jnp.where(b < 10, 7, b - 10)))
    half = jnp.where(b < 6, 0, jnp.where(b < 10, b & 1, 1))
    vert = pick(to, VERTEX)
    tx = lax.shift_right_logical(g, 1)
    ty = 2 * (g & 1) + lax.shift_right_logical(vert, 2)
    tz = (vert & 2) + (lax.shift_right_logical(vert, 1) + vert & 1)
    tchip = tx * 16 + ty * 4 + tz
    tb = tchip * 2 + half
    hot = iota((DEVS, ROWS), 0) == tb
    before = ones(iota((ROWS, ROWS), 0) < iota((ROWS, ROWS), 1))
    rank = dot(ones(hot), before)
    slot = jnp.sum(jnp.where(hot, rank, 0.0), axis=0, keepdims=True).astype(I32)
    line = tb * 8 + slot

    value = place + 1 + 512 * half
    to_chip = iota((64, ROWS), 0) == tchip
    lanes = ones(iota((128, ROWS), 0) == (half * 8 + slot + 16 * (me % 8)))
    high = jnp.where(to_chip, lax.shift_right_logical(value, 4).astype(F32), 0.0).astype(BF16)
    low = jnp.where(to_chip, (value & 15).astype(F32), 0.0).astype(BF16)
    meta = 16.0 * dot_t(high, lanes) + dot_t(low, lanes)
    for n in range(64):
        meta_s[n] = meta[n : n + 1, :]

    emb_copy.wait()
    rows = emb[...]
    scale = lax.rsqrt(jnp.sum(rows * rows, axis=1, keepdims=True) + 1e-06)
    unit[...] = (rows * scale).astype(BF16)
    for a in range(8):
        take = ones(iota((128, ROWS), 0) + 128 * a == line)
        packed = dot(take, unit[...]).astype(BF16)
        sbuf[0, pl.ds(128 * a, 128), :] = packed[:, :HALF]
        sbuf[1, pl.ds(128 * a, 128), :] = packed[:, HALF:]

    @pl.when(lead & jnp.logical_not(root))
    def _():
        pl.semaphore_wait(barrier, 15)
        greet(2, 2, 3, 0)
        pl.semaphore_wait(barrier, 1)

    @pl.when(root)
    def _():
        pl.semaphore_wait(barrier, 22)
        for j in range(7, 0, -1):
            greet((2 + 2 * (j // 4)) % 4, (2 + 2 * (j // 2 % 2)) % 4, (3 + 2 * (j % 2)) % 4, 0)

    @pl.when(lead)
    def _():
        for j in range(15, 0, -1):
            greet(x + j // 8, y + j // 4 % 2, z - j // 2 % 2, j % 2)

    @pl.when(jnp.logical_not(lead))
    def _():
        pl.semaphore_wait(barrier, 1)

    def send_rows(e, _):
        tx, ty, tz, tk = relative(e)
        n = tx * 16 + ty * 4 + tz
        pltpu.make_async_remote_copy(
            src_ref=sbuf.at[tk, pl.ds(pl.multiple_of(16 * n, 16), 16)],
            dst_ref=rb.at[pl.ds(pl.multiple_of(16 * me, 16), 16)],
            send_sem=row_s, recv_sem=row_r,
            device_id=(2 * tx + tk, 4 * ty + tz), device_id_type=MESH,
        ).start()
        return _

    def send_meta(e, _):
        tx, ty, tz, tk = relative(e)
        n = tx * 16 + ty * 4 + tz
        pltpu.make_async_remote_copy(
            src_ref=meta_s.at[n], dst_ref=meta_r.at[me],
            send_sem=meta_ss, recv_sem=meta_rr,
            device_id=(2 * tx + tk, 4 * ty + tz), device_id_type=MESH,
        ).start()
        return _

    ids_copy.wait()
    at_home = y // 2 == k

    def send_ids(j, carry):
        hy, hz, hk = 2 * k + j // 8, (j // 2) % 4, j % 2
        to_self = (hy == y) & (hz == z) & (hk == k)

        @pl.when(to_self)
        def _():
            pltpu.make_async_copy(ids_ref, labs.at[col], lab_r).start()

        @pl.when(jnp.logical_not(to_self))
        def _():
            pltpu.make_async_remote_copy(
                src_ref=ids_ref, dst_ref=labs.at[col],
                send_sem=lab_s, recv_sem=lab_r,
                device_id=(2 * x + hk, 4 * hy + hz), device_id_type=MESH,
            ).start()

        return carry

    lax.fori_loop(1, 49, send_rows, 0)
    lax.fori_loop(0, 16, send_ids, 0)
    lax.fori_loop(1, DEVS, send_meta, 0)
    lax.fori_loop(49, DEVS, send_rows, 0)
    own_copy = pltpu.make_async_copy(
        sbuf.at[k, pl.ds(pl.multiple_of(16 * chip, 16), 16)],
        rb.at[pl.ds(pl.multiple_of(16 * me, 16), 16)], own_sem,
    )
    own_copy.start()
    meta_r[me] = meta_s[chip]

    pltpu.make_async_copy(labs, labs, lab_r).wait()
    large = labs[7, :, 0:1]
    first = jnp.where(share < 6, share, 2 * share - 6)
    second = jnp.where(share < 6, share + 10, 2 * share - 5)
    is_large = labs[first] == large
    eye = ones(iota((ROWS, ROWS), 0) == iota((ROWS, ROWS), 1))

    def column(r):
        return dot_t(eye, jnp.broadcast_to(r, (8, ROWS)).astype(BF16))[:, 0:1]

    rest_ids = jnp.where(is_large, labs[second], labs[first]).astype(F32)
    rest_col = column(rest_ids)
    large_col = column(jnp.where(is_large, 1.0, 0.0))
    index_col = iota((ROWS, 1), 0).astype(F32) + 1.0
    key_large = index_col + 512.0 * (1.0 - large_col)
    key_rest = index_col + 512.0 * large_col

    pltpu.make_async_copy(meta_r.at[pl.ds(0, DEVS - 1)], meta_r.at[pl.ds(0, DEVS - 1)], meta_rr).wait()
    for a in range(16):
        r = meta_r[8 * a]
        for i in range(1, 8):
            r = r + meta_r[8 * a + i]
        q[0:ROWS, pl.ds(128 * a, 128)] = ones(key_large == r)
        q[ROWS : 2 * ROWS, pl.ds(128 * a, 128)] = ones(key_rest == r)

    own_copy.wait()
    pltpu.make_async_copy(rb.at[pl.ds(0, 16 * (DEVS - 1))], rb.at[pl.ds(0, 16 * (DEVS - 1))], row_r).wait()

    def along(bit):
        ny = y + 1 - 2 * (y % 2) if bit == 2 else y
        nz = z + 1 - 2 * (z % 2) if bit == 0 else 3 - z if bit == 1 else z
        return (2 * x + k, 4 * ny + nz)

    def between(src, dst, n, send, recv, device):
        return pltpu.make_async_remote_copy(
            src_ref=xs.at[k, pl.ds(src, n)], dst_ref=xs.at[k, pl.ds(dst, n)],
            send_sem=send, recv_sem=recv, device_id=device, device_id_type=MESH,
        )

    sibling = (2 * x + 1 - k, col)

    def pair_copy(i, start, n):
        return between(start, start, n, pair_s.at[i], pair_r.at[i], sibling)

    def block_copy(bit, c):
        at, n = CHUNKS[c]
        src = pl.multiple_of(pick(p, SEND[bit]) + at, 16)
        return between(src, SLOT[1 + bit] + at, n, ici_s.at[bit, c], ici_r.at[bit, c], along(bit))

    n_chunks = len(CHUNKS)
    copies = [[block_copy(bit, c) for c in range(n_chunks)] for bit in range(3)]
    block_pairs = [[pair_copy(3 + bit * n_chunks + c, SLOT[1 + bit] + CHUNKS[c][0], CHUNKS[c][1]) for c in range(n_chunks)] for bit in range(3)]
    own_pair, second_pair = pair_copy(0, 0, ROWS), pair_copy(1, SECOND, ROWS)
    patch_pair, head_pair = pair_copy(2, PATCH, QUARTER), pair_copy(3 + 3 * n_chunks, HEAD, HEAD_ROWS)
    has_patch = (p != 1) & (p != 4) & (p != 5)
    has_head = (p != 2) & (p != 6) & (p != 4)
    gives_head = (p != 2) & (p != 6) & (p != 0)

    def patch_copy(i):
        frm, to, bit, src = PATCHES[i]
        return between(src, PATCH, QUARTER, patch_s.at[i % 2], patch_r, along(bit))

    def head_copy(bit):
        return between(SECOND, HEAD, HEAD_ROWS, head_s, head_r, along(bit))

    for c in range(n_chunks):
        at, n = CHUNKS[c]
        xs[k, pl.ds(at, n), :] = dot(q[at : at + n, :], rb[...]).astype(BF16)

        @pl.when(p != 6)
        def _():
            copies[0][c].start()

        @pl.when(p != 2)
        def _():
            copies[1][c].start()

        @pl.when(p == 6)
        def _():
            copies[2][c].start()

        if at + n == 2 * QUARTER:
            @pl.when(p == 4)
            def _():
                patch_copy(0).start()

    own_pair.start()
    xs[k, pl.ds(SECOND, ROWS), :] = dot(q[ROWS : 2 * ROWS, :], rb[...]).astype(BF16)
    for c in range(n_chunks):
        @pl.when(p == 6)
        def _():
            copies[0][c].start()

        @pl.when(p == 2)
        def _():
            copies[1][c].start()
            copies[2][c].start()

    second_pair.start()
    for v, bit in ((1, 0), (3, 1), (7, 2), (5, 1), (4, 0)):
        @pl.when(p == v)
        def _():
            head_copy(bit).start()

    mine = pl.multiple_of(QUARTER * k, QUARTER)
    starts = SLOT + (SECOND,)

    def columns_of(s):
        return pl.multiple_of(starts[s] + mine, QUARTER)

    def tile(j, nj, i, ni):
        return dot_t(xs[0, pl.ds(j, nj), :], xs[0, pl.ds(i, ni), :]) + dot_t(
            xs[1, pl.ds(j, nj), :], xs[1, pl.ds(i, ni), :]
        )

    def top(t):
        return jnp.max(t, axis=0, keepdims=True)

    def meet(s, j, nj):
        t = tile(j, nj, columns_of(s), QUARTER)
        if j <= starts[s] < j + nj:
            t = jnp.where(iota((nj, QUARTER), 0) == iota((nj, QUARTER), 1) + (starts[s] - j + mine), -1.0, t)
        acc[s] = jnp.maximum(acc[s], top(t))

    ob[...] = jnp.full(ob.shape, -1.0, F32)
    acc[...] = jnp.full(acc.shape, -1.0, F32)
    rest_row = jnp.where(k == 0, rest_ids[:, :QUARTER], rest_ids[:, QUARTER:])

    own_pair.wait_recv()
    meet(0, 0, ROWS)
    for c in range(n_chunks):
        copies[0][c].wait_recv()
        copies[1][c].wait_recv()

        @pl.when(jnp.logical_not(large_only))
        def _():
            copies[2][c].start()

        block_pairs[0][c].start()
        block_pairs[1][c].start()
        if CHUNKS[c][0] + CHUNKS[c][1] == QUARTER:
            @pl.when(p == 6)
            def _():
                patch_copy(1).start()

            @pl.when(p == 2)
            def _():
                patch_copy(3).start()

    @pl.when(p == 6)
    def _():
        patch_copy(2).start()

    @pl.when(p == 2)
    def _():
        patch_copy(4).start()

    second_pair.wait_recv()
    t = tile(SECOND, ROWS, columns_of(4), QUARTER)
    own = iota((ROWS, QUARTER), 0) == iota((ROWS, QUARTER), 1) + mine
    acc[4] = top(jnp.where((rest_col == rest_row) & jnp.logical_not(own), t, -1.0))
    for c in range(n_chunks):
        block_pairs[0][c].wait_recv()
        block_pairs[1][c].wait_recv()
    meet(0, ROWS, 2 * ROWS)
    meet(1, 0, 3 * ROWS)
    meet(2, 0, 3 * ROWS)

    @pl.when(large_only)
    def _():
        for s in range(3):
            meet(s, SECOND, ROWS)
        meet(4, 0, 3 * ROWS)

    for c in range(n_chunks - 1):
        copies[2][c].wait_recv()
        block_pairs[2][c].start()
    for c in range(n_chunks - 2):
        block_pairs[2][c].wait_recv()
    for s in range(3):
        meet(s, SLOT[3], QUARTER)

    @pl.when(large_only)
    def _():
        meet(4, SLOT[3], QUARTER)

    copies[2][n_chunks - 1].wait_recv()
    block_pairs[2][n_chunks - 1].start()

    @pl.when(has_head)
    def _():
        head_copy(0).wait_recv()
        head_pair.start()

    @pl.when(has_patch)
    def _():
        patch_copy(0).wait_recv()
        patch_pair.start()

    for c in range(n_chunks - 2, n_chunks):
        block_pairs[2][c].wait_recv()
    for s in range(3):
        meet(s, SLOT[3] + QUARTER, QUARTER)
    meet(3, 0, 4 * ROWS)

    @pl.when(large_only)
    def _():
        meet(4, SLOT[3] + QUARTER, QUARTER)
        meet(3, SECOND, ROWS)

    def raise_to(b, at, n, v):
        ob[b, :, pl.ds(at, n)] = jnp.maximum(ob[b, :, pl.ds(at, n)], v)

    @pl.when(has_head)
    def _():
        head_pair.wait_recv()
        nxt = labs[share + 1]
        head_ids = jnp.where(nxt == large, labs[share + 11], nxt).astype(F32)
        head_col = column(head_ids)[:HEAD_ROWS]
        t = tile(HEAD, HEAD_ROWS, columns_of(4), QUARTER)
        acc[4] = jnp.maximum(acc[4], top(jnp.where(head_col == rest_row, t, -1.0)))
        t = tile(columns_of(4), QUARTER, HEAD, HEAD_ROWS)
        some_col = jnp.where(k == 0, rest_col[:QUARTER], rest_col[QUARTER:])
        m = top(jnp.where(some_col == head_ids[:, :HEAD_ROWS], t, -1.0))
        m = jnp.concatenate([m, jnp.full((1, ROWS - HEAD_ROWS), -1.0, F32)], axis=1)
        raise_to(share + 1, 0, ROWS, jnp.where(nxt == large, -1.0, m))
        raise_to(share + 11, 0, ROWS, jnp.where(nxt == large, m, -1.0))

    @pl.when(has_patch)
    def _():
        patch_pair.wait_recv()
        patch_cols = pl.multiple_of(PATCH + 128 * k, 128)

        def meets(start):
            t = tile(PATCH, QUARTER, pl.multiple_of(start + mine, QUARTER), QUARTER)
            s = jnp.where(start == SECOND, 4, start // ROWS)
            acc[s] = jnp.maximum(acc[s], top(t))
            return top(tile(pl.multiple_of(start, ROWS), ROWS, patch_cols, 128))

        at = pl.multiple_of(QUARTER * pick(p, PATCH_HALF) + 128 * k, 128)
        v = pick(p, PATCH_BLOCK)
        here = labs[v, :, pl.ds(at, 128)] == large

        def give(m):
            raise_to(v, at, 128, jnp.where(here, m, -1.0))
            raise_to(v + 10, at, 128, jnp.where(here, -1.0, m))

        give(meets(pick(p, PATCH_MEETS)))

        @pl.when(p == 2)
        def _():
            give(meets(jnp.int32(SLOT[2])))

    for s in range(4):
        v = pick(p, tuple(h[s] for h in HELD))
        here = labs[v, :, pl.ds(mine, QUARTER)] == large
        raise_to(v, mine, QUARTER, jnp.where(here, acc[s], -1.0))

        @pl.when(v < 6)
        def _():
            raise_to(v + 10, mine, QUARTER, jnp.where(here, -1.0, acc[s]))

    here = labs[first, :, pl.ds(mine, QUARTER)] == large
    raise_to(second, mine, QUARTER, jnp.where(here, acc[4], -1.0))
    raise_to(first, mine, QUARTER, jnp.where(here, -1.0, acc[4]))

    def send_best(b, carry):
        to_self = at_home & (b == col)

        @pl.when(to_self)
        def _():
            pltpu.make_async_copy(ob.at[b], fin.at[p * 2 + k], fin_r).start()

        @pl.when(jnp.logical_not(to_self))
        def _():
            pltpu.make_async_remote_copy(
                src_ref=ob.at[b], dst_ref=fin.at[p * 2 + k],
                send_sem=fin_s, recv_sem=fin_r, device_id=(group, b), device_id_type=MESH,
            ).start()

        return carry

    lax.fori_loop(0, 16, send_best, 0)

    pltpu.make_async_copy(sbuf.at[0, pl.ds(0, 1008)], sbuf.at[0, pl.ds(0, 1008)], row_s).wait()
    pltpu.make_async_copy(sbuf.at[0], sbuf.at[0], row_s).wait()
    pltpu.make_async_copy(meta_r.at[pl.ds(0, DEVS - 1)], meta_r.at[pl.ds(0, DEVS - 1)], meta_ss).wait()
    for per_bit in copies + block_pairs:
        for cp in per_bit:
            cp.wait_send()
    own_pair.wait_send()
    second_pair.wait_send()

    @pl.when(has_head)
    def _():
        head_pair.wait_send()

    @pl.when(has_patch)
    def _():
        patch_pair.wait_send()

    @pl.when(gives_head)
    def _():
        head_copy(0).wait_send()

    for v, which in ((4, (0,)), (6, (1, 2)), (2, (3, 4))):
        @pl.when(p == v)
        def _():
            for i in which:
                patch_copy(i).wait_send()

    @pl.when(at_home)
    def _():
        pltpu.make_async_copy(labs.at[pl.ds(0, 15)], labs.at[pl.ds(0, 15)], lab_s).wait()
        pltpu.make_async_copy(fin.at[pl.ds(0, 15)], fin.at[pl.ds(0, 15)], fin_s).wait()

    @pl.when(jnp.logical_not(at_home))
    def _():
        pltpu.make_async_copy(labs, labs, lab_s).wait()
        pltpu.make_async_copy(fin, fin, fin_s).wait()

    pltpu.make_async_copy(fin, fin, fin_r).wait()
    best = fin[0]
    for i in range(1, 16):
        best = jnp.maximum(best, fin[i])
    out_ref[...] = best


def shards(embeddings, dest_pos, cluster_ids):
    dma, n_pairs = pltpu.SemaphoreType.DMA, 4 + 3 * len(CHUNKS)
    return pl.pallas_call(
        kernel,
        out_shape=jax.ShapeDtypeStruct((1, ROWS), F32),
        in_specs=[
            pl.BlockSpec(memory_space=pltpu.HBM),
            pl.BlockSpec(memory_space=pltpu.HBM),
            pl.BlockSpec(memory_space=pltpu.HBM),
        ],
        out_specs=pl.BlockSpec(memory_space=pltpu.VMEM),
        scratch_shapes=[
            pltpu.VMEM((ROWS, WIDTH), F32),
            pltpu.VMEM((1, ROWS), I32),
            pltpu.VMEM((1, ROWS), I32),
            pltpu.VMEM((ROWS, WIDTH), BF16),
            pltpu.VMEM((2, 1024, HALF), BF16),
            pltpu.VMEM((16 * DEVS, HALF), BF16),
            pltpu.VMEM((64, 1, 128), F32),
            pltpu.VMEM((DEVS, 1, 128), F32),
            pltpu.VMEM((16, 1, ROWS), I32),
            pltpu.VMEM((2 * ROWS, 16 * DEVS), BF16),
            pltpu.VMEM((2, X_ROWS, HALF), BF16),
            pltpu.VMEM((5, 1, QUARTER), F32),
            pltpu.VMEM((16, 1, ROWS), F32),
            pltpu.VMEM((16, 1, ROWS), F32),
            dma, dma, dma, dma, dma, dma, dma, dma, dma, dma,
            dma((3, len(CHUNKS))), dma((3, len(CHUNKS))), dma((n_pairs,)), dma((n_pairs,)),
            dma((2,)), dma, dma, dma, dma, dma,
        ],
        compiler_params=pltpu.CompilerParams(
            collective_id=0, has_side_effects=True, vmem_limit_bytes=62 * 2**20
        ),
        name="best_match",
    )(embeddings, dest_pos.reshape(1, ROWS), cluster_ids)


def solution(mesh):
    return jax.shard_map(
        shards,
        mesh=mesh,
        in_specs=(P(("row", "col"), None), P(("row", "col")), P("row", "col")),
        out_specs=P("row", "col"),
        check_vma=False,
    )
```

```python
import functools

import jax
import jax.numpy as jnp
from jax import lax
from jax.experimental import pallas as pl
from jax.experimental.pallas import tpu as pltpu
from jax.sharding import PartitionSpec as P

MESH = pl.DeviceIdType.MESH
F32, BF16, I32 = jnp.float32, jnp.bfloat16, jnp.int32
DEVS = 128
ROWS = 512
WIDTH = 1024
HALF = WIDTH // 2
QUARTER = ROWS // 2
CHIP = (0, 1, 7, 2, 5, 4, 6, 3)
VERTEX = (0, 1, 3, 7, 5, 4, 6, 2)
HELD = ((0, 1, 9, 4), (1, 0, 2, 3), (8, 2, 0, 6), (2, 8, 1, 7), (5, 4, 6, 1), (4, 5, 3, 2), (6, 3, 5, 9), (3, 7, 4, 8))
SLOT = (0, 512, 1024, 1536)
SECOND, PATCH, HEAD = 2048, 2560, 2816
HEAD_ROWS = 272
X_ROWS = HEAD + HEAD_ROWS
SEND = (
    (0, 0, 0, 0, 0, 0, SECOND, 0),
    (0, 0, SECOND, 0, 0, 0, 0, 0),
    (512, 1024, SECOND, 512, 512, 1024, 0, 512),
)
PATCH_BLOCK = (5, 0, 5, 0, 0, 0, 0, 5)
PATCH_HALF = (1, 0, 0, 0, 0, 0, 1, 1)
PATCH_MEETS = (0, 0, 0, 1536, 0, 0, SECOND, 1536)
PATCHES = ((4, 0, 2, 256), (6, 2, 2, 1024), (6, 7, 0, 1280), (2, 3, 0, 1024), (2, 6, 2, 1280))
CHUNKS = ((0, 128), (128, 128), (256, 128), (384, 128))
STRIDE, INVERSE, EARLY = 45, 37, 48


def pick(p, table):
    out = jnp.int32(table[0])
    for i in range(1, len(table)):
        if table[i] != table[0]:
            out = jnp.where(p == i, jnp.int32(table[i]), out)
    return out


def iota(shape, dim):
    return lax.broadcasted_iota(I32, shape, dim)


def ones(cond):
    return jnp.where(cond, jnp.float32(1.0), jnp.float32(0.0)).astype(BF16)


def dot_t(a, b):
    return lax.dot_general(a, b, (((1,), (1,)), ((), ())), preferred_element_type=F32)


def dot(a, b):
    return lax.dot_general(a, b, (((1,), (0,)), ((), ())), preferred_element_type=F32)


def kernel(
    emb_hbm, dest_hbm, ids_hbm, out_ref,
    emb, dest_ref, ids_ref, unit, sbuf, rb, part, meta_s, meta_r, labs, q, xs, acc, last, ob, fin,
    emb_sem, dest_sem, ids_sem, own_sem, row_s, row_r, meta_ss, meta_rr, meta_ps, meta_pr, lab_s, lab_r,
    ici_s, ici_r, pair_s, pair_r, patch_s, patch_r, head_s, head_r, fin_s, fin_r,
):
    row, col = lax.axis_index("row"), lax.axis_index("col")
    x, k, y, z = row // 2, row % 2, col // 4, col % 4
    chip = x * 16 + y * 4 + z
    group = 2 * x + y // 2
    p = (y % 2) * 4 + (z // 2) * 2 + (z // 2 + z) % 2
    share = pick(p, CHIP)
    large_only = (p == 2) | (p == 6)

    dest_copy = pltpu.make_async_copy(dest_hbm, dest_ref, dest_sem)
    dest_copy.start()
    emb_copy = pltpu.make_async_copy(emb_hbm, emb, emb_sem)
    emb_copy.start()
    ids_copy = pltpu.make_async_copy(ids_hbm, ids_ref, ids_sem)
    ids_copy.start()

    def relative(n):
        off = (n * STRIDE) % 64
        return (x + off // 16) % 4, (y + off // 4 % 4) % 4, (z + off % 4) % 4

    barrier = pltpu.get_barrier_semaphore()

    def greet(tx, ty, tz, tk):
        pl.semaphore_signal(barrier, inc=1, device_id=(2 * tx + tk, 4 * ty + tz), device_id_type=MESH)

    lead = (x % 2 == 0) & (y % 2 == 0) & (z % 2 == 0)

    @pl.when(jnp.logical_not(lead & (k == 0)))
    def _():
        greet(x - x % 2, y - y % 2, z - z % 2, 0)

    dest_copy.wait()
    dest = dest_ref[...]
    block = lax.shift_right_logical(dest, 9)
    place = dest & 511
    g, b = lax.shift_right_logical(block, 4), block & 15
    to = jnp.where(b < 6, b, jnp.where(b < 8, 6, jnp.where(b < 10, 7, b - 10)))
    half = jnp.where(b < 6, 0, jnp.where(b < 10, b & 1, 1))
    vert = pick(to, VERTEX)
    tx = lax.shift_right_logical(g, 1)
    ty = 2 * (g & 1) + lax.shift_right_logical(vert, 2)
    tz = (vert & 2) + (lax.shift_right_logical(vert, 1) + vert & 1)
    tchip = tx * 16 + ty * 4 + tz
    turn = (((tx - x) & 3) * 16 + ((ty - y) & 3) * 4 + ((tz - z) & 3)) * INVERSE & 3
    tb = tchip * 2 + half
    hot = iota((DEVS, ROWS), 0) == tb
    before = ones(iota((ROWS, ROWS), 0) < iota((ROWS, ROWS), 1))
    rank = dot(ones(hot), before)
    slot = jnp.sum(jnp.where(hot, rank, 0.0), axis=0, keepdims=True).astype(I32)
    line = tb * 8 + slot

    value = place + 1 + 512 * half
    to_chip = iota((64, ROWS), 0) == tchip
    lanes = ones(iota((128, ROWS), 0) == (half * 8 + slot + 16 * (2 * turn + k)))
    high = jnp.where(to_chip, lax.shift_right_logical(value, 4).astype(F32), 0.0).astype(BF16)
    low = jnp.where(to_chip, (value & 15).astype(F32), 0.0).astype(BF16)
    meta = 16.0 * dot_t(high, lanes) + dot_t(low, lanes)
    for n in range(64):
        meta_s[n] = meta[n : n + 1, :]

    emb_copy.wait()
    rows = emb[...]
    scale = lax.rsqrt(jnp.sum(rows * rows, axis=1, keepdims=True) + 1e-06)
    unit[...] = (rows * scale).astype(BF16)
    for a in range(8):
        take = ones(iota((128, ROWS), 0) + 128 * a == line)
        packed = dot(take, unit[...]).astype(BF16)
        sbuf[0, pl.ds(128 * a, 128), :] = packed[:, :HALF]
        sbuf[1, pl.ds(128 * a, 128), :] = packed[:, HALF:]

    @pl.when(lead & (k == 0))
    def _():
        pl.semaphore_wait(barrier, 15)
        for j in range(7, -1, -1):
            greet((x + 2 * (j // 4)) % 4, (y + 2 * (j // 2 % 2)) % 4, (z + 2 * (j % 2)) % 4, 1)
        pl.semaphore_wait(barrier, 1)

    @pl.when(lead & (k == 1))
    def _():
        pl.semaphore_wait(barrier, 8)
        for j in range(15, 0, -1):
            greet(x + j // 8, y + j // 4 % 2, z + j // 2 % 2, (1 + j) % 2)

    @pl.when(jnp.logical_not(lead))
    def _():
        pl.semaphore_wait(barrier, 1)

    def send_rows(e, carry):
        n, tk = e // 2, e % 2
        tx, ty, tz = relative(n)
        pltpu.make_async_remote_copy(
            src_ref=sbuf.at[tk, pl.ds(pl.multiple_of(16 * (tx * 16 + ty * 4 + tz), 16), 16)],
            dst_ref=rb.at[pl.ds(pl.multiple_of(16 * (2 * n + k), 16), 16)],
            send_sem=row_s, recv_sem=row_r.at[n // EARLY],
            device_id=(2 * tx + tk, 4 * ty + tz), device_id_type=MESH,
        ).start()
        return carry

    def send_meta(n, carry):
        tx, ty, tz = relative(n)
        pltpu.make_async_remote_copy(
            src_ref=meta_s.at[tx * 16 + ty * 4 + tz], dst_ref=meta_r.at[64 * k + n],
            send_sem=meta_ss, recv_sem=meta_rr,
            device_id=(2 * tx + k, 4 * ty + tz), device_id_type=MESH,
        ).start()
        return carry

    ids_copy.wait()
    at_home = y // 2 == k

    def send_ids(j, carry):
        hy, hz, hk = 2 * k + j // 8, (j // 2) % 4, j % 2
        to_self = (hy == y) & (hz == z) & (hk == k)

        @pl.when(to_self)
        def _():
            pltpu.make_async_copy(ids_ref, labs.at[col], lab_r).start()

        @pl.when(jnp.logical_not(to_self))
        def _():
            pltpu.make_async_remote_copy(
                src_ref=ids_ref, dst_ref=labs.at[col],
                send_sem=lab_s, recv_sem=lab_r,
                device_id=(2 * x + hk, 4 * hy + hz), device_id_type=MESH,
            ).start()

        return carry

    lax.fori_loop(2, 50, send_rows, 0)
    lax.fori_loop(0, 16, send_ids, 0)
    lax.fori_loop(1, 64, send_meta, 0)
    lax.fori_loop(50, DEVS, send_rows, 0)
    sibling = (2 * x + 1 - k, col)
    own_rows = pl.ds(pl.multiple_of(16 * chip, 16), 16)
    own_slot = pl.ds(pl.multiple_of(16 * k, 16), 16)
    sibling_copy = pltpu.make_async_remote_copy(
        src_ref=sbuf.at[1 - k, own_rows], dst_ref=rb.at[own_slot],
        send_sem=row_s, recv_sem=row_r.at[0], device_id=sibling, device_id_type=MESH,
    )
    sibling_copy.start()
    own_copy = pltpu.make_async_copy(sbuf.at[k, own_rows], rb.at[own_slot], own_sem)
    own_copy.start()
    meta_r[64 * k] = meta_s[chip]
    pltpu.make_async_copy(meta_s.at[pl.ds(0, 63)], meta_s.at[pl.ds(0, 63)], meta_rr).wait()
    meta_pair = pltpu.make_async_remote_copy(
        src_ref=meta_r.at[pl.ds(pl.multiple_of(64 * k, 64), 64)], dst_ref=meta_r.at[pl.ds(pl.multiple_of(64 * k, 64), 64)],
        send_sem=meta_ps, recv_sem=meta_pr, device_id=sibling, device_id_type=MESH,
    )
    meta_pair.start()

    pltpu.make_async_copy(labs, labs, lab_r).wait()
    large = labs[7, :, 0:1]
    first = jnp.where(share < 6, share, 2 * share - 6)
    second = jnp.where(share < 6, share + 10, 2 * share - 5)
    is_large = labs[first] == large
    eye = ones(iota((ROWS, ROWS), 0) == iota((ROWS, ROWS), 1))

    def column(r):
        return dot_t(eye, jnp.broadcast_to(r, (8, ROWS)).astype(BF16))[:, 0:1]

    rest_ids = jnp.where(is_large, labs[second], labs[first]).astype(F32)
    rest_col = column(rest_ids)
    large_col = column(jnp.where(is_large, 1.0, 0.0))
    index_col = iota((ROWS, 1), 0).astype(F32) + 1.0
    key_large = index_col + 512.0 * (1.0 - large_col)
    key_rest = index_col + 512.0 * large_col

    meta_pair.wait_recv()
    for a in range(16):
        r = meta_r[4 * a] + meta_r[64 + 4 * a]
        for i in range(1, 4):
            r = r + (meta_r[4 * a + i] + meta_r[64 + 4 * a + i])
        q[0:ROWS, pl.ds(128 * a, 128)] = ones(key_large == r)
        q[ROWS : 2 * ROWS, pl.ds(128 * a, 128)] = ones(key_rest == r)

    own_copy.wait()
    early = 32 * EARLY
    pltpu.make_async_copy(rb.at[pl.ds(0, early - 16)], rb.at[pl.ds(0, early - 16)], row_r.at[0]).wait()
    part[...] = dot(q[:, 0:early], rb[0:early, :])
    pltpu.make_async_copy(rb.at[pl.ds(early, 2048 - early)], rb.at[pl.ds(early, 2048 - early)], row_r.at[1]).wait()

    def along(bit):
        ny = y + 1 - 2 * (y % 2) if bit == 2 else y
        nz = z + 1 - 2 * (z % 2) if bit == 0 else 3 - z if bit == 1 else z
        return (2 * x + k, 4 * ny + nz)

    def between(src, dst, n, send, recv, device):
        return pltpu.make_async_remote_copy(
            src_ref=xs.at[k, pl.ds(src, n)], dst_ref=xs.at[k, pl.ds(dst, n)],
            send_sem=send, recv_sem=recv, device_id=device, device_id_type=MESH,
        )

    def pair_copy(i, start, n):
        return between(start, start, n, pair_s.at[i], pair_r.at[i], sibling)

    def block_copy(bit, c):
        at, n = CHUNKS[c]
        src = pl.multiple_of(pick(p, SEND[bit]) + at, 16)
        return between(src, SLOT[1 + bit] + at, n, ici_s.at[bit, c], ici_r.at[bit, c], along(bit))

    n_chunks = len(CHUNKS)
    copies = [[block_copy(bit, c) for c in range(n_chunks)] for bit in range(3)]
    block_pairs = [[pair_copy(3 + bit * n_chunks + c, SLOT[1 + bit] + CHUNKS[c][0], CHUNKS[c][1]) for c in range(n_chunks)] for bit in range(3)]
    own_pair, second_pair = pair_copy(0, 0, ROWS), pair_copy(1, SECOND, ROWS)
    patch_pair, head_pair = pair_copy(2, PATCH, QUARTER), pair_copy(3 + 3 * n_chunks, HEAD, HEAD_ROWS)
    has_patch = (p != 1) & (p != 4) & (p != 5)
    has_head = (p != 2) & (p != 6) & (p != 4)
    gives_head = (p != 2) & (p != 6) & (p != 0)

    def patch_copy(i):
        frm, to, bit, src = PATCHES[i]
        return between(src, PATCH, QUARTER, patch_s.at[i % 2], patch_r, along(bit))

    def head_copy(bit):
        return between(SECOND, HEAD, HEAD_ROWS, head_s, head_r, along(bit))

    def own_sends(c):
        @pl.when(p != 6)
        def _():
            copies[0][c].start()

        @pl.when(p != 2)
        def _():
            copies[1][c].start()

        @pl.when(p == 6)
        def _():
            copies[2][c].start()

        if CHUNKS[c][0] + CHUNKS[c][1] == ROWS:
            @pl.when(p == 4)
            def _():
                patch_copy(0).start()

    def unpacked(at, n):
        rows = slice(at, at + n)
        return (part[rows, :] + dot(q[rows, early:], rb[early:, :])).astype(BF16)

    for at in range(0, ROWS, QUARTER):
        xs[k, pl.ds(at, QUARTER), :] = unpacked(at, QUARTER)
        for c in range(n_chunks):
            if at <= CHUNKS[c][0] < at + QUARTER:
                own_sends(c)

    own_pair.start()
    xs[k, pl.ds(SECOND, ROWS), :] = unpacked(ROWS, ROWS)
    for c in range(n_chunks):
        @pl.when(p == 6)
        def _():
            copies[0][c].start()

        @pl.when(p == 2)
        def _():
            copies[1][c].start()
            copies[2][c].start()

    second_pair.start()
    for v, bit in ((1, 0), (3, 1), (7, 2), (5, 1), (4, 0)):
        @pl.when(p == v)
        def _():
            head_copy(bit).start()

    mine = pl.multiple_of(QUARTER * k, QUARTER)
    starts = SLOT + (SECOND,)

    def columns_of(s):
        return pl.multiple_of(starts[s] + mine, QUARTER)

    def tile(j, nj, i, ni):
        return dot_t(xs[0, pl.ds(j, nj), :], xs[0, pl.ds(i, ni), :]) + dot_t(
            xs[1, pl.ds(j, nj), :], xs[1, pl.ds(i, ni), :]
        )

    def top(t):
        return jnp.max(t, axis=0, keepdims=True)

    def meet(s, j, nj):
        t = tile(j, nj, columns_of(s), QUARTER)
        if j <= starts[s] < j + nj:
            t = jnp.where(iota((nj, QUARTER), 0) == iota((nj, QUARTER), 1) + (starts[s] - j + mine), -1.0, t)
        acc[s] = jnp.maximum(acc[s], top(t))

    def across(t):
        m = t[:, :128]
        for i in range(128, t.shape[1], 128):
            m = jnp.maximum(m, t[:, i : i + 128])
        return jnp.max(jnp.transpose(m), axis=0, keepdims=True)

    def late(at):
        rows, lanes = SLOT[3] + at, pl.ds(at, QUARTER)

        def against(s):
            t = tile(rows, QUARTER, columns_of(s), QUARTER)
            acc[s] = jnp.maximum(acc[s], top(t))
            return t

        t = jnp.maximum(jnp.maximum(against(0), against(1)), against(2))
        last[:, lanes] = across(t)

        @pl.when(large_only)
        def _():
            last[:, lanes] = jnp.maximum(last[:, lanes], across(against(4)))

        @pl.when(k == at // QUARTER)
        def _():
            t = tile(rows, QUARTER, rows, QUARTER)
            same = iota((QUARTER, QUARTER), 0) == iota((QUARTER, QUARTER), 1)
            last[:, lanes] = jnp.maximum(last[:, lanes], top(jnp.where(same, -1.0, t)))

        if at:
            @pl.when(k == 0)
            def _():
                t = tile(rows, QUARTER, SLOT[3], QUARTER)
                last[:, 0:QUARTER] = jnp.maximum(last[:, 0:QUARTER], top(t))
                last[:, lanes] = jnp.maximum(last[:, lanes], across(t))

    ob[...] = jnp.full(ob.shape, -1.0, F32)
    acc[...] = jnp.full(acc.shape, -1.0, F32)
    rest_row = jnp.where(k == 0, rest_ids[:, :QUARTER], rest_ids[:, QUARTER:])

    own_pair.wait_recv()
    meet(0, 0, ROWS)
    for c in range(n_chunks):
        copies[0][c].wait_recv()
        copies[1][c].wait_recv()

        @pl.when(jnp.logical_not(large_only))
        def _():
            copies[2][c].start()

        block_pairs[0][c].start()
        block_pairs[1][c].start()
        if CHUNKS[c][0] + CHUNKS[c][1] == QUARTER:
            @pl.when(p == 6)
            def _():
                patch_copy(1).start()

            @pl.when(p == 2)
            def _():
                patch_copy(3).start()

    @pl.when(p == 6)
    def _():
        patch_copy(2).start()

    @pl.when(p == 2)
    def _():
        patch_copy(4).start()

    second_pair.wait_recv()
    t = tile(SECOND, ROWS, columns_of(4), QUARTER)
    own = iota((ROWS, QUARTER), 0) == iota((ROWS, QUARTER), 1) + mine
    acc[4] = top(jnp.where((rest_col == rest_row) & jnp.logical_not(own), t, -1.0))
    for c in range(n_chunks):
        block_pairs[0][c].wait_recv()
        block_pairs[1][c].wait_recv()
    meet(0, ROWS, 2 * ROWS)
    meet(1, 0, 3 * ROWS)
    meet(2, 0, 3 * ROWS)

    @pl.when(large_only)
    def _():
        for s in range(3):
            meet(s, SECOND, ROWS)
        meet(4, 0, 3 * ROWS)

    for c in range(n_chunks - 1):
        copies[2][c].wait_recv()
        block_pairs[2][c].start()
    for c in range(n_chunks):
        if sum(CHUNKS[c]) <= QUARTER:
            block_pairs[2][c].wait_recv()
    late(0)
    copies[2][n_chunks - 1].wait_recv()
    block_pairs[2][n_chunks - 1].start()

    @pl.when(has_head)
    def _():
        head_copy(0).wait_recv()
        head_pair.start()

    @pl.when(has_patch)
    def _():
        patch_copy(0).wait_recv()
        patch_pair.start()

    for c in range(n_chunks):
        if sum(CHUNKS[c]) > QUARTER:
            block_pairs[2][c].wait_recv()
    late(QUARTER)

    def raise_to(b, at, n, v):
        ob[b, :, pl.ds(at, n)] = jnp.maximum(ob[b, :, pl.ds(at, n)], v)

    @pl.when(has_head)
    def _():
        head_pair.wait_recv()
        nxt = labs[share + 1]
        head_ids = jnp.where(nxt == large, labs[share + 11], nxt).astype(F32)
        head_col = column(head_ids)[:HEAD_ROWS]
        t = jnp.where(head_col == rest_row, tile(HEAD, HEAD_ROWS, columns_of(4), QUARTER), -1.0)
        acc[4] = jnp.maximum(acc[4], top(t))
        m = across(jnp.concatenate([t, jnp.full((ROWS - HEAD_ROWS, QUARTER), -1.0, F32)], axis=0))
        raise_to(share + 1, 0, ROWS, jnp.where(nxt == large, -1.0, m))
        raise_to(share + 11, 0, ROWS, jnp.where(nxt == large, m, -1.0))

    @pl.when(has_patch)
    def _():
        patch_pair.wait_recv()
        def meets(start):
            t = tile(PATCH, QUARTER, pl.multiple_of(start + mine, QUARTER), QUARTER)
            s = jnp.where(start == SECOND, 4, start // ROWS)
            acc[s] = jnp.maximum(acc[s], top(t))
            return across(t)

        at = pl.multiple_of(QUARTER * pick(p, PATCH_HALF), QUARTER)
        v = pick(p, PATCH_BLOCK)
        here = labs[v, :, pl.ds(at, QUARTER)] == large

        def give(m):
            raise_to(v, at, QUARTER, jnp.where(here, m, -1.0))
            raise_to(v + 10, at, QUARTER, jnp.where(here, -1.0, m))

        give(meets(pick(p, PATCH_MEETS)))

        @pl.when(p == 2)
        def _():
            give(meets(jnp.int32(SLOT[2])))

    for s in range(3):
        v = pick(p, tuple(h[s] for h in HELD))
        here = labs[v, :, pl.ds(mine, QUARTER)] == large
        raise_to(v, mine, QUARTER, jnp.where(here, acc[s], -1.0))

        @pl.when(v < 6)
        def _():
            raise_to(v + 10, mine, QUARTER, jnp.where(here, -1.0, acc[s]))

    last[:, pl.ds(mine, QUARTER)] = jnp.maximum(last[:, pl.ds(mine, QUARTER)], acc[3])
    v = pick(p, tuple(h[3] for h in HELD))
    in_large = labs[v] == large
    raise_to(v, 0, ROWS, jnp.where(in_large, last[...], -1.0))

    @pl.when(v < 6)
    def _():
        raise_to(v + 10, 0, ROWS, jnp.where(in_large, -1.0, last[...]))

    here = labs[first, :, pl.ds(mine, QUARTER)] == large
    raise_to(second, mine, QUARTER, jnp.where(here, acc[4], -1.0))
    raise_to(first, mine, QUARTER, jnp.where(here, -1.0, acc[4]))

    def send_best(b, carry):
        to_self = at_home & (b == col)

        @pl.when(to_self)
        def _():
            pltpu.make_async_copy(ob.at[b], fin.at[p * 2 + k], fin_r).start()

        @pl.when(jnp.logical_not(to_self))
        def _():
            pltpu.make_async_remote_copy(
                src_ref=ob.at[b], dst_ref=fin.at[p * 2 + k],
                send_sem=fin_s, recv_sem=fin_r, device_id=(group, b), device_id_type=MESH,
            ).start()

        return carry

    lax.fori_loop(0, 16, send_best, 0)

    pltpu.make_async_copy(sbuf.at[0, pl.ds(0, 1008)], sbuf.at[0, pl.ds(0, 1008)], row_s).wait()
    pltpu.make_async_copy(sbuf.at[0], sbuf.at[0], row_s).wait()
    pltpu.make_async_copy(meta_s.at[pl.ds(0, 63)], meta_s.at[pl.ds(0, 63)], meta_ss).wait()
    meta_pair.wait_send()
    for per_bit in copies + block_pairs:
        for cp in per_bit:
            cp.wait_send()
    own_pair.wait_send()
    second_pair.wait_send()

    @pl.when(has_head)
    def _():
        head_pair.wait_send()

    @pl.when(has_patch)
    def _():
        patch_pair.wait_send()

    @pl.when(gives_head)
    def _():
        head_copy(0).wait_send()

    for v, which in ((4, (0,)), (6, (1, 2)), (2, (3, 4))):
        @pl.when(p == v)
        def _():
            for i in which:
                patch_copy(i).wait_send()

    @pl.when(at_home)
    def _():
        pltpu.make_async_copy(labs.at[pl.ds(0, 15)], labs.at[pl.ds(0, 15)], lab_s).wait()
        pltpu.make_async_copy(fin.at[pl.ds(0, 15)], fin.at[pl.ds(0, 15)], fin_s).wait()

    @pl.when(jnp.logical_not(at_home))
    def _():
        pltpu.make_async_copy(labs, labs, lab_s).wait()
        pltpu.make_async_copy(fin, fin, fin_s).wait()

    pltpu.make_async_copy(fin, fin, fin_r).wait()
    best = fin[0]
    for i in range(1, 16):
        best = jnp.maximum(best, fin[i])
    out_ref[...] = best


def shards(embeddings, dest_pos, cluster_ids):
    dma, n_pairs = pltpu.SemaphoreType.DMA, 4 + 3 * len(CHUNKS)
    return pl.pallas_call(
        kernel,
        out_shape=jax.ShapeDtypeStruct((1, ROWS), F32),
        in_specs=[
            pl.BlockSpec(memory_space=pltpu.HBM),
            pl.BlockSpec(memory_space=pltpu.HBM),
            pl.BlockSpec(memory_space=pltpu.HBM),
        ],
        out_specs=pl.BlockSpec(memory_space=pltpu.VMEM),
        scratch_shapes=[
            pltpu.VMEM((ROWS, WIDTH), F32),
            pltpu.VMEM((1, ROWS), I32),
            pltpu.VMEM((1, ROWS), I32),
            pltpu.VMEM((ROWS, WIDTH), BF16),
            pltpu.VMEM((2, 1024, HALF), BF16),
            pltpu.VMEM((16 * DEVS, HALF), BF16),
            pltpu.VMEM((2 * ROWS, HALF), F32),
            pltpu.VMEM((64, 1, 128), F32),
            pltpu.VMEM((DEVS, 1, 128), F32),
            pltpu.VMEM((16, 1, ROWS), I32),
            pltpu.VMEM((2 * ROWS, 16 * DEVS), BF16),
            pltpu.VMEM((2, X_ROWS, HALF), BF16),
            pltpu.VMEM((5, 1, QUARTER), F32),
            pltpu.VMEM((1, ROWS), F32),
            pltpu.VMEM((16, 1, ROWS), F32),
            pltpu.VMEM((16, 1, ROWS), F32),
            dma, dma, dma, dma, dma, dma((2,)), dma, dma, dma, dma, dma, dma,
            dma((3, len(CHUNKS))), dma((3, len(CHUNKS))), dma((n_pairs,)), dma((n_pairs,)),
            dma((2,)), dma, dma, dma, dma, dma,
        ],
        compiler_params=pltpu.CompilerParams(
            collective_id=0, has_side_effects=True, vmem_limit_bytes=62 * 2**20
        ),
        name="best_match",
    )(embeddings, dest_pos.reshape(1, ROWS), cluster_ids)


def solution(mesh):
    return jax.shard_map(
        shards,
        mesh=mesh,
        in_specs=(P(("row", "col"), None), P(("row", "col")), P("row", "col")),
        out_specs=P("row", "col"),
        check_vma=False,
    )
```

```python
import functools

import jax
import jax.numpy as jnp
from jax import lax
from jax.experimental import pallas as pl
from jax.experimental.pallas import tpu as pltpu
from jax.sharding import PartitionSpec as P

MESH = pl.DeviceIdType.MESH
F32, BF16, I32 = jnp.float32, jnp.bfloat16, jnp.int32
DEVS = 128
ROWS = 512
WIDTH = 1024
HALF = WIDTH // 2
QUARTER = ROWS // 2
CHIP = (0, 1, 7, 2, 5, 4, 6, 3)
VERTEX = (0, 1, 3, 7, 5, 4, 6, 2)
HELD = ((0, 1, 9, 4), (1, 0, 2, 3), (8, 2, 0, 6), (2, 8, 1, 7), (5, 4, 6, 1), (4, 5, 3, 2), (6, 3, 5, 9), (3, 7, 4, 8))
SLOT = (0, 512, 1024, 1536)
SECOND, PATCH, HEAD, TAIL = 2048, 2560, 2816, 2960
EDGE = 144
X_ROWS = TAIL + EDGE
SEND = (
    (0, 0, 0, 0, 0, 0, SECOND, 0),
    (0, 0, SECOND, 0, 0, 0, 0, 0),
    (512, 1024, SECOND, 512, 512, 1024, 0, 512),
)
PATCH_BLOCK = (5, 0, 5, 0, 0, 0, 0, 5)
PATCH_HALF = (1, 0, 0, 0, 0, 0, 1, 1)
PATCH_MEETS = (0, 0, 0, 1536, 0, 0, SECOND, 1536)
PATCHES = ((4, 0, 2, 256), (6, 2, 2, 1024), (6, 7, 0, 1280), (2, 3, 0, 1024), (2, 6, 2, 1280))
MEET = (
    ((0, 1), (0, 2), (1, 2)), ((0, 1), (0, 2), (1, 2)), ((0, 2), (0, 4), (1, 4)), ((0, 1), (0, 2), (1, 2)),
    ((0, 1), (0, 2), (1, 2)), ((0, 1), (0, 2), (1, 2)), ((0, 1), (0, 4), (2, 4)), ((0, 1), (0, 2), (1, 2)),
)
CHUNKS = ((0, 128), (128, 128), (256, 128), (384, 128))
STRIDE, INVERSE, EARLY = 45, 37, 48


def pick(p, table):
    out = jnp.int32(table[0])
    for i in range(1, len(table)):
        if table[i] != table[0]:
            out = jnp.where(p == i, jnp.int32(table[i]), out)
    return out


def iota(shape, dim):
    return lax.broadcasted_iota(I32, shape, dim)


def ones(cond):
    return jnp.where(cond, jnp.float32(1.0), jnp.float32(0.0)).astype(BF16)


def dot_t(a, b):
    return lax.dot_general(a, b, (((1,), (1,)), ((), ())), preferred_element_type=F32)


def dot(a, b):
    return lax.dot_general(a, b, (((1,), (0,)), ((), ())), preferred_element_type=F32)


def kernel(
    emb_hbm, dest_hbm, ids_hbm, fin,
    emb, dest_ref, ids_ref, unit, sbuf, rb, part, meta_s, meta_r, labs, q, xs, acc, last, ob,
    emb_sem, dest_sem, ids_sem, own_sem, row_s, row_r, meta_ss, meta_rr, meta_ps, meta_pr, lab_s, lab_r,
    ici_s, ici_r, pair_s, pair_r, patch_s, patch_r, edge_s, edge_r, fin_s, fin_r,
):
    row, col = lax.axis_index("row"), lax.axis_index("col")
    x, k, y, z = row // 2, row % 2, col // 4, col % 4
    chip = x * 16 + y * 4 + z
    group = 2 * x + y // 2
    p = (y % 2) * 4 + (z // 2) * 2 + (z // 2 + z) % 2
    share = pick(p, CHIP)
    large_only = (p == 2) | (p == 6)

    dest_copy = pltpu.make_async_copy(dest_hbm, dest_ref, dest_sem)
    dest_copy.start()
    emb_copy = pltpu.make_async_copy(emb_hbm, emb, emb_sem)
    emb_copy.start()
    ids_copy = pltpu.make_async_copy(ids_hbm, ids_ref, ids_sem)
    ids_copy.start()

    def relative(n):
        off = (n * STRIDE) % 64
        return (x + off // 16) % 4, (y + off // 4 % 4) % 4, (z + off % 4) % 4

    barrier = pltpu.get_barrier_semaphore()

    def greet(tx, ty, tz, tk):
        pl.semaphore_signal(barrier, inc=1, device_id=(2 * tx + tk, 4 * ty + tz), device_id_type=MESH)

    lead = (x % 2 == 0) & (y % 2 == 0) & (z % 2 == 0)

    @pl.when(jnp.logical_not(lead & (k == 0)))
    def _():
        greet(x - x % 2, y - y % 2, z - z % 2, 0)

    dest_copy.wait()
    dest = dest_ref[...]
    block = lax.shift_right_logical(dest, 9)
    place = dest & 511
    g, b = lax.shift_right_logical(block, 4), block & 15
    to = jnp.where(b < 6, b, jnp.where(b < 8, 6, jnp.where(b < 10, 7, b - 10)))
    half = jnp.where(b < 6, 0, jnp.where(b < 10, b & 1, 1))
    vert = pick(to, VERTEX)
    tx = lax.shift_right_logical(g, 1)
    ty = 2 * (g & 1) + lax.shift_right_logical(vert, 2)
    tz = (vert & 2) + (lax.shift_right_logical(vert, 1) + vert & 1)
    tchip = tx * 16 + ty * 4 + tz
    turn = (((tx - x) & 3) * 16 + ((ty - y) & 3) * 4 + ((tz - z) & 3)) * INVERSE & 3
    tb = tchip * 2 + half
    hot = iota((DEVS, ROWS), 0) == tb
    before = ones(iota((ROWS, ROWS), 0) < iota((ROWS, ROWS), 1))
    rank = dot(ones(hot), before)
    slot = jnp.sum(jnp.where(hot, rank, 0.0), axis=0, keepdims=True).astype(I32)
    line = tb * 8 + slot

    value = place + 1 + 512 * half
    to_chip = iota((64, ROWS), 0) == tchip
    lanes = ones(iota((128, ROWS), 0) == (half * 8 + slot + 16 * (2 * turn + k)))
    high = jnp.where(to_chip, lax.shift_right_logical(value, 4).astype(F32), 0.0).astype(BF16)
    low = jnp.where(to_chip, (value & 15).astype(F32), 0.0).astype(BF16)
    meta = 16.0 * dot_t(high, lanes) + dot_t(low, lanes)
    for n in range(64):
        meta_s[n] = meta[n : n + 1, :]

    emb_copy.wait()
    rows = emb[...]
    scale = lax.rsqrt(jnp.sum(rows * rows, axis=1, keepdims=True) + 1e-06)
    unit[...] = (rows * scale).astype(BF16)
    for a in range(8):
        take = ones(iota((128, ROWS), 0) + 128 * a == line)
        packed = dot(take, unit[...]).astype(BF16)
        sbuf[0, pl.ds(128 * a, 128), :] = packed[:, :HALF]
        sbuf[1, pl.ds(128 * a, 128), :] = packed[:, HALF:]

    @pl.when(lead & (k == 0))
    def _():
        pl.semaphore_wait(barrier, 15)
        for j in range(7, -1, -1):
            greet((x + 2 * (j // 4)) % 4, (y + 2 * (j // 2 % 2)) % 4, (z + 2 * (j % 2)) % 4, 1)
        pl.semaphore_wait(barrier, 1)

    @pl.when(lead & (k == 1))
    def _():
        pl.semaphore_wait(barrier, 8)
        for j in range(15, 0, -1):
            greet(x + j // 8, y + j // 4 % 2, z + j // 2 % 2, (1 + j) % 2)

    @pl.when(jnp.logical_not(lead))
    def _():
        pl.semaphore_wait(barrier, 1)

    def send_rows(e, carry):
        n, tk = e // 2, e % 2
        tx, ty, tz = relative(n)
        pltpu.make_async_remote_copy(
            src_ref=sbuf.at[tk, pl.ds(pl.multiple_of(16 * (tx * 16 + ty * 4 + tz), 16), 16)],
            dst_ref=rb.at[pl.ds(pl.multiple_of(16 * (2 * n + k), 16), 16)],
            send_sem=row_s, recv_sem=row_r.at[n // EARLY],
            device_id=(2 * tx + tk, 4 * ty + tz), device_id_type=MESH,
        ).start()
        return carry

    def send_meta(n, carry):
        tx, ty, tz = relative(n)
        pltpu.make_async_remote_copy(
            src_ref=meta_s.at[tx * 16 + ty * 4 + tz], dst_ref=meta_r.at[64 * k + n],
            send_sem=meta_ss, recv_sem=meta_rr,
            device_id=(2 * tx + k, 4 * ty + tz), device_id_type=MESH,
        ).start()
        return carry

    ids_copy.wait()
    at_home = y // 2 == k

    def send_ids(j, carry):
        hy, hz, hk = 2 * k + j // 8, (j // 2) % 4, j % 2
        to_self = (hy == y) & (hz == z) & (hk == k)

        @pl.when(to_self)
        def _():
            pltpu.make_async_copy(ids_ref, labs.at[col], lab_r).start()

        @pl.when(jnp.logical_not(to_self))
        def _():
            pltpu.make_async_remote_copy(
                src_ref=ids_ref, dst_ref=labs.at[col],
                send_sem=lab_s, recv_sem=lab_r,
                device_id=(2 * x + hk, 4 * hy + hz), device_id_type=MESH,
            ).start()

        return carry

    lax.fori_loop(2, 50, send_rows, 0)
    lax.fori_loop(0, 16, send_ids, 0)
    lax.fori_loop(1, 64, send_meta, 0)
    lax.fori_loop(50, DEVS, send_rows, 0)
    sibling = (2 * x + 1 - k, col)
    own_rows = pl.ds(pl.multiple_of(16 * chip, 16), 16)
    own_slot = pl.ds(pl.multiple_of(16 * k, 16), 16)
    sibling_copy = pltpu.make_async_remote_copy(
        src_ref=sbuf.at[1 - k, own_rows], dst_ref=rb.at[own_slot],
        send_sem=row_s, recv_sem=row_r.at[0], device_id=sibling, device_id_type=MESH,
    )
    sibling_copy.start()
    own_copy = pltpu.make_async_copy(sbuf.at[k, own_rows], rb.at[own_slot], own_sem)
    own_copy.start()
    meta_r[64 * k] = meta_s[chip]
    pltpu.make_async_copy(meta_s.at[pl.ds(0, 63)], meta_s.at[pl.ds(0, 63)], meta_rr).wait()
    meta_pair = pltpu.make_async_remote_copy(
        src_ref=meta_r.at[pl.ds(pl.multiple_of(64 * k, 64), 64)], dst_ref=meta_r.at[pl.ds(pl.multiple_of(64 * k, 64), 64)],
        send_sem=meta_ps, recv_sem=meta_pr, device_id=sibling, device_id_type=MESH,
    )
    meta_pair.start()

    pltpu.make_async_copy(labs, labs, lab_r).wait()
    large = labs[7, :, 0:1]
    first = jnp.where(share < 6, share, 2 * share - 6)
    second = jnp.where(share < 6, share + 10, 2 * share - 5)
    is_large = labs[first] == large
    eye = ones(iota((ROWS, ROWS), 0) == iota((ROWS, ROWS), 1))

    def column(r):
        return dot_t(eye, jnp.broadcast_to(r, (8, ROWS)).astype(BF16))[:, 0:1]

    rest_ids = jnp.where(is_large, labs[second], labs[first]).astype(F32)
    rest_col = column(rest_ids)
    large_col = column(jnp.where(is_large, 1.0, 0.0))
    index_col = iota((ROWS, 1), 0).astype(F32) + 1.0
    key_large = index_col + 512.0 * (1.0 - large_col)
    key_rest = index_col + 512.0 * large_col

    meta_pair.wait_recv()
    for a in range(16):
        r = meta_r[4 * a] + meta_r[64 + 4 * a]
        for i in range(1, 4):
            r = r + (meta_r[4 * a + i] + meta_r[64 + 4 * a + i])
        q[0:ROWS, pl.ds(128 * a, 128)] = ones(key_large == r)
        q[ROWS : 2 * ROWS, pl.ds(128 * a, 128)] = ones(key_rest == r)

    own_copy.wait()
    early = 32 * EARLY
    pltpu.make_async_copy(rb.at[pl.ds(0, early - 16)], rb.at[pl.ds(0, early - 16)], row_r.at[0]).wait()
    part[...] = dot(q[:, 0:early], rb[0:early, :])
    pltpu.make_async_copy(rb.at[pl.ds(early, 2048 - early)], rb.at[pl.ds(early, 2048 - early)], row_r.at[1]).wait()

    def along(bit):
        ny = y + 1 - 2 * (y % 2) if bit == 2 else y
        nz = z + 1 - 2 * (z % 2) if bit == 0 else 3 - z if bit == 1 else z
        return (2 * x + k, 4 * ny + nz)

    def between(src, dst, n, send, recv, device):
        return pltpu.make_async_remote_copy(
            src_ref=xs.at[k, pl.ds(src, n)], dst_ref=xs.at[k, pl.ds(dst, n)],
            send_sem=send, recv_sem=recv, device_id=device, device_id_type=MESH,
        )

    def pair_copy(i, start, n):
        return between(start, start, n, pair_s.at[i], pair_r.at[i], sibling)

    def block_copy(bit, c):
        at, n = CHUNKS[c]
        src = pl.multiple_of(pick(p, SEND[bit]) + at, 16)
        return between(src, SLOT[1 + bit] + at, n, ici_s.at[bit, c], ici_r.at[bit, c], along(bit))

    n_chunks = len(CHUNKS)
    copies = [[block_copy(bit, c) for c in range(n_chunks)] for bit in range(3)]
    block_pairs = [[pair_copy(3 + bit * n_chunks + c, SLOT[1 + bit] + CHUNKS[c][0], CHUNKS[c][1]) for c in range(n_chunks)] for bit in range(3)]
    own_pair, second_pair = pair_copy(0, 0, ROWS), pair_copy(1, SECOND, ROWS)
    patch_pair = pair_copy(2, PATCH, QUARTER)
    head_pair, tail_pair = pair_copy(3 + 3 * n_chunks, HEAD, EDGE), pair_copy(4 + 3 * n_chunks, TAIL, EDGE)
    has_patch = (p != 1) & (p != 4) & (p != 5)
    has_head = (p != 2) & (p != 6) & (p != 4)
    has_tail = (p != 2) & (p != 6) & (p != 0)

    def patch_copy(i):
        frm, to, bit, src = PATCHES[i]
        return between(src, PATCH, QUARTER, patch_s.at[i % 2], patch_r, along(bit))

    def head_copy(bit):
        return between(SECOND, HEAD, EDGE, edge_s.at[0], edge_r.at[0], along(bit))

    def tail_copy(bit):
        return between(SECOND + ROWS - EDGE, TAIL, EDGE, edge_s.at[1], edge_r.at[1], along(bit))

    def own_sends(c):
        @pl.when(p != 6)
        def _():
            copies[0][c].start()

        @pl.when(p != 2)
        def _():
            copies[1][c].start()

        @pl.when(p == 6)
        def _():
            copies[2][c].start()

        if CHUNKS[c][0] + CHUNKS[c][1] == ROWS:
            @pl.when(p == 4)
            def _():
                patch_copy(0).start()

    def unpacked(at, n):
        rows = slice(at, at + n)
        return (part[rows, :] + dot(q[rows, early:], rb[early:, :])).astype(BF16)

    for at in range(0, ROWS, QUARTER):
        xs[k, pl.ds(at, QUARTER), :] = unpacked(at, QUARTER)
        for c in range(n_chunks):
            if at <= CHUNKS[c][0] < at + QUARTER:
                own_sends(c)

    own_pair.start()
    xs[k, pl.ds(SECOND, ROWS), :] = unpacked(ROWS, ROWS)
    for c in range(n_chunks):
        @pl.when(p == 6)
        def _():
            copies[0][c].start()

        @pl.when(p == 2)
        def _():
            copies[1][c].start()
            copies[2][c].start()

    second_pair.start()
    for v, w, bit in ((0, 1, 0), (1, 3, 1), (3, 7, 2), (7, 5, 1), (5, 4, 0)):
        @pl.when(p == v)
        def _():
            tail_copy(bit).start()

        @pl.when(p == w)
        def _():
            head_copy(bit).start()

    mine = pl.multiple_of(QUARTER * k, QUARTER)
    starts = SLOT + (SECOND,)

    meetings = [tuple(pick(p, tuple(m[i][side] for m in MEET)) for side in range(2)) for i in range(3)]

    def columns_of(s):
        return pl.multiple_of(starts[s] + mine, QUARTER)

    def tile(j, nj, i, ni):
        return dot_t(xs[0, pl.ds(j, nj), :], xs[0, pl.ds(i, ni), :]) + dot_t(
            xs[1, pl.ds(j, nj), :], xs[1, pl.ds(i, ni), :]
        )

    def top(t):
        return jnp.max(t, axis=0, keepdims=True)

    def meet(s, other):
        i, j = pl.multiple_of(s * ROWS + mine, QUARTER), pl.multiple_of(other * ROWS, ROWS)
        acc[s] = jnp.maximum(acc[s], top(tile(j, ROWS, i, QUARTER)))

    def across(t):
        m = t[:, :128]
        for i in range(128, t.shape[1], 128):
            m = jnp.maximum(m, t[:, i : i + 128])
        return jnp.max(jnp.transpose(m), axis=0, keepdims=True)

    def late(at):
        rows, lanes = SLOT[3] + at, pl.ds(at, QUARTER)

        def against(s):
            t = tile(rows, QUARTER, columns_of(s), QUARTER)
            acc[s] = jnp.maximum(acc[s], top(t))
            return t

        t = jnp.maximum(jnp.maximum(against(0), against(1)), against(2))
        last[:, lanes] = across(t)

        @pl.when(large_only)
        def _():
            last[:, lanes] = jnp.maximum(last[:, lanes], across(against(4)))

    ob[...] = jnp.full(ob.shape, -1.0, F32)
    acc[...] = jnp.full(acc.shape, -1.0, F32)
    rest_row = jnp.where(k == 0, rest_ids[:, :QUARTER], rest_ids[:, QUARTER:])

    own = iota((ROWS, QUARTER), 0) == iota((ROWS, QUARTER), 1) + mine
    own_pair.wait_recv()
    acc[0] = top(jnp.where(own, -1.0, tile(0, ROWS, columns_of(0), QUARTER)))
    for c in range(n_chunks):
        copies[0][c].wait_recv()
        copies[1][c].wait_recv()

        @pl.when(jnp.logical_not(large_only))
        def _():
            copies[2][c].start()

        block_pairs[0][c].start()
        block_pairs[1][c].start()
        if CHUNKS[c][0] + CHUNKS[c][1] == QUARTER:
            @pl.when(p == 6)
            def _():
                patch_copy(1).start()

            @pl.when(p == 2)
            def _():
                patch_copy(3).start()

    @pl.when(p == 6)
    def _():
        patch_copy(2).start()

    @pl.when(p == 2)
    def _():
        patch_copy(4).start()

    second_pair.wait_recv()
    t = tile(SECOND, ROWS, columns_of(4), QUARTER)
    acc[4] = top(jnp.where((rest_col == rest_row) & jnp.logical_not(own), t, -1.0))
    for c in range(n_chunks):
        block_pairs[0][c].wait_recv()
        block_pairs[1][c].wait_recv()
    for a, b in meetings:
        meet(a, b)
        meet(b, a)
    for c in range(n_chunks - 1):
        copies[2][c].wait_recv()
        block_pairs[2][c].start()
    for c in range(n_chunks):
        if sum(CHUNKS[c]) <= QUARTER:
            block_pairs[2][c].wait_recv()
    @pl.when(has_head)
    def _():
        head_copy(0).wait_recv()
        head_pair.start()

    @pl.when(has_tail)
    def _():
        tail_copy(0).wait_recv()
        tail_pair.start()

    late(0)
    copies[2][n_chunks - 1].wait_recv()
    block_pairs[2][n_chunks - 1].start()

    @pl.when(has_patch)
    def _():
        patch_copy(0).wait_recv()
        patch_pair.start()

    def raise_to(b, at, n, v):
        ob[b, :, pl.ds(at, n)] = jnp.maximum(ob[b, :, pl.ds(at, n)], v)

    def beside(pair, start, step, at):
        pair.wait_recv()
        ids = labs[share + step]
        is_here = ids == large
        there = jnp.where(is_here, labs[share + step + 10], ids).astype(F32)
        where = ROWS - EDGE if at else 0
        t = tile(start, EDGE, columns_of(4), QUARTER)
        t = jnp.where(column(there)[where : where + EDGE] == rest_row, t, -1.0)
        acc[4] = jnp.maximum(acc[4], top(t))
        none = jnp.full((QUARTER - EDGE, QUARTER), -1.0, F32)
        m = across(jnp.concatenate([none, t] if at else [t, none], axis=0))
        is_here = is_here[:, at : at + QUARTER]
        raise_to(share + step, at, QUARTER, jnp.where(is_here, -1.0, m))
        raise_to(share + step + 10, at, QUARTER, jnp.where(is_here, m, -1.0))

    @pl.when(has_head)
    def _():
        beside(head_pair, HEAD, 1, 0)

    @pl.when(has_tail)
    def _():
        beside(tail_pair, TAIL, -1, QUARTER)

    for c in range(n_chunks):
        if sum(CHUNKS[c]) > QUARTER:
            block_pairs[2][c].wait_recv()
    late(QUARTER)

    @pl.when(has_patch)
    def _():
        patch_pair.wait_recv()
        def meets(start):
            t = tile(PATCH, QUARTER, pl.multiple_of(start + mine, QUARTER), QUARTER)
            s = jnp.where(start == SECOND, 4, start // ROWS)
            acc[s] = jnp.maximum(acc[s], top(t))
            return across(t)

        at = pl.multiple_of(QUARTER * pick(p, PATCH_HALF), QUARTER)
        v = pick(p, PATCH_BLOCK)
        here = labs[v, :, pl.ds(at, QUARTER)] == large

        def give(m):
            raise_to(v, at, QUARTER, jnp.where(here, m, -1.0))
            raise_to(v + 10, at, QUARTER, jnp.where(here, -1.0, m))

        give(meets(pick(p, PATCH_MEETS)))

        @pl.when(p == 2)
        def _():
            give(meets(jnp.int32(SLOT[2])))

    def give_block(v, at, n, m):
        here = labs[v, :, pl.ds(at, n)] == large
        raise_to(v, at, n, jnp.where(here, m, -1.0))
        raise_to(jnp.minimum(v + 10, 15), at, n, jnp.where(here | (v >= 6), -1.0, m))

    for s in range(3):
        give_block(pick(p, tuple(h[s] for h in HELD)), mine, QUARTER, acc[s])
    last[:, pl.ds(mine, QUARTER)] = jnp.maximum(last[:, pl.ds(mine, QUARTER)], acc[3])
    give_block(pick(p, tuple(h[3] for h in HELD)), 0, ROWS, last[...])
    here = labs[first, :, pl.ds(mine, QUARTER)] == large
    raise_to(second, mine, QUARTER, jnp.where(here, acc[4], -1.0))
    raise_to(first, mine, QUARTER, jnp.where(here, -1.0, acc[4]))

    def send_best(b, carry):
        to_self = at_home & (b == col)

        @pl.when(to_self)
        def _():
            pltpu.make_async_copy(ob.at[b], fin.at[p * 2 + k], fin_r).start()

        @pl.when(jnp.logical_not(to_self))
        def _():
            pltpu.make_async_remote_copy(
                src_ref=ob.at[b], dst_ref=fin.at[p * 2 + k],
                send_sem=fin_s, recv_sem=fin_r, device_id=(group, b), device_id_type=MESH,
            ).start()

        return carry

    lax.fori_loop(0, 16, send_best, 0)

    pltpu.make_async_copy(sbuf.at[0, pl.ds(0, 1008)], sbuf.at[0, pl.ds(0, 1008)], row_s).wait()
    pltpu.make_async_copy(sbuf.at[0], sbuf.at[0], row_s).wait()
    pltpu.make_async_copy(meta_s.at[pl.ds(0, 63)], meta_s.at[pl.ds(0, 63)], meta_ss).wait()
    meta_pair.wait_send()
    for per_bit in copies + block_pairs:
        for cp in per_bit:
            cp.wait_send()
    own_pair.wait_send()
    second_pair.wait_send()

    @pl.when(has_head)
    def _():
        head_pair.wait_send()
        tail_copy(0).wait_send()

    @pl.when(has_tail)
    def _():
        tail_pair.wait_send()
        head_copy(0).wait_send()

    @pl.when(has_patch)
    def _():
        patch_pair.wait_send()

    for v, which in ((4, (0,)), (6, (1, 2)), (2, (3, 4))):
        @pl.when(p == v)
        def _():
            for i in which:
                patch_copy(i).wait_send()

    @pl.when(at_home)
    def _():
        pltpu.make_async_copy(labs.at[pl.ds(0, 15)], labs.at[pl.ds(0, 15)], lab_s).wait()
        pltpu.make_async_copy(fin.at[pl.ds(0, 15)], fin.at[pl.ds(0, 15)], fin_s).wait()

    @pl.when(jnp.logical_not(at_home))
    def _():
        pltpu.make_async_copy(labs, labs, lab_s).wait()
        pltpu.make_async_copy(fin, fin, fin_s).wait()

    pltpu.make_async_copy(fin, fin, fin_r).wait()


def shards(embeddings, dest_pos, cluster_ids):
    dma, n_pairs = pltpu.SemaphoreType.DMA, 5 + 3 * len(CHUNKS)
    bests = pl.pallas_call(
        kernel,
        out_shape=jax.ShapeDtypeStruct((16, 1, ROWS), F32),
        in_specs=[
            pl.BlockSpec(memory_space=pltpu.HBM),
            pl.BlockSpec(memory_space=pltpu.HBM),
            pl.BlockSpec(memory_space=pltpu.HBM),
        ],
        out_specs=pl.BlockSpec(memory_space=pltpu.HBM),
        scratch_shapes=[
            pltpu.VMEM((ROWS, WIDTH), F32),
            pltpu.VMEM((1, ROWS), I32),
            pltpu.VMEM((1, ROWS), I32),
            pltpu.VMEM((ROWS, WIDTH), BF16),
            pltpu.VMEM((2, 1024, HALF), BF16),
            pltpu.VMEM((16 * DEVS, HALF), BF16),
            pltpu.VMEM((2 * ROWS, HALF), F32),
            pltpu.VMEM((64, 1, 128), F32),
            pltpu.VMEM((DEVS, 1, 128), F32),
            pltpu.VMEM((16, 1, ROWS), I32),
            pltpu.VMEM((2 * ROWS, 16 * DEVS), BF16),
            pltpu.VMEM((2, X_ROWS, HALF), BF16),
            pltpu.VMEM((5, 1, QUARTER), F32),
            pltpu.VMEM((1, ROWS), F32),
            pltpu.VMEM((16, 1, ROWS), F32),
            dma, dma, dma, dma, dma, dma((2,)), dma, dma, dma, dma, dma, dma,
            dma((3, len(CHUNKS))), dma((3, len(CHUNKS))), dma((n_pairs,)), dma((n_pairs,)),
            dma((2,)), dma, dma((2,)), dma((2,)), dma, dma,
        ],
        compiler_params=pltpu.CompilerParams(
            collective_id=0, has_side_effects=True, vmem_limit_bytes=62 * 2**20
        ),
        name="best_match",
    )(embeddings, dest_pos.reshape(1, ROWS), cluster_ids)
    return jnp.max(bests, axis=0)


def solution(mesh):
    return jax.shard_map(
        shards,
        mesh=mesh,
        in_specs=(P(("row", "col"), None), P(("row", "col")), P("row", "col")),
        out_specs=P("row", "col"),
        check_vma=False,
    )
```

```python
import functools

import jax
import jax.numpy as jnp
from jax import lax
from jax.experimental import pallas as pl
from jax.experimental.pallas import tpu as pltpu
from jax.sharding import PartitionSpec as P

MESH = pl.DeviceIdType.MESH
F32, BF16, I32 = jnp.float32, jnp.bfloat16, jnp.int32
DEVS = 128
ROWS = 512
WIDTH = 1024
HALF = WIDTH // 2
QUARTER = ROWS // 2
CHIP = (0, 1, 7, 2, 5, 4, 6, 3)
VERTEX = (0, 1, 3, 7, 5, 4, 6, 2)
HELD = ((0, 1, 9, 4), (1, 0, 2, 3), (8, 2, 0, 6), (2, 8, 1, 7), (5, 4, 6, 1), (4, 5, 3, 2), (6, 3, 5, 9), (3, 7, 4, 8))
SLOT = (0, 512, 1024, 1536)
SECOND, PATCH, HEAD, TAIL = 2048, 2560, 2816, 2960
EDGE = 144
X_ROWS = TAIL + EDGE
SEND = (
    (0, 0, 0, 0, 0, 0, SECOND, 0),
    (0, 0, SECOND, 0, 0, 0, 0, 0),
    (512, 1024, SECOND, 512, 512, 1024, 0, 512),
)
PATCH_BLOCK = (5, 0, 5, 0, 0, 0, 0, 5)
PATCH_HALF = (1, 0, 0, 0, 0, 0, 1, 1)
PATCH_MEETS = (0, 0, 0, 1536, 0, 0, SECOND, 1536)
PATCHES = ((4, 0, 2, 256), (6, 2, 2, 1024), (6, 7, 0, 1280), (2, 3, 0, 1024), (2, 6, 2, 1280))
MEET = (
    ((0, 1), (0, 2), (1, 2)), ((0, 1), (0, 2), (1, 2)), ((0, 2), (0, 4), (1, 4)), ((0, 1), (0, 2), (1, 2)),
    ((0, 1), (0, 2), (1, 2)), ((0, 1), (0, 2), (1, 2)), ((0, 1), (0, 4), (2, 4)), ((0, 1), (0, 2), (1, 2)),
)
CHUNKS = ((0, 128), (128, 128), (256, 128), (384, 128))
STRIDE, INVERSE, EARLY = 45, 37, 48


def pick(p, table):
    out = jnp.int32(table[0])
    for i in range(1, len(table)):
        if table[i] != table[0]:
            out = jnp.where(p == i, jnp.int32(table[i]), out)
    return out


def iota(shape, dim):
    return lax.broadcasted_iota(I32, shape, dim)


def ones(cond):
    return jnp.where(cond, jnp.float32(1.0), jnp.float32(0.0)).astype(BF16)


def dot_t(a, b):
    return lax.dot_general(a, b, (((1,), (1,)), ((), ())), preferred_element_type=F32)


def dot(a, b):
    return lax.dot_general(a, b, (((1,), (0,)), ((), ())), preferred_element_type=F32)


def kernel(
    emb_hbm, dest_hbm, ids_hbm, fin,
    emb, dest_ref, ids_ref, unit, sbuf, rb, part, meta_s, meta_r, labs, q, xs, acc, last, ob,
    emb_sem, dest_sem, ids_sem, own_sem, row_s, row_r, meta_ss, meta_rr, meta_ps, meta_pr, lab_s, lab_r,
    ici_s, ici_r, pair_s, pair_r, patch_s, patch_r, edge_s, edge_r, fin_s, fin_r,
):
    row, col = lax.axis_index("row"), lax.axis_index("col")
    x, k, y, z = row // 2, row % 2, col // 4, col % 4
    chip = x * 16 + y * 4 + z
    group = 2 * x + y // 2
    p = (y % 2) * 4 + (z // 2) * 2 + (z // 2 + z) % 2
    share = pick(p, CHIP)
    large_only = (p == 2) | (p == 6)

    dest_copy = pltpu.make_async_copy(dest_hbm, dest_ref, dest_sem)
    dest_copy.start()
    emb_copy = pltpu.make_async_copy(emb_hbm, emb, emb_sem)
    emb_copy.start()
    ids_copy = pltpu.make_async_copy(ids_hbm, ids_ref, ids_sem)
    ids_copy.start()

    def relative(n):
        off = (n * STRIDE) % 64
        return (x + off // 16) % 4, (y + off // 4 % 4) % 4, (z + off % 4) % 4

    barrier = pltpu.get_barrier_semaphore()

    def greet(tx, ty, tz, tk):
        pl.semaphore_signal(barrier, inc=1, device_id=(2 * tx + tk, 4 * ty + tz), device_id_type=MESH)

    lead = (x % 2 == 0) & (y % 2 == 1) & (z % 2 == 0)

    @pl.when(jnp.logical_not(lead & (k == 0)))
    def _():
        greet(x - x % 2, y - y % 2 + 1, z - z % 2, 0)

    dest_copy.wait()
    dest = dest_ref[...]
    block = lax.shift_right_logical(dest, 9)
    place = dest & 511
    g, b = lax.shift_right_logical(block, 4), block & 15
    to = jnp.where(b < 6, b, jnp.where(b < 8, 6, jnp.where(b < 10, 7, b - 10)))
    half = jnp.where(b < 6, 0, jnp.where(b < 10, b & 1, 1))
    vert = pick(to, VERTEX)
    tx = lax.shift_right_logical(g, 1)
    ty = 2 * (g & 1) + lax.shift_right_logical(vert, 2)
    tz = (vert & 2) + (lax.shift_right_logical(vert, 1) + vert & 1)
    tchip = tx * 16 + ty * 4 + tz
    turn = (((tx - x) & 3) * 16 + ((ty - y) & 3) * 4 + ((tz - z) & 3)) * INVERSE & 3
    tb = tchip * 2 + half
    hot = iota((DEVS, ROWS), 0) == tb
    before = ones(iota((ROWS, ROWS), 0) < iota((ROWS, ROWS), 1))
    rank = dot(ones(hot), before)
    slot = jnp.sum(jnp.where(hot, rank, 0.0), axis=0, keepdims=True).astype(I32)
    line = tb * 8 + slot

    value = place + 1 + 512 * half
    to_chip = iota((64, ROWS), 0) == tchip
    lanes = ones(iota((128, ROWS), 0) == (half * 8 + slot + 16 * (2 * turn + k)))
    high = jnp.where(to_chip, lax.shift_right_logical(value, 4).astype(F32), 0.0).astype(BF16)
    low = jnp.where(to_chip, (value & 15).astype(F32), 0.0).astype(BF16)
    meta = 16.0 * dot_t(high, lanes) + dot_t(low, lanes)
    for n in range(64):
        meta_s[n] = meta[n : n + 1, :]

    emb_copy.wait()
    rows = emb[...]
    scale = lax.rsqrt(jnp.sum(rows * rows, axis=1, keepdims=True) + 1e-06)
    unit[...] = (rows * scale).astype(BF16)
    for a in range(8):
        take = ones(iota((128, ROWS), 0) + 128 * a == line)
        packed = dot(take, unit[...]).astype(BF16)
        sbuf[0, pl.ds(128 * a, 128), :] = packed[:, :HALF]
        sbuf[1, pl.ds(128 * a, 128), :] = packed[:, HALF:]

    @pl.when(lead & (k == 0))
    def _():
        pl.semaphore_wait(barrier, 15)
        for j in range(7, -1, -1):
            greet((x + 2 * (j // 4)) % 4, (y + 2 * (j // 2 % 2)) % 4, (z + 2 * (j % 2)) % 4, 1)
        pl.semaphore_wait(barrier, 1)

    @pl.when(lead & (k == 1))
    def _():
        pl.semaphore_wait(barrier, 8)
        for j in range(15, 0, -1):
            greet(x + j // 8, y - j // 4 % 2, z + j // 2 % 2, (1 + j) % 2)

    @pl.when(jnp.logical_not(lead))
    def _():
        pl.semaphore_wait(barrier, 1)

    def send_rows(e, carry):
        n, tk = e // 2, e % 2
        tx, ty, tz = relative(n)
        pltpu.make_async_remote_copy(
            src_ref=sbuf.at[tk, pl.ds(pl.multiple_of(16 * (tx * 16 + ty * 4 + tz), 16), 16)],
            dst_ref=rb.at[pl.ds(pl.multiple_of(16 * (2 * n + k), 16), 16)],
            send_sem=row_s, recv_sem=row_r.at[n // EARLY],
            device_id=(2 * tx + tk, 4 * ty + tz), device_id_type=MESH,
        ).start()
        return carry

    def send_meta(n, carry):
        tx, ty, tz = relative(n)
        pltpu.make_async_remote_copy(
            src_ref=meta_s.at[tx * 16 + ty * 4 + tz], dst_ref=meta_r.at[64 * k + n],
            send_sem=meta_ss, recv_sem=meta_rr,
            device_id=(2 * tx + k, 4 * ty + tz), device_id_type=MESH,
        ).start()
        return carry

    ids_copy.wait()
    at_home = y // 2 == k

    def send_ids(j, carry):
        hy, hz, hk = 2 * k + j // 8, (j // 2) % 4, j % 2
        to_self = (hy == y) & (hz == z) & (hk == k)

        @pl.when(to_self)
        def _():
            pltpu.make_async_copy(ids_ref, labs.at[col], lab_r).start()

        @pl.when(jnp.logical_not(to_self))
        def _():
            pltpu.make_async_remote_copy(
                src_ref=ids_ref, dst_ref=labs.at[col],
                send_sem=lab_s, recv_sem=lab_r,
                device_id=(2 * x + hk, 4 * hy + hz), device_id_type=MESH,
            ).start()

        return carry

    lax.fori_loop(2, 50, send_rows, 0)
    lax.fori_loop(0, 16, send_ids, 0)
    lax.fori_loop(1, 64, send_meta, 0)
    lax.fori_loop(50, DEVS, send_rows, 0)
    sibling = (2 * x + 1 - k, col)
    own_rows = pl.ds(pl.multiple_of(16 * chip, 16), 16)
    own_slot = pl.ds(pl.multiple_of(16 * k, 16), 16)
    sibling_copy = pltpu.make_async_remote_copy(
        src_ref=sbuf.at[1 - k, own_rows], dst_ref=rb.at[own_slot],
        send_sem=row_s, recv_sem=row_r.at[0], device_id=sibling, device_id_type=MESH,
    )
    sibling_copy.start()
    own_copy = pltpu.make_async_copy(sbuf.at[k, own_rows], rb.at[own_slot], own_sem)
    own_copy.start()
    meta_r[64 * k] = meta_s[chip]
    pltpu.make_async_copy(meta_s.at[pl.ds(0, 63)], meta_s.at[pl.ds(0, 63)], meta_rr).wait()
    meta_pair = pltpu.make_async_remote_copy(
        src_ref=meta_r.at[pl.ds(pl.multiple_of(64 * k, 64), 64)], dst_ref=meta_r.at[pl.ds(pl.multiple_of(64 * k, 64), 64)],
        send_sem=meta_ps, recv_sem=meta_pr, device_id=sibling, device_id_type=MESH,
    )
    meta_pair.start()

    pltpu.make_async_copy(labs, labs, lab_r).wait()
    large = labs[7, :, 0:1]
    first = jnp.where(share < 6, share, 2 * share - 6)
    second = jnp.where(share < 6, share + 10, 2 * share - 5)
    is_large = labs[first] == large
    eye = ones(iota((ROWS, ROWS), 0) == iota((ROWS, ROWS), 1))

    def column(r):
        return dot_t(eye, jnp.broadcast_to(r, (8, ROWS)).astype(BF16))[:, 0:1]

    rest_ids = jnp.where(is_large, labs[second], labs[first]).astype(F32)
    rest_col = column(rest_ids)
    large_col = column(jnp.where(is_large, 1.0, 0.0))

    def beside_ids(c):
        is_here = labs[c] == large
        return is_here, column(jnp.where(is_here, labs[c + 10], labs[c]).astype(F32))

    is_next, next_col = beside_ids(jnp.minimum(share + 1, 5))
    is_prev, prev_col = beside_ids(jnp.clip(share - 1, 0, 5))
    next_col, prev_col = next_col[:EDGE], prev_col[ROWS - EDGE :]

    index_col = iota((ROWS, 1), 0).astype(F32) + 1.0
    key_large = index_col + 512.0 * (1.0 - large_col)
    key_rest = index_col + 512.0 * large_col

    meta_pair.wait_recv()
    for a in range(16):
        r = meta_r[4 * a] + meta_r[64 + 4 * a]
        for i in range(1, 4):
            r = r + (meta_r[4 * a + i] + meta_r[64 + 4 * a + i])
        q[0:ROWS, pl.ds(128 * a, 128)] = ones(key_large == r)
        q[ROWS : 2 * ROWS, pl.ds(128 * a, 128)] = ones(key_rest == r)

    own_copy.wait()
    early = 32 * EARLY
    pltpu.make_async_copy(rb.at[pl.ds(0, early - 16)], rb.at[pl.ds(0, early - 16)], row_r.at[0]).wait()
    part[...] = dot(q[:, 0:early], rb[0:early, :])
    pltpu.make_async_copy(rb.at[pl.ds(early, 2048 - early)], rb.at[pl.ds(early, 2048 - early)], row_r.at[1]).wait()

    def along(bit):
        ny = y + 1 - 2 * (y % 2) if bit == 2 else y
        nz = z + 1 - 2 * (z % 2) if bit == 0 else 3 - z if bit == 1 else z
        return (2 * x + k, 4 * ny + nz)

    def between(src, dst, n, send, recv, device):
        return pltpu.make_async_remote_copy(
            src_ref=xs.at[k, pl.ds(src, n)], dst_ref=xs.at[k, pl.ds(dst, n)],
            send_sem=send, recv_sem=recv, device_id=device, device_id_type=MESH,
        )

    def pair_copy(i, start, n):
        return between(start, start, n, pair_s.at[i], pair_r.at[i], sibling)

    def block_copy(bit, c):
        at, n = CHUNKS[c]
        src = pl.multiple_of(pick(p, SEND[bit]) + at, 16)
        return between(src, SLOT[1 + bit] + at, n, ici_s.at[bit, c], ici_r.at[bit, c], along(bit))

    n_chunks = len(CHUNKS)
    copies = [[block_copy(bit, c) for c in range(n_chunks)] for bit in range(3)]
    block_pairs = [[pair_copy(3 + bit * n_chunks + c, SLOT[1 + bit] + CHUNKS[c][0], CHUNKS[c][1]) for c in range(n_chunks)] for bit in range(3)]
    own_pair, second_pair = pair_copy(0, 0, ROWS), pair_copy(1, SECOND, ROWS)
    patch_pair = pair_copy(2, PATCH, QUARTER)
    head_pair, tail_pair = pair_copy(3 + 3 * n_chunks, HEAD, EDGE), pair_copy(4 + 3 * n_chunks, TAIL, EDGE)
    has_patch = (p != 1) & (p != 4) & (p != 5)
    has_head = (p != 2) & (p != 6) & (p != 4)
    has_tail = (p != 2) & (p != 6) & (p != 0)

    def patch_copy(i):
        frm, to, bit, src = PATCHES[i]
        return between(src, PATCH, QUARTER, patch_s.at[i % 2], patch_r, along(bit))

    def head_copy(bit):
        return between(SECOND, HEAD, EDGE, edge_s.at[0], edge_r.at[0], along(bit))

    def tail_copy(bit):
        return between(SECOND + ROWS - EDGE, TAIL, EDGE, edge_s.at[1], edge_r.at[1], along(bit))

    def own_sends(c):
        @pl.when(p != 6)
        def _():
            copies[0][c].start()

        @pl.when(p != 2)
        def _():
            copies[1][c].start()

        @pl.when(p == 6)
        def _():
            copies[2][c].start()

        if CHUNKS[c][0] + CHUNKS[c][1] == ROWS:
            @pl.when(p == 4)
            def _():
                patch_copy(0).start()

    def unpacked(at, n):
        rows = slice(at, at + n)
        return (part[rows, :] + dot(q[rows, early:], rb[early:, :])).astype(BF16)

    for at in range(0, ROWS, QUARTER):
        xs[k, pl.ds(at, QUARTER), :] = unpacked(at, QUARTER)
        for c in range(n_chunks):
            if at <= CHUNKS[c][0] < at + QUARTER:
                own_sends(c)

    own_pair.start()
    xs[k, pl.ds(SECOND, ROWS), :] = unpacked(ROWS, ROWS)
    for c in range(n_chunks):
        @pl.when(p == 6)
        def _():
            copies[0][c].start()

        @pl.when(p == 2)
        def _():
            copies[1][c].start()
            copies[2][c].start()

    second_pair.start()
    for v, w, bit in ((0, 1, 0), (1, 3, 1), (3, 7, 2), (7, 5, 1), (5, 4, 0)):
        @pl.when(p == v)
        def _():
            tail_copy(bit).start()

        @pl.when(p == w)
        def _():
            head_copy(bit).start()

    mine = pl.multiple_of(QUARTER * k, QUARTER)
    starts = SLOT + (SECOND,)

    meetings = [tuple(pick(p, tuple(m[i][side] for m in MEET)) for side in range(2)) for i in range(3)]

    def columns_of(s):
        return pl.multiple_of(starts[s] + mine, QUARTER)

    def tile(j, nj, i, ni):
        return dot_t(xs[0, pl.ds(j, nj), :], xs[0, pl.ds(i, ni), :]) + dot_t(
            xs[1, pl.ds(j, nj), :], xs[1, pl.ds(i, ni), :]
        )

    def top(t):
        return jnp.max(t, axis=0, keepdims=True)

    def meet(s, other):
        i, j = pl.multiple_of(s * ROWS + mine, QUARTER), pl.multiple_of(other * ROWS, ROWS)
        acc[s] = jnp.maximum(acc[s], top(tile(j, ROWS, i, QUARTER)))

    def across(t):
        m = t[:, :128]
        for i in range(128, t.shape[1], 128):
            m = jnp.maximum(m, t[:, i : i + 128])
        return jnp.max(jnp.transpose(m), axis=0, keepdims=True)

    def late(at):
        rows, lanes = SLOT[3] + at, pl.ds(at, QUARTER)

        def against(s):
            t = tile(rows, QUARTER, columns_of(s), QUARTER)
            acc[s] = jnp.maximum(acc[s], top(t))
            return t

        t = jnp.maximum(jnp.maximum(against(0), against(1)), against(2))
        last[:, lanes] = across(t)

        @pl.when(large_only)
        def _():
            last[:, lanes] = jnp.maximum(last[:, lanes], across(against(4)))

    ob[...] = jnp.full(ob.shape, -1.0, F32)
    acc[...] = jnp.full(acc.shape, -1.0, F32)
    rest_row = jnp.where(k == 0, rest_ids[:, :QUARTER], rest_ids[:, QUARTER:])

    own = iota((ROWS, QUARTER), 0) == iota((ROWS, QUARTER), 1) + mine
    own_pair.wait_recv()
    acc[0] = top(jnp.where(own, -1.0, tile(0, ROWS, columns_of(0), QUARTER)))
    for c in range(n_chunks):
        copies[0][c].wait_recv()
        copies[1][c].wait_recv()

        @pl.when(jnp.logical_not(large_only))
        def _():
            copies[2][c].start()

        block_pairs[0][c].start()
        block_pairs[1][c].start()
        if CHUNKS[c][0] + CHUNKS[c][1] == QUARTER:
            @pl.when(p == 6)
            def _():
                patch_copy(1).start()

            @pl.when(p == 2)
            def _():
                patch_copy(3).start()

    @pl.when(p == 6)
    def _():
        patch_copy(2).start()

    @pl.when(p == 2)
    def _():
        patch_copy(4).start()

    second_pair.wait_recv()
    t = tile(SECOND, ROWS, columns_of(4), QUARTER)
    acc[4] = top(jnp.where((rest_col == rest_row) & jnp.logical_not(own), t, -1.0))
    for c in range(n_chunks):
        block_pairs[0][c].wait_recv()
        block_pairs[1][c].wait_recv()
    for a, b in meetings:
        meet(a, b)
        meet(b, a)
    for c in range(n_chunks - 1):
        copies[2][c].wait_recv()
        block_pairs[2][c].start()
    for c in range(n_chunks):
        if sum(CHUNKS[c]) <= QUARTER:
            block_pairs[2][c].wait_recv()
    @pl.when(has_head)
    def _():
        head_copy(0).wait_recv()
        head_pair.start()

    @pl.when(has_tail)
    def _():
        tail_copy(0).wait_recv()
        tail_pair.start()

    late(0)
    copies[2][n_chunks - 1].wait_recv()
    block_pairs[2][n_chunks - 1].start()

    @pl.when(has_patch)
    def _():
        patch_copy(0).wait_recv()
        patch_pair.start()

    def raise_to(b, at, n, v):
        ob[b, :, pl.ds(at, n)] = jnp.maximum(ob[b, :, pl.ds(at, n)], v)

    def beside(pair, start, step, at, is_here, there_col):
        pair.wait_recv()
        t = jnp.where(there_col == rest_row, tile(start, EDGE, columns_of(4), QUARTER), -1.0)
        acc[4] = jnp.maximum(acc[4], top(t))
        none = jnp.full((QUARTER - EDGE, QUARTER), -1.0, F32)
        m = across(jnp.concatenate([none, t] if at else [t, none], axis=0))
        is_here = is_here[:, at : at + QUARTER]
        raise_to(share + step, at, QUARTER, jnp.where(is_here, -1.0, m))
        raise_to(share + step + 10, at, QUARTER, jnp.where(is_here, m, -1.0))

    @pl.when(has_head)
    def _():
        beside(head_pair, HEAD, 1, 0, is_next, next_col)

    @pl.when(has_tail)
    def _():
        beside(tail_pair, TAIL, -1, QUARTER, is_prev, prev_col)

    for c in range(n_chunks):
        if sum(CHUNKS[c]) > QUARTER:
            block_pairs[2][c].wait_recv()
    late(QUARTER)

    @pl.when(has_patch)
    def _():
        patch_pair.wait_recv()
        def meets(start):
            t = tile(PATCH, QUARTER, pl.multiple_of(start + mine, QUARTER), QUARTER)
            s = jnp.where(start == SECOND, 4, start // ROWS)
            acc[s] = jnp.maximum(acc[s], top(t))
            return across(t)

        at = pl.multiple_of(QUARTER * pick(p, PATCH_HALF), QUARTER)
        v = pick(p, PATCH_BLOCK)
        here = labs[v, :, pl.ds(at, QUARTER)] == large

        def give(m):
            raise_to(v, at, QUARTER, jnp.where(here, m, -1.0))
            raise_to(v + 10, at, QUARTER, jnp.where(here, -1.0, m))

        give(meets(pick(p, PATCH_MEETS)))

        @pl.when(p == 2)
        def _():
            give(meets(jnp.int32(SLOT[2])))

    def give_block(v, at, n, m):
        here = labs[v, :, pl.ds(at, n)] == large
        raise_to(v, at, n, jnp.where(here, m, -1.0))
        raise_to(jnp.minimum(v + 10, 15), at, n, jnp.where(here | (v >= 6), -1.0, m))

    for s in range(3):
        give_block(pick(p, tuple(h[s] for h in HELD)), mine, QUARTER, acc[s])
    last[:, pl.ds(mine, QUARTER)] = jnp.maximum(last[:, pl.ds(mine, QUARTER)], acc[3])
    give_block(pick(p, tuple(h[3] for h in HELD)), 0, ROWS, last[...])
    here = labs[first, :, pl.ds(mine, QUARTER)] == large
    raise_to(second, mine, QUARTER, jnp.where(here, acc[4], -1.0))
    raise_to(first, mine, QUARTER, jnp.where(here, -1.0, acc[4]))

    def send_best(b, carry):
        to_self = at_home & (b == col)

        @pl.when(to_self)
        def _():
            pltpu.make_async_copy(ob.at[b], fin.at[p * 2 + k], fin_r).start()

        @pl.when(jnp.logical_not(to_self))
        def _():
            pltpu.make_async_remote_copy(
                src_ref=ob.at[b], dst_ref=fin.at[p * 2 + k],
                send_sem=fin_s, recv_sem=fin_r, device_id=(group, b), device_id_type=MESH,
            ).start()

        return carry

    lax.fori_loop(0, 16, send_best, 0)

    pltpu.make_async_copy(sbuf.at[0, pl.ds(0, 1008)], sbuf.at[0, pl.ds(0, 1008)], row_s).wait()
    pltpu.make_async_copy(sbuf.at[0], sbuf.at[0], row_s).wait()
    pltpu.make_async_copy(meta_s.at[pl.ds(0, 63)], meta_s.at[pl.ds(0, 63)], meta_ss).wait()
    meta_pair.wait_send()
    for per_bit in copies + block_pairs:
        for cp in per_bit:
            cp.wait_send()
    own_pair.wait_send()
    second_pair.wait_send()

    @pl.when(has_head)
    def _():
        head_pair.wait_send()
        tail_copy(0).wait_send()

    @pl.when(has_tail)
    def _():
        tail_pair.wait_send()
        head_copy(0).wait_send()

    @pl.when(has_patch)
    def _():
        patch_pair.wait_send()

    for v, which in ((4, (0,)), (6, (1, 2)), (2, (3, 4))):
        @pl.when(p == v)
        def _():
            for i in which:
                patch_copy(i).wait_send()

    @pl.when(at_home)
    def _():
        pltpu.make_async_copy(labs.at[pl.ds(0, 15)], labs.at[pl.ds(0, 15)], lab_s).wait()
        pltpu.make_async_copy(fin.at[pl.ds(0, 15)], fin.at[pl.ds(0, 15)], fin_s).wait()

    @pl.when(jnp.logical_not(at_home))
    def _():
        pltpu.make_async_copy(labs, labs, lab_s).wait()
        pltpu.make_async_copy(fin, fin, fin_s).wait()

    pltpu.make_async_copy(fin, fin, fin_r).wait()


def shards(embeddings, dest_pos, cluster_ids):
    dma, n_pairs = pltpu.SemaphoreType.DMA, 5 + 3 * len(CHUNKS)
    bests = pl.pallas_call(
        kernel,
        out_shape=jax.ShapeDtypeStruct((16, 1, ROWS), F32),
        in_specs=[
            pl.BlockSpec(memory_space=pltpu.HBM),
            pl.BlockSpec(memory_space=pltpu.HBM),
            pl.BlockSpec(memory_space=pltpu.HBM),
        ],
        out_specs=pl.BlockSpec(memory_space=pltpu.HBM),
        scratch_shapes=[
            pltpu.VMEM((ROWS, WIDTH), F32),
            pltpu.VMEM((1, ROWS), I32),
            pltpu.VMEM((1, ROWS), I32),
            pltpu.VMEM((ROWS, WIDTH), BF16),
            pltpu.VMEM((2, 1024, HALF), BF16),
            pltpu.VMEM((16 * DEVS, HALF), BF16),
            pltpu.VMEM((2 * ROWS, HALF), F32),
            pltpu.VMEM((64, 1, 128), F32),
            pltpu.VMEM((DEVS, 1, 128), F32),
            pltpu.VMEM((16, 1, ROWS), I32),
            pltpu.VMEM((2 * ROWS, 16 * DEVS), BF16),
            pltpu.VMEM((2, X_ROWS, HALF), BF16),
            pltpu.VMEM((5, 1, QUARTER), F32),
            pltpu.VMEM((1, ROWS), F32),
            pltpu.VMEM((16, 1, ROWS), F32),
            dma, dma, dma, dma, dma, dma((2,)), dma, dma, dma, dma, dma, dma,
            dma((3, len(CHUNKS))), dma((3, len(CHUNKS))), dma((n_pairs,)), dma((n_pairs,)),
            dma((2,)), dma, dma((2,)), dma((2,)), dma, dma,
        ],
        compiler_params=pltpu.CompilerParams(
            collective_id=0, has_side_effects=True, vmem_limit_bytes=62 * 2**20
        ),
        name="best_match",
    )(embeddings, dest_pos.reshape(1, ROWS), cluster_ids)
    return jnp.max(bests, axis=0)


def solution(mesh):
    return jax.shard_map(
        shards,
        mesh=mesh,
        in_specs=(P(("row", "col"), None), P(("row", "col")), P("row", "col")),
        out_specs=P("row", "col"),
        check_vma=False,
    )
```

```python
import functools

import jax
import jax.numpy as jnp
from jax import lax
from jax.experimental import pallas as pl
from jax.experimental.pallas import tpu as pltpu
from jax.sharding import PartitionSpec as P

MESH = pl.DeviceIdType.MESH
F32, BF16, I32 = jnp.float32, jnp.bfloat16, jnp.int32
DEVS = 128
ROWS = 512
WIDTH = 1024
HALF = WIDTH // 2
QUARTER = ROWS // 2
CHIP = (0, 1, 7, 2, 5, 4, 6, 3)
VERTEX = (0, 1, 3, 7, 5, 4, 6, 2)
HELD = ((0, 1, 9, 4), (1, 0, 2, 3), (8, 2, 0, 6), (2, 8, 1, 7), (5, 4, 6, 1), (4, 5, 3, 2), (6, 3, 5, 9), (3, 7, 4, 8))
SLOT = (0, 512, 1024, 1536)
SECOND, PATCH, HEAD, TAIL = 2048, 2560, 2816, 2960
EDGE = 144
X_ROWS = TAIL + EDGE
SEND = (
    (0, 0, 0, 0, 0, 0, SECOND, 0),
    (0, 0, SECOND, 0, 0, 0, 0, 0),
    (512, 1024, SECOND, 512, 512, 1024, 0, 512),
)
PATCH_BLOCK = (5, 0, 5, 0, 0, 0, 0, 5)
PATCH_HALF = (1, 0, 0, 0, 0, 0, 1, 1)
PATCH_MEETS = (0, 0, 0, 1536, 0, 0, SECOND, 1536)
PATCHES = ((4, 0, 2, 256), (6, 2, 2, 1024), (6, 7, 0, 1280), (2, 3, 0, 1024), (2, 6, 2, 1280))
MEET = (
    ((0, 1), (0, 2), (1, 2)), ((0, 1), (0, 2), (1, 2)), ((0, 2), (0, 4), (1, 4)), ((0, 1), (0, 2), (1, 2)),
    ((0, 1), (0, 2), (1, 2)), ((0, 1), (0, 2), (1, 2)), ((0, 1), (0, 4), (2, 4)), ((0, 1), (0, 2), (1, 2)),
)
CHUNKS = ((0, 128), (128, 128), (256, 128), (384, 128))
STRIDE, INVERSE, EARLY = 45, 37, 48


def pick(p, table):
    out = jnp.int32(table[0])
    for i in range(1, len(table)):
        if table[i] != table[0]:
            out = jnp.where(p == i, jnp.int32(table[i]), out)
    return out


def iota(shape, dim):
    return lax.broadcasted_iota(I32, shape, dim)


def ones(cond):
    return jnp.where(cond, jnp.float32(1.0), jnp.float32(0.0)).astype(BF16)


def dot_t(a, b):
    return lax.dot_general(a, b, (((1,), (1,)), ((), ())), preferred_element_type=F32)


def dot(a, b):
    return lax.dot_general(a, b, (((1,), (0,)), ((), ())), preferred_element_type=F32)


def kernel(
    emb_hbm, dest_hbm, ids_hbm, fin,
    emb, dest_ref, ids_ref, unit, sbuf, rb, part, meta_s, meta_r, labs, q, xs, acc, last, ob,
    emb_sem, dest_sem, ids_sem, own_sem, row_s, row_r, meta_ss, meta_rr, meta_ps, meta_pr, lab_s, lab_r,
    ici_s, ici_r, pair_s, pair_r, patch_s, patch_r, edge_s, edge_r, fin_s, fin_r,
):
    row, col = lax.axis_index("row"), lax.axis_index("col")
    x, k, y, z = row // 2, row % 2, col // 4, col % 4
    chip = x * 16 + y * 4 + z
    group = 2 * x + y // 2
    turned = (z + 2) % 4
    p = (y + 1) % 2 * 4 + (turned // 2) * 2 + (turned // 2 + turned) % 2
    share = pick(p, CHIP)
    large_only = (p == 2) | (p == 6)

    dest_copy = pltpu.make_async_copy(dest_hbm, dest_ref, dest_sem)
    dest_copy.start()
    emb_copy = pltpu.make_async_copy(emb_hbm, emb, emb_sem)
    emb_copy.start()
    ids_copy = pltpu.make_async_copy(ids_hbm, ids_ref, ids_sem)
    ids_copy.start()

    def relative(n):
        off = (n * STRIDE) % 64
        return (x + off // 16) % 4, (y + off // 4 % 4) % 4, (z + off % 4) % 4

    barrier = pltpu.get_barrier_semaphore()

    def greet(tx, ty, tz, tk):
        pl.semaphore_signal(barrier, inc=1, device_id=(2 * tx + tk, 4 * ty + tz), device_id_type=MESH)

    lead = (x % 2 == 0) & (y % 2 == 1) & (z % 2 == 0)

    @pl.when(jnp.logical_not(lead & (k == 0)))
    def _():
        greet(x - x % 2, y - y % 2 + 1, z - z % 2, 0)

    dest_copy.wait()
    dest = dest_ref[...]
    block = lax.shift_right_logical(dest, 9)
    place = dest & 511
    g, b = lax.shift_right_logical(block, 4), block & 15
    to = jnp.where(b < 6, b, jnp.where(b < 8, 6, jnp.where(b < 10, 7, b - 10)))
    half = jnp.where(b < 6, 0, jnp.where(b < 10, b & 1, 1))
    vert = pick(to, VERTEX)
    tx = lax.shift_right_logical(g, 1)
    ty = 2 * (g & 1) + (lax.shift_right_logical(vert, 2) + 1 & 1)
    tz = (vert & 2) + (lax.shift_right_logical(vert, 1) + vert & 1) + 2 & 3
    tchip = tx * 16 + ty * 4 + tz
    turn = (((tx - x) & 3) * 16 + ((ty - y) & 3) * 4 + ((tz - z) & 3)) * INVERSE & 3
    tb = tchip * 2 + half
    hot = iota((DEVS, ROWS), 0) == tb
    before = ones(iota((ROWS, ROWS), 0) < iota((ROWS, ROWS), 1))
    rank = dot(ones(hot), before)
    slot = jnp.sum(jnp.where(hot, rank, 0.0), axis=0, keepdims=True).astype(I32)
    line = tb * 8 + slot

    value = place + 1 + 512 * half
    to_chip = iota((64, ROWS), 0) == tchip
    lanes = ones(iota((128, ROWS), 0) == (half * 8 + slot + 16 * (2 * turn + k)))
    high = jnp.where(to_chip, lax.shift_right_logical(value, 4).astype(F32), 0.0).astype(BF16)
    low = jnp.where(to_chip, (value & 15).astype(F32), 0.0).astype(BF16)
    meta = 16.0 * dot_t(high, lanes) + dot_t(low, lanes)
    for n in range(64):
        meta_s[n] = meta[n : n + 1, :]

    emb_copy.wait()
    rows = emb[...]
    scale = lax.rsqrt(jnp.sum(rows * rows, axis=1, keepdims=True) + 1e-06)
    unit[...] = (rows * scale).astype(BF16)
    for a in range(8):
        take = ones(iota((128, ROWS), 0) + 128 * a == line)
        packed = dot(take, unit[...]).astype(BF16)
        sbuf[0, pl.ds(128 * a, 128), :] = packed[:, :HALF]
        sbuf[1, pl.ds(128 * a, 128), :] = packed[:, HALF:]

    @pl.when(lead & (k == 0))
    def _():
        pl.semaphore_wait(barrier, 15)
        for j in range(7, -1, -1):
            greet((x + 2 * (j // 4)) % 4, (y + 2 * (j // 2 % 2)) % 4, (z + 2 * (j % 2)) % 4, 1)
        pl.semaphore_wait(barrier, 1)

    @pl.when(lead & (k == 1))
    def _():
        pl.semaphore_wait(barrier, 8)
        for j in range(15, 0, -1):
            greet(x + j // 8, y - j // 4 % 2, z + j // 2 % 2, (1 + j) % 2)

    @pl.when(jnp.logical_not(lead))
    def _():
        pl.semaphore_wait(barrier, 1)

    def send_rows(e, carry):
        n, tk = e // 2, e % 2
        tx, ty, tz = relative(n)
        pltpu.make_async_remote_copy(
            src_ref=sbuf.at[tk, pl.ds(pl.multiple_of(16 * (tx * 16 + ty * 4 + tz), 16), 16)],
            dst_ref=rb.at[pl.ds(pl.multiple_of(16 * (2 * n + k), 16), 16)],
            send_sem=row_s, recv_sem=row_r.at[n // EARLY],
            device_id=(2 * tx + tk, 4 * ty + tz), device_id_type=MESH,
        ).start()
        return carry

    def send_meta(n, carry):
        tx, ty, tz = relative(n)
        pltpu.make_async_remote_copy(
            src_ref=meta_s.at[tx * 16 + ty * 4 + tz], dst_ref=meta_r.at[64 * k + n],
            send_sem=meta_ss, recv_sem=meta_rr,
            device_id=(2 * tx + k, 4 * ty + tz), device_id_type=MESH,
        ).start()
        return carry

    ids_copy.wait()
    at_home = y // 2 == k

    def send_ids(j, carry):
        hy, hz, hk = 2 * k + j // 8, (j // 2) % 4, j % 2
        to_self = (hy == y) & (hz == z) & (hk == k)

        @pl.when(to_self)
        def _():
            pltpu.make_async_copy(ids_ref, labs.at[col], lab_r).start()

        @pl.when(jnp.logical_not(to_self))
        def _():
            pltpu.make_async_remote_copy(
                src_ref=ids_ref, dst_ref=labs.at[col],
                send_sem=lab_s, recv_sem=lab_r,
                device_id=(2 * x + hk, 4 * hy + hz), device_id_type=MESH,
            ).start()

        return carry

    lax.fori_loop(2, 50, send_rows, 0)
    lax.fori_loop(0, 16, send_ids, 0)
    lax.fori_loop(1, 64, send_meta, 0)
    lax.fori_loop(50, DEVS, send_rows, 0)
    sibling = (2 * x + 1 - k, col)
    own_rows = pl.ds(pl.multiple_of(16 * chip, 16), 16)
    own_slot = pl.ds(pl.multiple_of(16 * k, 16), 16)
    sibling_copy = pltpu.make_async_remote_copy(
        src_ref=sbuf.at[1 - k, own_rows], dst_ref=rb.at[own_slot],
        send_sem=row_s, recv_sem=row_r.at[0], device_id=sibling, device_id_type=MESH,
    )
    sibling_copy.start()
    own_copy = pltpu.make_async_copy(sbuf.at[k, own_rows], rb.at[own_slot], own_sem)
    own_copy.start()
    meta_r[64 * k] = meta_s[chip]
    pltpu.make_async_copy(meta_s.at[pl.ds(0, 63)], meta_s.at[pl.ds(0, 63)], meta_rr).wait()
    meta_pair = pltpu.make_async_remote_copy(
        src_ref=meta_r.at[pl.ds(pl.multiple_of(64 * k, 64), 64)], dst_ref=meta_r.at[pl.ds(pl.multiple_of(64 * k, 64), 64)],
        send_sem=meta_ps, recv_sem=meta_pr, device_id=sibling, device_id_type=MESH,
    )
    meta_pair.start()

    pltpu.make_async_copy(labs, labs, lab_r).wait()
    large = labs[7, :, 0:1]
    first = jnp.where(share < 6, share, 2 * share - 6)
    second = jnp.where(share < 6, share + 10, 2 * share - 5)
    is_large = labs[first] == large
    eye = ones(iota((ROWS, ROWS), 0) == iota((ROWS, ROWS), 1))

    def column(r):
        return dot_t(eye, jnp.broadcast_to(r, (8, ROWS)).astype(BF16))[:, 0:1]

    rest_ids = jnp.where(is_large, labs[second], labs[first]).astype(F32)
    rest_col = column(rest_ids)
    large_col = column(jnp.where(is_large, 1.0, 0.0))

    def beside_ids(c):
        is_here = labs[c] == large
        return is_here, column(jnp.where(is_here, labs[c + 10], labs[c]).astype(F32))

    is_next, next_col = beside_ids(jnp.minimum(share + 1, 5))
    is_prev, prev_col = beside_ids(jnp.clip(share - 1, 0, 5))
    next_col, prev_col = next_col[:EDGE], prev_col[ROWS - EDGE :]

    index_col = iota((ROWS, 1), 0).astype(F32) + 1.0
    key_large = index_col + 512.0 * (1.0 - large_col)
    key_rest = index_col + 512.0 * large_col

    meta_pair.wait_recv()
    for a in range(16):
        r = meta_r[4 * a] + meta_r[64 + 4 * a]
        for i in range(1, 4):
            r = r + (meta_r[4 * a + i] + meta_r[64 + 4 * a + i])
        q[0:ROWS, pl.ds(128 * a, 128)] = ones(key_large == r)
        q[ROWS : 2 * ROWS, pl.ds(128 * a, 128)] = ones(key_rest == r)

    own_copy.wait()
    early = 32 * EARLY
    pltpu.make_async_copy(rb.at[pl.ds(0, early - 16)], rb.at[pl.ds(0, early - 16)], row_r.at[0]).wait()
    part[...] = dot(q[:, 0:early], rb[0:early, :])
    pltpu.make_async_copy(rb.at[pl.ds(early, 2048 - early)], rb.at[pl.ds(early, 2048 - early)], row_r.at[1]).wait()

    def along(bit):
        ny = y + 1 - 2 * (y % 2) if bit == 2 else y
        nz = turned + 1 - 2 * (turned % 2) if bit == 0 else 3 - turned if bit == 1 else turned
        nz = (nz + 2) % 4
        return (2 * x + k, 4 * ny + nz)

    def between(src, dst, n, send, recv, device):
        return pltpu.make_async_remote_copy(
            src_ref=xs.at[k, pl.ds(src, n)], dst_ref=xs.at[k, pl.ds(dst, n)],
            send_sem=send, recv_sem=recv, device_id=device, device_id_type=MESH,
        )

    def pair_copy(i, start, n):
        return between(start, start, n, pair_s.at[i], pair_r.at[i], sibling)

    def block_copy(bit, c):
        at, n = CHUNKS[c]
        src = pl.multiple_of(pick(p, SEND[bit]) + at, 16)
        return between(src, SLOT[1 + bit] + at, n, ici_s.at[bit, c], ici_r.at[bit, c], along(bit))

    n_chunks = len(CHUNKS)
    copies = [[block_copy(bit, c) for c in range(n_chunks)] for bit in range(3)]
    block_pairs = [[pair_copy(3 + bit * n_chunks + c, SLOT[1 + bit] + CHUNKS[c][0], CHUNKS[c][1]) for c in range(n_chunks)] for bit in range(3)]
    own_pair, second_pair = pair_copy(0, 0, ROWS), pair_copy(1, SECOND, ROWS)
    patch_pair = pair_copy(2, PATCH, QUARTER)
    head_pair, tail_pair = pair_copy(3 + 3 * n_chunks, HEAD, EDGE), pair_copy(4 + 3 * n_chunks, TAIL, EDGE)
    has_patch = (p != 1) & (p != 4) & (p != 5)
    has_head = (p != 2) & (p != 6) & (p != 4)
    has_tail = (p != 2) & (p != 6) & (p != 0)

    def patch_copy(i):
        frm, to, bit, src = PATCHES[i]
        return between(src, PATCH, QUARTER, patch_s.at[i % 2], patch_r, along(bit))

    def head_copy(bit):
        return between(SECOND, HEAD, EDGE, edge_s.at[0], edge_r.at[0], along(bit))

    def tail_copy(bit):
        return between(SECOND + ROWS - EDGE, TAIL, EDGE, edge_s.at[1], edge_r.at[1], along(bit))

    def own_sends(c):
        @pl.when(p != 6)
        def _():
            copies[0][c].start()

        @pl.when(p != 2)
        def _():
            copies[1][c].start()

        @pl.when(p == 6)
        def _():
            copies[2][c].start()

        if CHUNKS[c][0] + CHUNKS[c][1] == ROWS:
            @pl.when(p == 4)
            def _():
                patch_copy(0).start()

    def unpacked(at, n):
        rows = slice(at, at + n)
        return (part[rows, :] + dot(q[rows, early:], rb[early:, :])).astype(BF16)

    for at in range(0, ROWS, QUARTER):
        xs[k, pl.ds(at, QUARTER), :] = unpacked(at, QUARTER)
        for c in range(n_chunks):
            if at <= CHUNKS[c][0] < at + QUARTER:
                own_sends(c)

    own_pair.start()
    xs[k, pl.ds(SECOND, ROWS), :] = unpacked(ROWS, ROWS)
    for c in range(n_chunks):
        @pl.when(p == 6)
        def _():
            copies[0][c].start()

        @pl.when(p == 2)
        def _():
            copies[1][c].start()
            copies[2][c].start()

    second_pair.start()
    for v, w, bit in ((0, 1, 0), (1, 3, 1), (3, 7, 2), (7, 5, 1), (5, 4, 0)):
        @pl.when(p == v)
        def _():
            tail_copy(bit).start()

        @pl.when(p == w)
        def _():
            head_copy(bit).start()

    mine = pl.multiple_of(QUARTER * k, QUARTER)
    starts = SLOT + (SECOND,)

    meetings = [tuple(pick(p, tuple(m[i][side] for m in MEET)) for side in range(2)) for i in range(3)]

    def columns_of(s):
        return pl.multiple_of(starts[s] + mine, QUARTER)

    def tile(j, nj, i, ni):
        return dot_t(xs[0, pl.ds(j, nj), :], xs[0, pl.ds(i, ni), :]) + dot_t(
            xs[1, pl.ds(j, nj), :], xs[1, pl.ds(i, ni), :]
        )

    def top(t):
        return jnp.max(t, axis=0, keepdims=True)

    def meet(s, other):
        i, j = pl.multiple_of(s * ROWS + mine, QUARTER), pl.multiple_of(other * ROWS, ROWS)
        acc[s] = jnp.maximum(acc[s], top(tile(j, ROWS, i, QUARTER)))

    def across(t):
        m = t[:, :128]
        for i in range(128, t.shape[1], 128):
            m = jnp.maximum(m, t[:, i : i + 128])
        return jnp.max(jnp.transpose(m), axis=0, keepdims=True)

    def late(at):
        rows, lanes = SLOT[3] + at, pl.ds(at, QUARTER)

        def against(s):
            t = tile(rows, QUARTER, columns_of(s), QUARTER)
            acc[s] = jnp.maximum(acc[s], top(t))
            return t

        t = jnp.maximum(jnp.maximum(against(0), against(1)), against(2))
        last[:, lanes] = across(t)

        @pl.when(large_only)
        def _():
            last[:, lanes] = jnp.maximum(last[:, lanes], across(against(4)))

    ob[...] = jnp.full(ob.shape, -1.0, F32)
    acc[...] = jnp.full(acc.shape, -1.0, F32)
    rest_row = jnp.where(k == 0, rest_ids[:, :QUARTER], rest_ids[:, QUARTER:])

    own = iota((ROWS, QUARTER), 0) == iota((ROWS, QUARTER), 1) + mine
    own_pair.wait_recv()
    acc[0] = top(jnp.where(own, -1.0, tile(0, ROWS, columns_of(0), QUARTER)))
    for c in range(n_chunks):
        copies[0][c].wait_recv()
        copies[1][c].wait_recv()

        @pl.when(jnp.logical_not(large_only))
        def _():
            copies[2][c].start()

        block_pairs[0][c].start()
        block_pairs[1][c].start()
        if CHUNKS[c][0] + CHUNKS[c][1] == QUARTER:
            @pl.when(p == 6)
            def _():
                patch_copy(1).start()

            @pl.when(p == 2)
            def _():
                patch_copy(3).start()

    @pl.when(p == 6)
    def _():
        patch_copy(2).start()

    @pl.when(p == 2)
    def _():
        patch_copy(4).start()

    second_pair.wait_recv()
    t = tile(SECOND, ROWS, columns_of(4), QUARTER)
    acc[4] = top(jnp.where((rest_col == rest_row) & jnp.logical_not(own), t, -1.0))
    for c in range(n_chunks):
        block_pairs[0][c].wait_recv()
        block_pairs[1][c].wait_recv()
    for a, b in meetings:
        meet(a, b)
        meet(b, a)
    for c in range(n_chunks - 1):
        copies[2][c].wait_recv()
        block_pairs[2][c].start()
    for c in range(n_chunks):
        if sum(CHUNKS[c]) <= QUARTER:
            block_pairs[2][c].wait_recv()
    @pl.when(has_head)
    def _():
        head_copy(0).wait_recv()
        head_pair.start()

    @pl.when(has_tail)
    def _():
        tail_copy(0).wait_recv()
        tail_pair.start()

    late(0)
    copies[2][n_chunks - 1].wait_recv()
    block_pairs[2][n_chunks - 1].start()

    @pl.when(has_patch)
    def _():
        patch_copy(0).wait_recv()
        patch_pair.start()

    def raise_to(b, at, n, v):
        ob[b, :, pl.ds(at, n)] = jnp.maximum(ob[b, :, pl.ds(at, n)], v)

    def beside(pair, start, step, at, is_here, there_col):
        pair.wait_recv()
        t = jnp.where(there_col == rest_row, tile(start, EDGE, columns_of(4), QUARTER), -1.0)
        acc[4] = jnp.maximum(acc[4], top(t))
        none = jnp.full((QUARTER - EDGE, QUARTER), -1.0, F32)
        m = across(jnp.concatenate([none, t] if at else [t, none], axis=0))
        is_here = is_here[:, at : at + QUARTER]
        raise_to(share + step, at, QUARTER, jnp.where(is_here, -1.0, m))
        raise_to(share + step + 10, at, QUARTER, jnp.where(is_here, m, -1.0))

    @pl.when(has_head)
    def _():
        beside(head_pair, HEAD, 1, 0, is_next, next_col)

    @pl.when(has_tail)
    def _():
        beside(tail_pair, TAIL, -1, QUARTER, is_prev, prev_col)

    for c in range(n_chunks):
        if sum(CHUNKS[c]) > QUARTER:
            block_pairs[2][c].wait_recv()
    late(QUARTER)

    @pl.when(has_patch)
    def _():
        patch_pair.wait_recv()
        def meets(start):
            t = tile(PATCH, QUARTER, pl.multiple_of(start + mine, QUARTER), QUARTER)
            s = jnp.where(start == SECOND, 4, start // ROWS)
            acc[s] = jnp.maximum(acc[s], top(t))
            return across(t)

        at = pl.multiple_of(QUARTER * pick(p, PATCH_HALF), QUARTER)
        v = pick(p, PATCH_BLOCK)
        here = labs[v, :, pl.ds(at, QUARTER)] == large

        def give(m):
            raise_to(v, at, QUARTER, jnp.where(here, m, -1.0))
            raise_to(v + 10, at, QUARTER, jnp.where(here, -1.0, m))

        give(meets(pick(p, PATCH_MEETS)))

        @pl.when(p == 2)
        def _():
            give(meets(jnp.int32(SLOT[2])))

    def give_block(v, at, n, m):
        here = labs[v, :, pl.ds(at, n)] == large
        raise_to(v, at, n, jnp.where(here, m, -1.0))
        raise_to(jnp.minimum(v + 10, 15), at, n, jnp.where(here | (v >= 6), -1.0, m))

    for s in range(3):
        give_block(pick(p, tuple(h[s] for h in HELD)), mine, QUARTER, acc[s])
    last[:, pl.ds(mine, QUARTER)] = jnp.maximum(last[:, pl.ds(mine, QUARTER)], acc[3])
    give_block(pick(p, tuple(h[3] for h in HELD)), 0, ROWS, last[...])
    here = labs[first, :, pl.ds(mine, QUARTER)] == large
    raise_to(second, mine, QUARTER, jnp.where(here, acc[4], -1.0))
    raise_to(first, mine, QUARTER, jnp.where(here, -1.0, acc[4]))

    def send_best(b, carry):
        to_self = at_home & (b == col)

        @pl.when(to_self)
        def _():
            pltpu.make_async_copy(ob.at[b], fin.at[p * 2 + k], fin_r).start()

        @pl.when(jnp.logical_not(to_self))
        def _():
            pltpu.make_async_remote_copy(
                src_ref=ob.at[b], dst_ref=fin.at[p * 2 + k],
                send_sem=fin_s, recv_sem=fin_r, device_id=(group, b), device_id_type=MESH,
            ).start()

        return carry

    lax.fori_loop(0, 16, send_best, 0)

    pltpu.make_async_copy(sbuf.at[0, pl.ds(0, 1008)], sbuf.at[0, pl.ds(0, 1008)], row_s).wait()
    pltpu.make_async_copy(sbuf.at[0], sbuf.at[0], row_s).wait()
    pltpu.make_async_copy(meta_s.at[pl.ds(0, 63)], meta_s.at[pl.ds(0, 63)], meta_ss).wait()
    meta_pair.wait_send()
    for per_bit in copies + block_pairs:
        for cp in per_bit:
            cp.wait_send()
    own_pair.wait_send()
    second_pair.wait_send()

    @pl.when(has_head)
    def _():
        head_pair.wait_send()
        tail_copy(0).wait_send()

    @pl.when(has_tail)
    def _():
        tail_pair.wait_send()
        head_copy(0).wait_send()

    @pl.when(has_patch)
    def _():
        patch_pair.wait_send()

    for v, which in ((4, (0,)), (6, (1, 2)), (2, (3, 4))):
        @pl.when(p == v)
        def _():
            for i in which:
                patch_copy(i).wait_send()

    @pl.when(at_home)
    def _():
        pltpu.make_async_copy(labs.at[pl.ds(0, 15)], labs.at[pl.ds(0, 15)], lab_s).wait()
        pltpu.make_async_copy(fin.at[pl.ds(0, 15)], fin.at[pl.ds(0, 15)], fin_s).wait()

    @pl.when(jnp.logical_not(at_home))
    def _():
        pltpu.make_async_copy(labs, labs, lab_s).wait()
        pltpu.make_async_copy(fin, fin, fin_s).wait()

    pltpu.make_async_copy(fin, fin, fin_r).wait()


def shards(embeddings, dest_pos, cluster_ids):
    dma, n_pairs = pltpu.SemaphoreType.DMA, 5 + 3 * len(CHUNKS)
    bests = pl.pallas_call(
        kernel,
        out_shape=jax.ShapeDtypeStruct((16, 1, ROWS), F32),
        in_specs=[
            pl.BlockSpec(memory_space=pltpu.HBM),
            pl.BlockSpec(memory_space=pltpu.HBM),
            pl.BlockSpec(memory_space=pltpu.HBM),
        ],
        out_specs=pl.BlockSpec(memory_space=pltpu.HBM),
        scratch_shapes=[
            pltpu.VMEM((ROWS, WIDTH), F32),
            pltpu.VMEM((1, ROWS), I32),
            pltpu.VMEM((1, ROWS), I32),
            pltpu.VMEM((ROWS, WIDTH), BF16),
            pltpu.VMEM((2, 1024, HALF), BF16),
            pltpu.VMEM((16 * DEVS, HALF), BF16),
            pltpu.VMEM((2 * ROWS, HALF), F32),
            pltpu.VMEM((64, 1, 128), F32),
            pltpu.VMEM((DEVS, 1, 128), F32),
            pltpu.VMEM((16, 1, ROWS), I32),
            pltpu.VMEM((2 * ROWS, 16 * DEVS), BF16),
            pltpu.VMEM((2, X_ROWS, HALF), BF16),
            pltpu.VMEM((5, 1, QUARTER), F32),
            pltpu.VMEM((1, ROWS), F32),
            pltpu.VMEM((16, 1, ROWS), F32),
            dma, dma, dma, dma, dma, dma((2,)), dma, dma, dma, dma, dma, dma,
            dma((3, len(CHUNKS))), dma((3, len(CHUNKS))), dma((n_pairs,)), dma((n_pairs,)),
            dma((2,)), dma, dma((2,)), dma((2,)), dma, dma,
        ],
        compiler_params=pltpu.CompilerParams(
            collective_id=0, has_side_effects=True, vmem_limit_bytes=62 * 2**20
        ),
        name="best_match",
    )(embeddings, dest_pos.reshape(1, ROWS), cluster_ids)
    return jnp.max(bests, axis=0)


def solution(mesh):
    return jax.shard_map(
        shards,
        mesh=mesh,
        in_specs=(P(("row", "col"), None), P(("row", "col")), P("row", "col")),
        out_specs=P("row", "col"),
        check_vma=False,
    )
```

```python
import functools

import jax
import jax.numpy as jnp
from jax import lax
from jax.experimental import pallas as pl
from jax.experimental.pallas import tpu as pltpu
from jax.sharding import PartitionSpec as P

MESH = pl.DeviceIdType.MESH
F32, BF16, I32 = jnp.float32, jnp.bfloat16, jnp.int32
DEVS = 128
ROWS = 512
WIDTH = 1024
HALF = WIDTH // 2
QUARTER = ROWS // 2
CHIP = (0, 1, 7, 2, 5, 4, 6, 3)
VERTEX = (0, 1, 3, 7, 5, 4, 6, 2)
HELD = ((0, 1, 9, 4), (1, 0, 2, 3), (8, 2, 0, 6), (2, 8, 1, 7), (5, 4, 6, 1), (4, 5, 3, 2), (6, 3, 5, 9), (3, 7, 4, 8))
SLOT = (0, 512, 1024, 1536)
SECOND, PATCH, HEAD, TAIL = 2048, 2560, 2816, 2960
EDGE = 144
X_ROWS = TAIL + EDGE
SEND = (
    (0, 0, 0, 0, 0, 0, SECOND, 0),
    (0, 0, SECOND, 0, 0, 0, 0, 0),
    (512, 1024, SECOND, 512, 512, 1024, 0, 512),
)
PATCH_BLOCK = (5, 0, 5, 0, 0, 0, 0, 5)
PATCH_HALF = (1, 0, 0, 0, 0, 0, 1, 1)
PATCH_MEETS = (0, 0, 0, 1536, 0, 0, SECOND, 1536)
PATCHES = ((4, 0, 2, 256), (6, 2, 2, 1024), (6, 7, 0, 1280), (2, 3, 0, 1024), (2, 6, 2, 1280))
MEET = (
    ((0, 1), (0, 2), (1, 2)), ((0, 1), (0, 2), (1, 2)), ((0, 2), (0, 4), (1, 4)), ((0, 1), (0, 2), (1, 2)),
    ((0, 1), (0, 2), (1, 2)), ((0, 1), (0, 2), (1, 2)), ((0, 1), (0, 4), (2, 4)), ((0, 1), (0, 2), (1, 2)),
)
CHUNKS = ((0, 128), (128, 128), (256, 128), (384, 128))
STRIDE, INVERSE, EARLY = 45, 37, 48


def pick(p, table):
    out = jnp.int32(table[0])
    for i in range(1, len(table)):
        if table[i] != table[0]:
            out = jnp.where(p == i, jnp.int32(table[i]), out)
    return out


def iota(shape, dim):
    return lax.broadcasted_iota(I32, shape, dim)


def ones(cond):
    return jnp.where(cond, jnp.float32(1.0), jnp.float32(0.0)).astype(BF16)


def dot_t(a, b):
    return lax.dot_general(a, b, (((1,), (1,)), ((), ())), preferred_element_type=F32)


def dot(a, b):
    return lax.dot_general(a, b, (((1,), (0,)), ((), ())), preferred_element_type=F32)


def kernel(
    emb_hbm, dest_hbm, ids_hbm, fin,
    emb, dest_ref, ids_ref, unit, sbuf, rb, part, meta_s, meta_r, labs, q, xs, acc, last, ob,
    emb_sem, dest_sem, ids_sem, own_sem, row_s, row_r, meta_ss, meta_rr, meta_ps, meta_pr, lab_s, lab_r,
    ici_s, ici_r, pair_s, pair_r, patch_s, patch_r, edge_s, edge_r, fin_s, fin_r,
):
    row, col = lax.axis_index("row"), lax.axis_index("col")
    x, k, y, z = row // 2, row % 2, col // 4, col % 4
    chip = x * 16 + y * 4 + z
    group = 2 * x + y // 2
    turned = (z + 2) % 4
    p = (y + 1) % 2 * 4 + (turned // 2) * 2 + (turned // 2 + turned) % 2
    share = pick(p, CHIP)
    large_only = (p == 2) | (p == 6)

    dest_copy = pltpu.make_async_copy(dest_hbm, dest_ref, dest_sem)
    dest_copy.start()
    emb_copy = pltpu.make_async_copy(emb_hbm, emb, emb_sem)
    emb_copy.start()
    ids_copy = pltpu.make_async_copy(ids_hbm, ids_ref, ids_sem)
    ids_copy.start()

    def relative(n):
        off = (n * STRIDE) % 64
        return (x + off // 16) % 4, (y + off // 4 % 4) % 4, (z + off % 4) % 4

    barrier = pltpu.get_barrier_semaphore()

    def greet(tx, ty, tz, tk):
        pl.semaphore_signal(barrier, inc=1, device_id=(2 * tx + tk, 4 * ty + tz), device_id_type=MESH)

    lead = (x % 2 == 0) & (y % 2 == 1) & (z % 2 == 0)

    @pl.when(jnp.logical_not(lead & (k == 0)))
    def _():
        greet(x - x % 2, y - y % 2 + 1, z - z % 2, 0)

    dest_copy.wait()
    dest = dest_ref[...]
    block = lax.shift_right_logical(dest, 9)
    place = dest & 511
    g, b = lax.shift_right_logical(block, 4), block & 15
    to = jnp.where(b < 6, b, jnp.where(b < 8, 6, jnp.where(b < 10, 7, b - 10)))
    half = jnp.where(b < 6, 0, jnp.where(b < 10, b & 1, 1))
    vert = pick(to, VERTEX)
    tx = lax.shift_right_logical(g, 1)
    ty = 2 * (g & 1) + (lax.shift_right_logical(vert, 2) + 1 & 1)
    tz = (vert & 2) + (lax.shift_right_logical(vert, 1) + vert & 1) + 2 & 3
    tchip = tx * 16 + ty * 4 + tz
    turn = (((tx - x) & 3) * 16 + ((ty - y) & 3) * 4 + ((tz - z) & 3)) * INVERSE & 3
    tb = tchip * 2 + half
    hot = iota((DEVS, ROWS), 0) == tb
    before = ones(iota((ROWS, ROWS), 0) < iota((ROWS, ROWS), 1))
    rank = dot(ones(hot), before)
    slot = jnp.sum(jnp.where(hot, rank, 0.0), axis=0, keepdims=True).astype(I32)
    line = tb * 8 + slot

    value = place + 1 + 512 * half
    to_chip = iota((64, ROWS), 0) == tchip
    lanes = ones(iota((128, ROWS), 0) == (half * 8 + slot + 16 * (2 * turn + k)))
    high = jnp.where(to_chip, lax.shift_right_logical(value, 4).astype(F32), 0.0).astype(BF16)
    low = jnp.where(to_chip, (value & 15).astype(F32), 0.0).astype(BF16)
    meta = 16.0 * dot_t(high, lanes) + dot_t(low, lanes)
    for n in range(64):
        meta_s[n] = meta[n : n + 1, :]

    emb_copy.wait()
    rows = emb[...]
    scale = lax.rsqrt(jnp.sum(rows * rows, axis=1, keepdims=True) + 1e-06)
    unit[...] = (rows * scale).astype(BF16)
    for a in range(8):
        take = ones(iota((128, ROWS), 0) + 128 * a == line)
        packed = dot(take, unit[...]).astype(BF16)
        sbuf[0, pl.ds(128 * a, 128), :] = packed[:, :HALF]
        sbuf[1, pl.ds(128 * a, 128), :] = packed[:, HALF:]

    @pl.when(lead & (k == 0))
    def _():
        pl.semaphore_wait(barrier, 15)
        for j in range(7, -1, -1):
            greet((x + 2 * (j // 4)) % 4, (y + 2 * (j // 2 % 2)) % 4, (z + 2 * (j % 2)) % 4, 1)
        pl.semaphore_wait(barrier, 1)

    @pl.when(lead & (k == 1))
    def _():
        pl.semaphore_wait(barrier, 8)
        for j in range(15, 0, -1):
            greet(x + j // 8, y - j // 4 % 2, z + j // 2 % 2, (1 + j) % 2)

    @pl.when(jnp.logical_not(lead))
    def _():
        pl.semaphore_wait(barrier, 1)

    def send_rows(e, carry):
        n, tk = e // 2, e % 2
        tx, ty, tz = relative(n)
        pltpu.make_async_remote_copy(
            src_ref=sbuf.at[tk, pl.ds(pl.multiple_of(16 * (tx * 16 + ty * 4 + tz), 16), 16)],
            dst_ref=rb.at[pl.ds(pl.multiple_of(16 * (2 * n + k), 16), 16)],
            send_sem=row_s, recv_sem=row_r.at[n // EARLY],
            device_id=(2 * tx + tk, 4 * ty + tz), device_id_type=MESH,
        ).start()
        return carry

    def send_meta(n, carry):
        tx, ty, tz = relative(n)
        pltpu.make_async_remote_copy(
            src_ref=meta_s.at[tx * 16 + ty * 4 + tz], dst_ref=meta_r.at[64 * k + n],
            send_sem=meta_ss, recv_sem=meta_rr,
            device_id=(2 * tx + k, 4 * ty + tz), device_id_type=MESH,
        ).start()
        return carry

    ids_copy.wait()
    at_home = y // 2 == k

    def send_ids(j, carry):
        hy, hz, hk = 2 * k + j // 8, (j // 2) % 4, j % 2
        to_self = (hy == y) & (hz == z) & (hk == k)

        @pl.when(to_self)
        def _():
            pltpu.make_async_copy(ids_ref, labs.at[col], lab_r).start()

        @pl.when(jnp.logical_not(to_self))
        def _():
            pltpu.make_async_remote_copy(
                src_ref=ids_ref, dst_ref=labs.at[col],
                send_sem=lab_s, recv_sem=lab_r,
                device_id=(2 * x + hk, 4 * hy + hz), device_id_type=MESH,
            ).start()

        return carry

    lax.fori_loop(2, 50, send_rows, 0)
    lax.fori_loop(0, 16, send_ids, 0)
    lax.fori_loop(1, 64, send_meta, 0)
    lax.fori_loop(50, DEVS, send_rows, 0)
    sibling = (2 * x + 1 - k, col)
    own_rows = pl.ds(pl.multiple_of(16 * chip, 16), 16)
    own_slot = pl.ds(pl.multiple_of(16 * k, 16), 16)
    sibling_copy = pltpu.make_async_remote_copy(
        src_ref=sbuf.at[1 - k, own_rows], dst_ref=rb.at[own_slot],
        send_sem=row_s, recv_sem=row_r.at[0], device_id=sibling, device_id_type=MESH,
    )
    sibling_copy.start()
    own_copy = pltpu.make_async_copy(sbuf.at[k, own_rows], rb.at[own_slot], own_sem)
    own_copy.start()
    meta_r[64 * k] = meta_s[chip]
    pltpu.make_async_copy(meta_s.at[pl.ds(0, 63)], meta_s.at[pl.ds(0, 63)], meta_rr).wait()
    meta_pair = pltpu.make_async_remote_copy(
        src_ref=meta_r.at[pl.ds(pl.multiple_of(64 * k, 64), 64)], dst_ref=meta_r.at[pl.ds(pl.multiple_of(64 * k, 64), 64)],
        send_sem=meta_ps, recv_sem=meta_pr, device_id=sibling, device_id_type=MESH,
    )
    meta_pair.start()

    pltpu.make_async_copy(labs, labs, lab_r).wait()
    large = labs[7, :, 0:1]
    first = jnp.where(share < 6, share, 2 * share - 6)
    second = jnp.where(share < 6, share + 10, 2 * share - 5)
    is_large = labs[first] == large
    eye = ones(iota((ROWS, ROWS), 0) == iota((ROWS, ROWS), 1))

    def column(r):
        return dot_t(eye, jnp.broadcast_to(r, (8, ROWS)).astype(BF16))[:, 0:1]

    rest_ids = jnp.where(is_large, labs[second], labs[first]).astype(F32)
    rest_col = column(rest_ids)
    large_col = column(jnp.where(is_large, 1.0, 0.0))

    def beside_ids(c):
        is_here = labs[c] == large
        return is_here, column(jnp.where(is_here, labs[c + 10], labs[c]).astype(F32))

    is_next, next_col = beside_ids(jnp.minimum(share + 1, 5))
    is_prev, prev_col = beside_ids(jnp.clip(share - 1, 0, 5))
    next_col, prev_col = next_col[:EDGE], prev_col[ROWS - EDGE :]

    index_col = iota((ROWS, 1), 0).astype(F32) + 1.0
    key_large = index_col + 512.0 * (1.0 - large_col)
    key_rest = index_col + 512.0 * large_col

    meta_pair.wait_recv()
    for a in range(16):
        r = meta_r[4 * a] + meta_r[64 + 4 * a]
        for i in range(1, 4):
            r = r + (meta_r[4 * a + i] + meta_r[64 + 4 * a + i])
        q[0:ROWS, pl.ds(128 * a, 128)] = ones(key_large == r)
        q[ROWS : 2 * ROWS, pl.ds(128 * a, 128)] = ones(key_rest == r)

    own_copy.wait()
    early = 32 * EARLY
    pltpu.make_async_copy(rb.at[pl.ds(0, early - 16)], rb.at[pl.ds(0, early - 16)], row_r.at[0]).wait()
    part[...] = dot(q[:, 0:early], rb[0:early, :])
    pltpu.make_async_copy(rb.at[pl.ds(early, 2048 - early)], rb.at[pl.ds(early, 2048 - early)], row_r.at[1]).wait()

    def along(bit):
        ny = y + 1 - 2 * (y % 2) if bit == 2 else y
        nz = turned + 1 - 2 * (turned % 2) if bit == 0 else 3 - turned if bit == 1 else turned
        nz = (nz + 2) % 4
        return (2 * x + k, 4 * ny + nz)

    def between(src, dst, n, send, recv, device):
        return pltpu.make_async_remote_copy(
            src_ref=xs.at[k, pl.ds(src, n)], dst_ref=xs.at[k, pl.ds(dst, n)],
            send_sem=send, recv_sem=recv, device_id=device, device_id_type=MESH,
        )

    def pair_copy(i, start, n):
        return between(start, start, n, pair_s.at[i], pair_r.at[i], sibling)

    def block_copy(bit, c):
        at, n = CHUNKS[c]
        src = pl.multiple_of(pick(p, SEND[bit]) + at, 16)
        return between(src, SLOT[1 + bit] + at, n, ici_s.at[bit, c], ici_r.at[bit, c], along(bit))

    n_chunks = len(CHUNKS)
    copies = [[block_copy(bit, c) for c in range(n_chunks)] for bit in range(3)]
    block_pairs = [[pair_copy(3 + bit * n_chunks + c, SLOT[1 + bit] + CHUNKS[c][0], CHUNKS[c][1]) for c in range(n_chunks)] for bit in range(3)]
    own_pair, second_pair = pair_copy(0, 0, ROWS), pair_copy(1, SECOND, ROWS)
    patch_pair = pair_copy(2, PATCH, QUARTER)
    head_pair, tail_pair = pair_copy(3 + 3 * n_chunks, HEAD, EDGE), pair_copy(4 + 3 * n_chunks, TAIL, EDGE)
    has_patch = (p != 1) & (p != 4) & (p != 5)
    has_head = (p != 2) & (p != 6) & (p != 4)
    has_tail = (p != 2) & (p != 6) & (p != 0)

    def patch_copy(i):
        frm, to, bit, src = PATCHES[i]
        return between(src, PATCH, QUARTER, patch_s.at[i % 2], patch_r, along(bit))

    def head_copy(bit):
        return between(SECOND, HEAD, EDGE, edge_s.at[0], edge_r.at[0], along(bit))

    def tail_copy(bit):
        return between(SECOND + ROWS - EDGE, TAIL, EDGE, edge_s.at[1], edge_r.at[1], along(bit))

    def own_sends(c):
        @pl.when(p != 6)
        def _():
            copies[0][c].start()

        @pl.when(p != 2)
        def _():
            copies[1][c].start()

        @pl.when(p == 6)
        def _():
            copies[2][c].start()

        if CHUNKS[c][0] + CHUNKS[c][1] == ROWS:
            @pl.when(p == 4)
            def _():
                patch_copy(0).start()

    def unpacked(at, n):
        rows = slice(at, at + n)
        return (part[rows, :] + dot(q[rows, early:], rb[early:, :])).astype(BF16)

    xs[k, pl.ds(0, ROWS), :] = unpacked(0, ROWS)
    for c in range(n_chunks):
        own_sends(c)

    own_pair.start()
    xs[k, pl.ds(SECOND, ROWS), :] = unpacked(ROWS, ROWS)
    for c in range(n_chunks):
        @pl.when(p == 6)
        def _():
            copies[0][c].start()

        @pl.when(p == 2)
        def _():
            copies[1][c].start()
            copies[2][c].start()

    second_pair.start()
    for v, w, bit in ((0, 1, 0), (1, 3, 1), (3, 7, 2), (7, 5, 1), (5, 4, 0)):
        @pl.when(p == v)
        def _():
            tail_copy(bit).start()

        @pl.when(p == w)
        def _():
            head_copy(bit).start()

    mine = pl.multiple_of(QUARTER * k, QUARTER)
    starts = SLOT + (SECOND,)

    meetings = [tuple(pick(p, tuple(m[i][side] for m in MEET)) for side in range(2)) for i in range(3)]

    def columns_of(s):
        return pl.multiple_of(starts[s] + mine, QUARTER)

    def tile(j, nj, i, ni):
        return dot_t(xs[0, pl.ds(j, nj), :], xs[0, pl.ds(i, ni), :]) + dot_t(
            xs[1, pl.ds(j, nj), :], xs[1, pl.ds(i, ni), :]
        )

    def top(t):
        return jnp.max(t, axis=0, keepdims=True)

    def meet(s, other):
        i, j = pl.multiple_of(s * ROWS + mine, QUARTER), pl.multiple_of(other * ROWS, ROWS)
        acc[s] = jnp.maximum(acc[s], top(tile(j, ROWS, i, QUARTER)))

    def across(t):
        m = t[:, :128]
        for i in range(128, t.shape[1], 128):
            m = jnp.maximum(m, t[:, i : i + 128])
        return jnp.max(jnp.transpose(m), axis=0, keepdims=True)

    def late(at):
        rows, lanes = SLOT[3] + at, pl.ds(at, QUARTER)

        def against(s):
            t = tile(rows, QUARTER, columns_of(s), QUARTER)
            acc[s] = jnp.maximum(acc[s], top(t))
            return t

        t = jnp.maximum(jnp.maximum(against(0), against(1)), against(2))
        last[:, lanes] = across(t)

        @pl.when(large_only)
        def _():
            last[:, lanes] = jnp.maximum(last[:, lanes], across(against(4)))

    ob[...] = jnp.full(ob.shape, -1.0, F32)
    acc[...] = jnp.full(acc.shape, -1.0, F32)
    rest_row = jnp.where(k == 0, rest_ids[:, :QUARTER], rest_ids[:, QUARTER:])

    own = iota((ROWS, QUARTER), 0) == iota((ROWS, QUARTER), 1) + mine
    own_pair.wait_recv()
    acc[0] = top(jnp.where(own, -1.0, tile(0, ROWS, columns_of(0), QUARTER)))
    for c in range(n_chunks):
        copies[0][c].wait_recv()
        copies[1][c].wait_recv()

        @pl.when(jnp.logical_not(large_only))
        def _():
            copies[2][c].start()

        block_pairs[0][c].start()
        block_pairs[1][c].start()
        if CHUNKS[c][0] + CHUNKS[c][1] == QUARTER:
            @pl.when(p == 6)
            def _():
                patch_copy(1).start()

            @pl.when(p == 2)
            def _():
                patch_copy(3).start()

    @pl.when(p == 6)
    def _():
        patch_copy(2).start()

    @pl.when(p == 2)
    def _():
        patch_copy(4).start()

    second_pair.wait_recv()
    t = tile(SECOND, ROWS, columns_of(4), QUARTER)
    acc[4] = top(jnp.where((rest_col == rest_row) & jnp.logical_not(own), t, -1.0))
    for c in range(n_chunks):
        block_pairs[0][c].wait_recv()
        block_pairs[1][c].wait_recv()
    for a, b in meetings:
        meet(a, b)
        meet(b, a)
    for c in range(n_chunks - 1):
        copies[2][c].wait_recv()
        block_pairs[2][c].start()
    for c in range(n_chunks):
        if sum(CHUNKS[c]) <= QUARTER:
            block_pairs[2][c].wait_recv()
    @pl.when(has_head)
    def _():
        head_copy(0).wait_recv()
        head_pair.start()

    @pl.when(has_tail)
    def _():
        tail_copy(0).wait_recv()
        tail_pair.start()

    late(0)
    copies[2][n_chunks - 1].wait_recv()
    block_pairs[2][n_chunks - 1].start()

    @pl.when(has_patch)
    def _():
        patch_copy(0).wait_recv()
        patch_pair.start()

    def raise_to(b, at, n, v):
        ob[b, :, pl.ds(at, n)] = jnp.maximum(ob[b, :, pl.ds(at, n)], v)

    def beside(pair, start, step, at, is_here, there_col):
        pair.wait_recv()
        t = jnp.where(there_col == rest_row, tile(start, EDGE, columns_of(4), QUARTER), -1.0)
        acc[4] = jnp.maximum(acc[4], top(t))
        none = jnp.full((QUARTER - EDGE, QUARTER), -1.0, F32)
        m = across(jnp.concatenate([none, t] if at else [t, none], axis=0))
        is_here = is_here[:, at : at + QUARTER]
        raise_to(share + step, at, QUARTER, jnp.where(is_here, -1.0, m))
        raise_to(share + step + 10, at, QUARTER, jnp.where(is_here, m, -1.0))

    @pl.when(has_head)
    def _():
        beside(head_pair, HEAD, 1, 0, is_next, next_col)

    @pl.when(has_tail)
    def _():
        beside(tail_pair, TAIL, -1, QUARTER, is_prev, prev_col)

    for c in range(n_chunks):
        if sum(CHUNKS[c]) > QUARTER:
            block_pairs[2][c].wait_recv()
    late(QUARTER)

    @pl.when(has_patch)
    def _():
        patch_pair.wait_recv()
        def meets(start):
            t = tile(PATCH, QUARTER, pl.multiple_of(start + mine, QUARTER), QUARTER)
            s = jnp.where(start == SECOND, 4, start // ROWS)
            acc[s] = jnp.maximum(acc[s], top(t))
            return t

        at = pl.multiple_of(QUARTER * pick(p, PATCH_HALF), QUARTER)
        v = pick(p, PATCH_BLOCK)
        here = labs[v, :, pl.ds(at, QUARTER)] == large

        def give(m):
            raise_to(v, at, QUARTER, jnp.where(here, m, -1.0))
            raise_to(v + 10, at, QUARTER, jnp.where(here, -1.0, m))

        t = meets(pick(p, PATCH_MEETS))

        @pl.when(p != 2)
        def _():
            give(across(t))

        @pl.when(p == 2)
        def _():
            give(across(jnp.maximum(t, meets(jnp.int32(SLOT[2])))))

    def give_block(v, at, n, m):
        here = labs[v, :, pl.ds(at, n)] == large
        raise_to(v, at, n, jnp.where(here, m, -1.0))
        raise_to(jnp.minimum(v + 10, 15), at, n, jnp.where(here | (v >= 6), -1.0, m))

    for s in range(3):
        give_block(pick(p, tuple(h[s] for h in HELD)), mine, QUARTER, acc[s])
    last[:, pl.ds(mine, QUARTER)] = jnp.maximum(last[:, pl.ds(mine, QUARTER)], acc[3])
    give_block(pick(p, tuple(h[3] for h in HELD)), 0, ROWS, last[...])
    here = labs[first, :, pl.ds(mine, QUARTER)] == large
    raise_to(second, mine, QUARTER, jnp.where(here, acc[4], -1.0))
    raise_to(first, mine, QUARTER, jnp.where(here, -1.0, acc[4]))

    def send_best(b, carry):
        to_self = at_home & (b == col)

        @pl.when(to_self)
        def _():
            pltpu.make_async_copy(ob.at[b], fin.at[p * 2 + k], fin_r).start()

        @pl.when(jnp.logical_not(to_self))
        def _():
            pltpu.make_async_remote_copy(
                src_ref=ob.at[b], dst_ref=fin.at[p * 2 + k],
                send_sem=fin_s, recv_sem=fin_r, device_id=(group, b), device_id_type=MESH,
            ).start()

        return carry

    lax.fori_loop(0, 16, send_best, 0)

    pltpu.make_async_copy(sbuf.at[0, pl.ds(0, 1008)], sbuf.at[0, pl.ds(0, 1008)], row_s).wait()
    pltpu.make_async_copy(sbuf.at[0], sbuf.at[0], row_s).wait()
    pltpu.make_async_copy(meta_s.at[pl.ds(0, 63)], meta_s.at[pl.ds(0, 63)], meta_ss).wait()
    meta_pair.wait_send()
    for per_bit in copies + block_pairs:
        for cp in per_bit:
            cp.wait_send()
    own_pair.wait_send()
    second_pair.wait_send()

    @pl.when(has_head)
    def _():
        head_pair.wait_send()
        tail_copy(0).wait_send()

    @pl.when(has_tail)
    def _():
        tail_pair.wait_send()
        head_copy(0).wait_send()

    @pl.when(has_patch)
    def _():
        patch_pair.wait_send()

    for v, which in ((4, (0,)), (6, (1, 2)), (2, (3, 4))):
        @pl.when(p == v)
        def _():
            for i in which:
                patch_copy(i).wait_send()

    @pl.when(at_home)
    def _():
        pltpu.make_async_copy(labs.at[pl.ds(0, 15)], labs.at[pl.ds(0, 15)], lab_s).wait()
        pltpu.make_async_copy(fin.at[pl.ds(0, 15)], fin.at[pl.ds(0, 15)], fin_s).wait()

    @pl.when(jnp.logical_not(at_home))
    def _():
        pltpu.make_async_copy(labs, labs, lab_s).wait()
        pltpu.make_async_copy(fin, fin, fin_s).wait()

    pltpu.make_async_copy(fin, fin, fin_r).wait()


def shards(embeddings, dest_pos, cluster_ids):
    dma, n_pairs = pltpu.SemaphoreType.DMA, 5 + 3 * len(CHUNKS)
    bests = pl.pallas_call(
        kernel,
        out_shape=jax.ShapeDtypeStruct((16, 1, ROWS), F32),
        in_specs=[
            pl.BlockSpec(memory_space=pltpu.HBM),
            pl.BlockSpec(memory_space=pltpu.HBM),
            pl.BlockSpec(memory_space=pltpu.HBM),
        ],
        out_specs=pl.BlockSpec(memory_space=pltpu.HBM),
        scratch_shapes=[
            pltpu.VMEM((ROWS, WIDTH), F32),
            pltpu.VMEM((1, ROWS), I32),
            pltpu.VMEM((1, ROWS), I32),
            pltpu.VMEM((ROWS, WIDTH), BF16),
            pltpu.VMEM((2, 1024, HALF), BF16),
            pltpu.VMEM((16 * DEVS, HALF), BF16),
            pltpu.VMEM((2 * ROWS, HALF), F32),
            pltpu.VMEM((64, 1, 128), F32),
            pltpu.VMEM((DEVS, 1, 128), F32),
            pltpu.VMEM((16, 1, ROWS), I32),
            pltpu.VMEM((2 * ROWS, 16 * DEVS), BF16),
            pltpu.VMEM((2, X_ROWS, HALF), BF16),
            pltpu.VMEM((5, 1, QUARTER), F32),
            pltpu.VMEM((1, ROWS), F32),
            pltpu.VMEM((16, 1, ROWS), F32),
            dma, dma, dma, dma, dma, dma((2,)), dma, dma, dma, dma, dma, dma,
            dma((3, len(CHUNKS))), dma((3, len(CHUNKS))), dma((n_pairs,)), dma((n_pairs,)),
            dma((2,)), dma, dma((2,)), dma((2,)), dma, dma,
        ],
        compiler_params=pltpu.CompilerParams(
            collective_id=0, has_side_effects=True, vmem_limit_bytes=62 * 2**20
        ),
        name="best_match",
    )(embeddings, dest_pos.reshape(1, ROWS), cluster_ids)
    return jnp.max(bests, axis=0)


def solution(mesh):
    return jax.shard_map(
        shards,
        mesh=mesh,
        in_specs=(P(("row", "col"), None), P(("row", "col")), P("row", "col")),
        out_specs=P("row", "col"),
        check_vma=False,
    )
```

```python
import functools

import jax
import jax.numpy as jnp
from jax import lax
from jax.experimental import pallas as pl
from jax.experimental.pallas import tpu as pltpu
from jax.sharding import PartitionSpec as P

MESH = pl.DeviceIdType.MESH
F32, BF16, I32 = jnp.float32, jnp.bfloat16, jnp.int32
DEVS = 128
ROWS = 512
WIDTH = 1024
HALF = WIDTH // 2
QUARTER = ROWS // 2
CHIP = (0, 1, 7, 2, 5, 4, 6, 3)
VERTEX = (0, 1, 3, 7, 5, 4, 6, 2)
HELD = ((0, 1, 9, 4), (1, 0, 2, 3), (8, 2, 0, 6), (2, 8, 1, 7), (5, 4, 6, 1), (4, 5, 3, 2), (6, 3, 5, 9), (3, 7, 4, 8))
SLOT = (0, 512, 1024, 1536)
SECOND, PATCH, HEAD, TAIL = 2048, 2560, 2816, 2960
EDGE = 144
X_ROWS = TAIL + EDGE
SEND = (
    (0, 0, 0, 0, 0, 0, SECOND, 0),
    (0, 0, SECOND, 0, 0, 0, 0, 0),
    (512, 1024, SECOND, 512, 512, 1024, 0, 512),
)
PATCH_BLOCK = (5, 0, 5, 0, 0, 0, 0, 5)
PATCH_HALF = (1, 0, 0, 0, 0, 0, 1, 1)
PATCH_MEETS = (0, 0, 0, 1536, 0, 0, SECOND, 1536)
PATCHES = ((4, 0, 2, 256), (6, 2, 2, 1024), (6, 7, 0, 1280), (2, 3, 0, 1024), (2, 6, 2, 1280))
MEET = (
    ((0, 1), (0, 2), (1, 2)), ((0, 1), (0, 2), (1, 2)), ((0, 2), (0, 4), (1, 4)), ((0, 1), (0, 2), (1, 2)),
    ((0, 1), (0, 2), (1, 2)), ((0, 1), (0, 2), (1, 2)), ((0, 1), (0, 4), (2, 4)), ((0, 1), (0, 2), (1, 2)),
)
CHUNKS = ((0, 128), (128, 128), (256, 128), (384, 128))
STRIDE, INVERSE, EARLY = 45, 37, 48


def pick(p, table):
    out = jnp.int32(table[0])
    for i in range(1, len(table)):
        if table[i] != table[0]:
            out = jnp.where(p == i, jnp.int32(table[i]), out)
    return out


def iota(shape, dim):
    return lax.broadcasted_iota(I32, shape, dim)


def ones(cond):
    return jnp.where(cond, jnp.float32(1.0), jnp.float32(0.0)).astype(BF16)


def dot_t(a, b):
    return lax.dot_general(a, b, (((1,), (1,)), ((), ())), preferred_element_type=F32)


def dot(a, b):
    return lax.dot_general(a, b, (((1,), (0,)), ((), ())), preferred_element_type=F32)


def kernel(
    emb_hbm, dest_hbm, ids_hbm, fin,
    emb, dest_ref, ids_ref, unit, sbuf, rb, part, meta_s, meta_r, labs, q, xs, acc, last, ob,
    emb_sem, dest_sem, ids_sem, own_sem, row_s, row_r, meta_ss, meta_rr, meta_ps, meta_pr, lab_s, lab_r,
    ici_s, ici_r, pair_s, pair_r, patch_s, patch_r, edge_s, edge_r, fin_s, fin_r,
):
    row, col = lax.axis_index("row"), lax.axis_index("col")
    x, k, y, z = row // 2, row % 2, col // 4, col % 4
    chip = x * 16 + y * 4 + z
    group = 2 * x + y // 2
    turned = (z + 2) % 4
    p = (y + 1) % 2 * 4 + (turned // 2) * 2 + (turned // 2 + turned) % 2
    share = pick(p, CHIP)
    large_only = (p == 2) | (p == 6)

    dest_copy = pltpu.make_async_copy(dest_hbm, dest_ref, dest_sem)
    dest_copy.start()
    emb_copy = pltpu.make_async_copy(emb_hbm, emb, emb_sem)
    emb_copy.start()
    ids_copy = pltpu.make_async_copy(ids_hbm, ids_ref, ids_sem)
    ids_copy.start()

    def relative(n):
        off = (n * STRIDE) % 64
        return (x + off // 16) % 4, (y + off // 4 % 4) % 4, (z + off % 4) % 4

    barrier = pltpu.get_barrier_semaphore()

    def greet(tx, ty, tz, tk):
        pl.semaphore_signal(barrier, inc=1, device_id=(2 * tx + tk, 4 * ty + tz), device_id_type=MESH)

    lead = (x % 2 == 0) & (y % 2 == 1) & (z % 2 == 0)

    @pl.when(jnp.logical_not(lead & (k == 0)))
    def _():
        greet(x - x % 2, y - y % 2 + 1, z - z % 2, 0)

    dest_copy.wait()
    dest = dest_ref[...]
    block = lax.shift_right_logical(dest, 9)
    place = dest & 511
    g, b = lax.shift_right_logical(block, 4), block & 15
    to = jnp.where(b < 6, b, jnp.where(b < 8, 6, jnp.where(b < 10, 7, b - 10)))
    half = jnp.where(b < 6, 0, jnp.where(b < 10, b & 1, 1))
    vert = pick(to, VERTEX)
    tx = lax.shift_right_logical(g, 1)
    ty = 2 * (g & 1) + (lax.shift_right_logical(vert, 2) + 1 & 1)
    tz = (vert & 2) + (lax.shift_right_logical(vert, 1) + vert & 1) + 2 & 3
    tchip = tx * 16 + ty * 4 + tz
    turn = (((tx - x) & 3) * 16 + ((ty - y) & 3) * 4 + ((tz - z) & 3)) * INVERSE & 3
    tb = tchip * 2 + half
    hot = iota((DEVS, ROWS), 0) == tb
    before = ones(iota((ROWS, ROWS), 0) < iota((ROWS, ROWS), 1))
    rank = dot(ones(hot), before)
    slot = jnp.sum(jnp.where(hot, rank, 0.0), axis=0, keepdims=True).astype(I32)
    line = tb * 8 + slot

    value = place + 1 + 512 * half
    to_chip = iota((64, ROWS), 0) == tchip
    lanes = ones(iota((128, ROWS), 0) == (half * 8 + slot + 16 * (2 * turn + k)))
    high = jnp.where(to_chip, lax.shift_right_logical(value, 4).astype(F32), 0.0).astype(BF16)
    low = jnp.where(to_chip, (value & 15).astype(F32), 0.0).astype(BF16)
    meta = 16.0 * dot_t(high, lanes) + dot_t(low, lanes)
    for n in range(64):
        meta_s[n] = meta[n : n + 1, :]

    emb_copy.wait()
    rows = emb[...]
    scale = lax.rsqrt(jnp.sum(rows * rows, axis=1, keepdims=True) + 1e-06)
    unit[...] = (rows * scale).astype(BF16)
    for a in range(8):
        take = ones(iota((128, ROWS), 0) + 128 * a == line)
        packed = dot(take, unit[...]).astype(BF16)
        sbuf[0, pl.ds(128 * a, 128), :] = packed[:, :HALF]
        sbuf[1, pl.ds(128 * a, 128), :] = packed[:, HALF:]

    @pl.when(lead & (k == 0))
    def _():
        pl.semaphore_wait(barrier, 15)
        for j in range(7, -1, -1):
            greet((x + 2 * (j // 4)) % 4, (y + 2 * (j // 2 % 2)) % 4, (z + 2 * (j % 2)) % 4, 1)
        pl.semaphore_wait(barrier, 1)

    @pl.when(lead & (k == 1))
    def _():
        pl.semaphore_wait(barrier, 8)
        for j in range(15, 0, -1):
            greet(x + j // 8, y - j // 4 % 2, z + j // 2 % 2, (1 + j) % 2)

    @pl.when(jnp.logical_not(lead))
    def _():
        pl.semaphore_wait(barrier, 1)

    def send_rows(e, carry):
        n, tk = e // 2, e % 2
        tx, ty, tz = relative(n)
        pltpu.make_async_remote_copy(
            src_ref=sbuf.at[tk, pl.ds(pl.multiple_of(16 * (tx * 16 + ty * 4 + tz), 16), 16)],
            dst_ref=rb.at[pl.ds(pl.multiple_of(16 * (2 * n + k), 16), 16)],
            send_sem=row_s, recv_sem=row_r.at[n // EARLY],
            device_id=(2 * tx + tk, 4 * ty + tz), device_id_type=MESH,
        ).start()
        return carry

    def send_meta(n, carry):
        tx, ty, tz = relative(n)
        pltpu.make_async_remote_copy(
            src_ref=meta_s.at[tx * 16 + ty * 4 + tz], dst_ref=meta_r.at[64 * k + n],
            send_sem=meta_ss, recv_sem=meta_rr,
            device_id=(2 * tx + k, 4 * ty + tz), device_id_type=MESH,
        ).start()
        return carry

    ids_copy.wait()
    at_home = y // 2 == k

    def send_ids(j, carry):
        hy, hz, hk = 2 * k + j // 8, (j // 2) % 4, j % 2
        to_self = (hy == y) & (hz == z) & (hk == k)

        @pl.when(to_self)
        def _():
            pltpu.make_async_copy(ids_ref, labs.at[col], lab_r).start()

        @pl.when(jnp.logical_not(to_self))
        def _():
            pltpu.make_async_remote_copy(
                src_ref=ids_ref, dst_ref=labs.at[col],
                send_sem=lab_s, recv_sem=lab_r,
                device_id=(2 * x + hk, 4 * hy + hz), device_id_type=MESH,
            ).start()

        return carry

    lax.fori_loop(2, 50, send_rows, 0)
    lax.fori_loop(0, 16, send_ids, 0)
    lax.fori_loop(1, 64, send_meta, 0)
    lax.fori_loop(50, DEVS, send_rows, 0)
    sibling = (2 * x + 1 - k, col)
    own_rows = pl.ds(pl.multiple_of(16 * chip, 16), 16)
    own_slot = pl.ds(pl.multiple_of(16 * k, 16), 16)
    sibling_copy = pltpu.make_async_remote_copy(
        src_ref=sbuf.at[1 - k, own_rows], dst_ref=rb.at[own_slot],
        send_sem=row_s, recv_sem=row_r.at[0], device_id=sibling, device_id_type=MESH,
    )
    sibling_copy.start()
    own_copy = pltpu.make_async_copy(sbuf.at[k, own_rows], rb.at[own_slot], own_sem)
    own_copy.start()
    meta_r[64 * k] = meta_s[chip]
    pltpu.make_async_copy(meta_s.at[pl.ds(0, 63)], meta_s.at[pl.ds(0, 63)], meta_rr).wait()
    meta_pair = pltpu.make_async_remote_copy(
        src_ref=meta_r.at[pl.ds(pl.multiple_of(64 * k, 64), 64)], dst_ref=meta_r.at[pl.ds(pl.multiple_of(64 * k, 64), 64)],
        send_sem=meta_ps, recv_sem=meta_pr, device_id=sibling, device_id_type=MESH,
    )
    meta_pair.start()

    pltpu.make_async_copy(labs, labs, lab_r).wait()
    large = labs[7, :, 0:1]
    first = jnp.where(share < 6, share, 2 * share - 6)
    second = jnp.where(share < 6, share + 10, 2 * share - 5)
    is_large = labs[first] == large
    eye = ones(iota((ROWS, ROWS), 0) == iota((ROWS, ROWS), 1))

    def column(r):
        return dot_t(eye, jnp.broadcast_to(r, (8, ROWS)).astype(BF16))[:, 0:1]

    rest_ids = jnp.where(is_large, labs[second], labs[first]).astype(F32)
    rest_col = column(rest_ids)
    large_col = column(jnp.where(is_large, 1.0, 0.0))

    def beside_ids(c):
        is_here = labs[c] == large
        return is_here, column(jnp.where(is_here, labs[c + 10], labs[c]).astype(F32))

    is_next, next_col = beside_ids(jnp.minimum(share + 1, 5))
    is_prev, prev_col = beside_ids(jnp.clip(share - 1, 0, 5))
    next_col, prev_col = next_col[:EDGE], prev_col[ROWS - EDGE :]

    index_col = iota((ROWS, 1), 0).astype(F32) + 1.0
    key_large = index_col + 512.0 * (1.0 - large_col)
    key_rest = index_col + 512.0 * large_col

    meta_pair.wait_recv()
    for a in range(16):
        r = meta_r[4 * a] + meta_r[64 + 4 * a]
        for i in range(1, 4):
            r = r + (meta_r[4 * a + i] + meta_r[64 + 4 * a + i])
        q[0:ROWS, pl.ds(128 * a, 128)] = ones(key_large == r)
        q[ROWS : 2 * ROWS, pl.ds(128 * a, 128)] = ones(key_rest == r)

    own_copy.wait()
    early = 32 * EARLY
    pltpu.make_async_copy(rb.at[pl.ds(0, early - 16)], rb.at[pl.ds(0, early - 16)], row_r.at[0]).wait()
    part[...] = dot(q[:, 0:early], rb[0:early, :])
    pltpu.make_async_copy(rb.at[pl.ds(early, 2048 - early)], rb.at[pl.ds(early, 2048 - early)], row_r.at[1]).wait()

    def along(bit):
        ny = y + 1 - 2 * (y % 2) if bit == 2 else y
        nz = turned + 1 - 2 * (turned % 2) if bit == 0 else 3 - turned if bit == 1 else turned
        nz = (nz + 2) % 4
        return (2 * x + k, 4 * ny + nz)

    def between(src, dst, n, send, recv, device):
        return pltpu.make_async_remote_copy(
            src_ref=xs.at[k, pl.ds(src, n)], dst_ref=xs.at[k, pl.ds(dst, n)],
            send_sem=send, recv_sem=recv, device_id=device, device_id_type=MESH,
        )

    def pair_copy(i, start, n):
        return between(start, start, n, pair_s.at[i], pair_r.at[i], sibling)

    def block_copy(bit, c):
        at, n = CHUNKS[c]
        src = pl.multiple_of(pick(p, SEND[bit]) + at, 16)
        return between(src, SLOT[1 + bit] + at, n, ici_s.at[bit, c], ici_r.at[bit, c], along(bit))

    n_chunks = len(CHUNKS)
    copies = [[block_copy(bit, c) for c in range(n_chunks)] for bit in range(3)]
    block_pairs = [[pair_copy(3 + bit * n_chunks + c, SLOT[1 + bit] + CHUNKS[c][0], CHUNKS[c][1]) for c in range(n_chunks)] for bit in range(3)]
    own_pair, second_pair = pair_copy(0, 0, ROWS), pair_copy(1, SECOND, ROWS)
    patch_pair = pair_copy(2, PATCH, QUARTER)
    head_pair, tail_pair = pair_copy(3 + 3 * n_chunks, HEAD, EDGE), pair_copy(4 + 3 * n_chunks, TAIL, EDGE)
    has_patch = (p != 1) & (p != 4) & (p != 5)
    has_head = (p != 2) & (p != 6) & (p != 4)
    has_tail = (p != 2) & (p != 6) & (p != 0)

    def patch_copy(i):
        frm, to, bit, src = PATCHES[i]
        return between(src, PATCH, QUARTER, patch_s.at[i % 2], patch_r, along(bit))

    def head_copy(bit):
        return between(SECOND, HEAD, EDGE, edge_s.at[0], edge_r.at[0], along(bit))

    def tail_copy(bit):
        return between(SECOND + ROWS - EDGE, TAIL, EDGE, edge_s.at[1], edge_r.at[1], along(bit))

    def own_sends(c):
        @pl.when(p != 6)
        def _():
            copies[0][c].start()

        @pl.when(p != 2)
        def _():
            copies[1][c].start()

        @pl.when(p == 6)
        def _():
            copies[2][c].start()

        if CHUNKS[c][0] + CHUNKS[c][1] == ROWS:
            @pl.when(p == 4)
            def _():
                patch_copy(0).start()

    def unpacked(at, n):
        rows = slice(at, at + n)
        return (part[rows, :] + dot(q[rows, early:], rb[early:, :])).astype(BF16)

    for at in range(0, ROWS, QUARTER):
        xs[k, pl.ds(at, QUARTER), :] = unpacked(at, QUARTER)
        for c in range(n_chunks):
            if at <= CHUNKS[c][0] < at + QUARTER:
                own_sends(c)

    own_pair.start()
    xs[k, pl.ds(SECOND, ROWS), :] = unpacked(ROWS, ROWS)
    for c in range(n_chunks):
        @pl.when(p == 6)
        def _():
            copies[0][c].start()

        @pl.when(p == 2)
        def _():
            copies[1][c].start()
            copies[2][c].start()

    second_pair.start()
    for v, w, bit in ((0, 1, 0), (1, 3, 1), (3, 7, 2), (7, 5, 1), (5, 4, 0)):
        @pl.when(p == v)
        def _():
            tail_copy(bit).start()

        @pl.when(p == w)
        def _():
            head_copy(bit).start()

    mine = pl.multiple_of(QUARTER * k, QUARTER)
    starts = SLOT + (SECOND,)

    meetings = [tuple(pick(p, tuple(m[i][side] for m in MEET)) for side in range(2)) for i in range(3)]

    def columns_of(s):
        return pl.multiple_of(starts[s] + mine, QUARTER)

    def tile(j, nj, i, ni):
        return dot_t(xs[0, pl.ds(j, nj), :], xs[0, pl.ds(i, ni), :]) + dot_t(
            xs[1, pl.ds(j, nj), :], xs[1, pl.ds(i, ni), :]
        )

    def top(t):
        return jnp.max(t, axis=0, keepdims=True)

    def meet(s, other):
        i, j = pl.multiple_of(s * ROWS + mine, QUARTER), pl.multiple_of(other * ROWS, ROWS)
        acc[s] = jnp.maximum(acc[s], top(tile(j, ROWS, i, QUARTER)))

    def across(t):
        m = t[:, :128]
        for i in range(128, t.shape[1], 128):
            m = jnp.maximum(m, t[:, i : i + 128])
        return jnp.max(jnp.transpose(m), axis=0, keepdims=True)

    def late(at):
        rows, lanes = SLOT[3] + at, pl.ds(at, QUARTER)

        def against(s):
            t = tile(rows, QUARTER, columns_of(s), QUARTER)
            acc[s] = jnp.maximum(acc[s], top(t))
            return t

        t = jnp.maximum(jnp.maximum(against(0), against(1)), against(2))
        last[:, lanes] = across(t)

        @pl.when(large_only)
        def _():
            last[:, lanes] = jnp.maximum(last[:, lanes], across(against(4)))

    ob[...] = jnp.full(ob.shape, -1.0, F32)
    acc[...] = jnp.full(acc.shape, -1.0, F32)
    rest_row = jnp.where(k == 0, rest_ids[:, :QUARTER], rest_ids[:, QUARTER:])

    own = iota((ROWS, QUARTER), 0) == iota((ROWS, QUARTER), 1) + mine
    own_pair.wait_recv()
    acc[0] = top(jnp.where(own, -1.0, tile(0, ROWS, columns_of(0), QUARTER)))
    for c in range(n_chunks):
        copies[0][c].wait_recv()

        @pl.when((p == 0) | (p == 3) | (p == 4) | (p == 7))
        def _():
            copies[2][c].start()

        copies[1][c].wait_recv()

        @pl.when((p == 1) | (p == 5))
        def _():
            copies[2][c].start()

        block_pairs[0][c].start()
        block_pairs[1][c].start()
        if CHUNKS[c][0] + CHUNKS[c][1] == QUARTER:
            @pl.when(p == 6)
            def _():
                patch_copy(1).start()

            @pl.when(p == 2)
            def _():
                patch_copy(3).start()

    @pl.when(p == 6)
    def _():
        patch_copy(2).start()

    @pl.when(p == 2)
    def _():
        patch_copy(4).start()

    second_pair.wait_recv()
    t = tile(SECOND, ROWS, columns_of(4), QUARTER)
    acc[4] = top(jnp.where((rest_col == rest_row) & jnp.logical_not(own), t, -1.0))
    for c in range(n_chunks):
        block_pairs[0][c].wait_recv()
        block_pairs[1][c].wait_recv()
    for a, b in meetings:
        meet(a, b)
        meet(b, a)
    for c in range(n_chunks - 1):
        copies[2][c].wait_recv()
        block_pairs[2][c].start()
    for c in range(n_chunks):
        if sum(CHUNKS[c]) <= QUARTER:
            block_pairs[2][c].wait_recv()
    @pl.when(has_head)
    def _():
        head_copy(0).wait_recv()
        head_pair.start()

    @pl.when(has_tail)
    def _():
        tail_copy(0).wait_recv()
        tail_pair.start()

    late(0)
    copies[2][n_chunks - 1].wait_recv()
    block_pairs[2][n_chunks - 1].start()

    @pl.when(has_patch)
    def _():
        patch_copy(0).wait_recv()
        patch_pair.start()

    def raise_to(b, at, n, v):
        ob[b, :, pl.ds(at, n)] = jnp.maximum(ob[b, :, pl.ds(at, n)], v)

    def beside(pair, start, step, at, is_here, there_col):
        pair.wait_recv()
        t = jnp.where(there_col == rest_row, tile(start, EDGE, columns_of(4), QUARTER), -1.0)
        acc[4] = jnp.maximum(acc[4], top(t))
        none = jnp.full((QUARTER - EDGE, QUARTER), -1.0, F32)
        m = across(jnp.concatenate([none, t] if at else [t, none], axis=0))
        is_here = is_here[:, at : at + QUARTER]
        raise_to(share + step, at, QUARTER, jnp.where(is_here, -1.0, m))
        raise_to(share + step + 10, at, QUARTER, jnp.where(is_here, m, -1.0))

    @pl.when(has_head)
    def _():
        beside(head_pair, HEAD, 1, 0, is_next, next_col)

    @pl.when(has_tail)
    def _():
        beside(tail_pair, TAIL, -1, QUARTER, is_prev, prev_col)

    for c in range(n_chunks):
        if sum(CHUNKS[c]) > QUARTER:
            block_pairs[2][c].wait_recv()
    late(QUARTER)

    @pl.when(has_patch)
    def _():
        patch_pair.wait_recv()
        def meets(start):
            t = tile(PATCH, QUARTER, pl.multiple_of(start + mine, QUARTER), QUARTER)
            s = jnp.where(start == SECOND, 4, start // ROWS)
            acc[s] = jnp.maximum(acc[s], top(t))
            return across(t)

        at = pl.multiple_of(QUARTER * pick(p, PATCH_HALF), QUARTER)
        v = pick(p, PATCH_BLOCK)
        here = labs[v, :, pl.ds(at, QUARTER)] == large

        def give(m):
            raise_to(v, at, QUARTER, jnp.where(here, m, -1.0))
            raise_to(v + 10, at, QUARTER, jnp.where(here, -1.0, m))

        give(meets(pick(p, PATCH_MEETS)))

        @pl.when(p == 2)
        def _():
            give(meets(jnp.int32(SLOT[2])))

    def give_block(v, at, n, m):
        here = labs[v, :, pl.ds(at, n)] == large
        raise_to(v, at, n, jnp.where(here, m, -1.0))
        raise_to(jnp.minimum(v + 10, 15), at, n, jnp.where(here | (v >= 6), -1.0, m))

    for s in range(3):
        give_block(pick(p, tuple(h[s] for h in HELD)), mine, QUARTER, acc[s])
    last[:, pl.ds(mine, QUARTER)] = jnp.maximum(last[:, pl.ds(mine, QUARTER)], acc[3])
    give_block(pick(p, tuple(h[3] for h in HELD)), 0, ROWS, last[...])
    here = labs[first, :, pl.ds(mine, QUARTER)] == large
    raise_to(second, mine, QUARTER, jnp.where(here, acc[4], -1.0))
    raise_to(first, mine, QUARTER, jnp.where(here, -1.0, acc[4]))

    def send_best(b, carry):
        to_self = at_home & (b == col)

        @pl.when(to_self)
        def _():
            pltpu.make_async_copy(ob.at[b], fin.at[p * 2 + k], fin_r).start()

        @pl.when(jnp.logical_not(to_self))
        def _():
            pltpu.make_async_remote_copy(
                src_ref=ob.at[b], dst_ref=fin.at[p * 2 + k],
                send_sem=fin_s, recv_sem=fin_r, device_id=(group, b), device_id_type=MESH,
            ).start()

        return carry

    lax.fori_loop(0, 16, send_best, 0)

    pltpu.make_async_copy(sbuf.at[0, pl.ds(0, 1008)], sbuf.at[0, pl.ds(0, 1008)], row_s).wait()
    pltpu.make_async_copy(sbuf.at[0], sbuf.at[0], row_s).wait()
    pltpu.make_async_copy(meta_s.at[pl.ds(0, 63)], meta_s.at[pl.ds(0, 63)], meta_ss).wait()
    meta_pair.wait_send()
    for per_bit in copies + block_pairs:
        for cp in per_bit:
            cp.wait_send()
    own_pair.wait_send()
    second_pair.wait_send()

    @pl.when(has_head)
    def _():
        head_pair.wait_send()
        tail_copy(0).wait_send()

    @pl.when(has_tail)
    def _():
        tail_pair.wait_send()
        head_copy(0).wait_send()

    @pl.when(has_patch)
    def _():
        patch_pair.wait_send()

    for v, which in ((4, (0,)), (6, (1, 2)), (2, (3, 4))):
        @pl.when(p == v)
        def _():
            for i in which:
                patch_copy(i).wait_send()

    @pl.when(at_home)
    def _():
        pltpu.make_async_copy(labs.at[pl.ds(0, 15)], labs.at[pl.ds(0, 15)], lab_s).wait()
        pltpu.make_async_copy(fin.at[pl.ds(0, 15)], fin.at[pl.ds(0, 15)], fin_s).wait()

    @pl.when(jnp.logical_not(at_home))
    def _():
        pltpu.make_async_copy(labs, labs, lab_s).wait()
        pltpu.make_async_copy(fin, fin, fin_s).wait()

    pltpu.make_async_copy(fin, fin, fin_r).wait()


def shards(embeddings, dest_pos, cluster_ids):
    dma, n_pairs = pltpu.SemaphoreType.DMA, 5 + 3 * len(CHUNKS)
    bests = pl.pallas_call(
        kernel,
        out_shape=jax.ShapeDtypeStruct((16, 1, ROWS), F32),
        in_specs=[
            pl.BlockSpec(memory_space=pltpu.HBM),
            pl.BlockSpec(memory_space=pltpu.HBM),
            pl.BlockSpec(memory_space=pltpu.HBM),
        ],
        out_specs=pl.BlockSpec(memory_space=pltpu.HBM),
        scratch_shapes=[
            pltpu.VMEM((ROWS, WIDTH), F32),
            pltpu.VMEM((1, ROWS), I32),
            pltpu.VMEM((1, ROWS), I32),
            pltpu.VMEM((ROWS, WIDTH), BF16),
            pltpu.VMEM((2, 1024, HALF), BF16),
            pltpu.VMEM((16 * DEVS, HALF), BF16),
            pltpu.VMEM((2 * ROWS, HALF), F32),
            pltpu.VMEM((64, 1, 128), F32),
            pltpu.VMEM((DEVS, 1, 128), F32),
            pltpu.VMEM((16, 1, ROWS), I32),
            pltpu.VMEM((2 * ROWS, 16 * DEVS), BF16),
            pltpu.VMEM((2, X_ROWS, HALF), BF16),
            pltpu.VMEM((5, 1, QUARTER), F32),
            pltpu.VMEM((1, ROWS), F32),
            pltpu.VMEM((16, 1, ROWS), F32),
            dma, dma, dma, dma, dma, dma((2,)), dma, dma, dma, dma, dma, dma,
            dma((3, len(CHUNKS))), dma((3, len(CHUNKS))), dma((n_pairs,)), dma((n_pairs,)),
            dma((2,)), dma, dma((2,)), dma((2,)), dma, dma,
        ],
        compiler_params=pltpu.CompilerParams(
            collective_id=0, has_side_effects=True, vmem_limit_bytes=62 * 2**20
        ),
        name="best_match",
    )(embeddings, dest_pos.reshape(1, ROWS), cluster_ids)
    return jnp.max(bests, axis=0)


def solution(mesh):
    return jax.shard_map(
        shards,
        mesh=mesh,
        in_specs=(P(("row", "col"), None), P(("row", "col")), P("row", "col")),
        out_specs=P("row", "col"),
        check_vma=False,
    )
```
